32 devices in a mesh: dp: 4 (over z), atoms: 8 (over y, x, core).
Axes of the slice: x: 2, y: 2, z: 4, core: 2. Of those that a mesh axis runs over, the one named last changes fastest.
Arguments:
- atom_single: bfloat16 [16, 2048, 128], P('dp', 'atoms'), may hold values from -6 to 6
- atom_cond: bfloat16 [16, 2048, 128], P('dp', 'atoms'), may hold values from -6 to 6
- atom_pair: bfloat16 [16, 16, 2048, 128], P('dp', None, 'atoms'), may hold values from -6 to 6
- atom_counts: int32 [16], P('dp'), may hold values from 512 to 2048, as said below
- cotangent: bfloat16 [16, 2048, 128], P('dp', 'atoms'), may hold values from -6 to 6
- first_gain: float32 [128], replicated, may hold values from 0.1 to 1.9
- first_scale: bfloat16 [128, 128], replicated, may hold values from -0.5 to 0.5
- first_lift: float32 [128], replicated, may hold values from -4 to 4
- first_shift: bfloat16 [128, 128], replicated, may hold values from -0.5 to 0.5
- query_weight: bfloat16 [128, 128], replicated, may hold values from -0.5 to 0.5
- query_bias: float32 [128], replicated, may hold values from -3 to 3
- key_weight: bfloat16 [128, 128], replicated, may hold values from -0.5 to 0.5
- value_weight: bfloat16 [128, 128], replicated, may hold values from -0.5 to 0.5
- gate_weight: bfloat16 [128, 128], replicated, may hold values from -0.5 to 0.5
- pair_gain: float32 [16], replicated, may hold values from 0.1 to 1.9
- pair_weight: float32 [16, 4], replicated, may hold values from -1.5 to 1.5
- output_weight: bfloat16 [128, 128], replicated, may hold values from -6 to 6
- branch_gate: bfloat16 [128, 128], replicated, may hold values from -0.5 to 0.5
- branch_lift: float32 [128], replicated, may hold values from -4 to 4
- second_gain: float32 [128], replicated, may hold values from 0.1 to 1.9
- second_scale: bfloat16 [128, 128], replicated, may hold values from -0.5 to 0.5
- second_lift: float32 [128], replicated, may hold values from -4 to 4
- second_shift: bfloat16 [128, 128], replicated, may hold values from -0.5 to 0.5
- hidden_gate: bfloat16 [128, 256], replicated, may hold values from -0.5 to 0.5
- hidden_up: bfloat16 [128, 256], replicated, may hold values from -0.5 to 0.5
- hidden_down: bfloat16 [256, 128], replicated, may hold values from -1 to 1
- closing_gate: bfloat16 [128, 128], replicated, may hold values from -0.5 to 0.5
- closing_lift: float32 [128], replicated, may hold values from -4 to 4
Outputs:
- layer_out: bfloat16 [16, 2048, 128], P('dp', 'atoms')
- atom_grad: float32 [16, 2048, 128], P('dp', 'atoms')
- pair_grad: float32 [16, 16, 2048, 128], P('dp', None, 'atoms')
- cond_grad: float32 [16, 2048, 128], P('dp', 'atoms')
- first_gain_grad: float32 [128], replicated
- first_scale_grad: float32 [128, 128], replicated
- first_lift_grad: float32 [128], replicated
- first_shift_grad: float32 [128, 128], replicated
- query_weight_grad: float32 [128, 128], replicated
- query_bias_grad: float32 [128], replicated
- key_weight_grad: float32 [128, 128], replicated
- value_weight_grad: float32 [128, 128], replicated
- gate_weight_grad: float32 [128, 128], replicated
- pair_gain_grad: float32 [16], replicated
- pair_weight_grad: float32 [16, 4], replicated
- output_weight_grad: float32 [128, 128], replicated
- branch_gate_grad: float32 [128, 128], replicated
- branch_lift_grad: float32 [128], replicated
- second_gain_grad: float32 [128], replicated
- second_scale_grad: float32 [128, 128], replicated
- second_lift_grad: float32 [128], replicated
- second_shift_grad: float32 [128, 128], replicated
- hidden_gate_grad: float32 [128, 256], replicated
- hidden_up_grad: float32 [128, 256], replicated
- hidden_down_grad: float32 [256, 128], replicated
- closing_gate_grad: float32 [128, 128], replicated
- closing_lift_grad: float32 [128], replicated
The draws below stay inside these ranges and needn't reach their ends.
Inputs may be any that keep to these rules, and one draw needn't show every extreme that they name: `atom_counts`: items are grouped in aligned groups of 4 (one index of dp); in each group one item, drawn from the seed, has all 2048 atoms and another has exactly 512. Atoms at positions at or beyond an item's count are padding.
All inputs are finite; a program needn't handle non-finite values.
Results may differ from the reference program's by a relative error of at most 0.009.
The reference program's roundings to bfloat16 on the way count: a program that leaves them out, or rounds other values in their place, can miss the bound.
Values may be sent and summed in bfloat16 or wider, within the bound.
A program may use at most 128 MiB of HBM per device.

```python
import jax
import jax.numpy as jnp
from jax import lax

C = 128
H = 4
CP = 16
F = 256
QW = 32
KW = 128
ITEMS_DP = 4
HD = 32
HALO = 48
ATOMS = 2048
BATCH = 16


def draw_atom_counts(key, part):
    key = jax.random.fold_in(key, 11)
    groups = BATCH // ITEMS_DP
    chosen_key, counts_key, other_key = jax.random.split(key, 3)
    chosen_slot = jax.random.randint(chosen_key, (groups, 1), 0, ITEMS_DP)
    step_slot = jax.random.randint(other_key, (groups, 1), 1, ITEMS_DP)
    small_slot = (chosen_slot + step_slot) % ITEMS_DP
    drawn_counts = jax.random.randint(counts_key, (groups, ITEMS_DP), ATOMS // 4, ATOMS + 1)
    slot_index = jnp.arange(ITEMS_DP, dtype=jnp.int32)[None, :]
    filled = jnp.where(slot_index == small_slot, ATOMS // 4, drawn_counts)
    filled = jnp.where(slot_index == chosen_slot, ATOMS, filled)
    return filled.reshape(BATCH).astype(jnp.int32)


def steps_of(key, extent, pieces, low, top_value):
    def one(axis_at, parts):
        steps = jax.random.uniform(jax.random.fold_in(jax.random.fold_in(key, 6), axis_at), (parts,), jnp.float32, low / len(pieces), top_value / len(pieces))
        return jnp.repeat(jnp.exp(steps), extent[axis_at] // parts).reshape((-1,) + (1,) * (len(extent) - axis_at - 1))

    factor_of = one(*pieces[0])
    for cut in pieces[1:]:
        factor_of = factor_of * one(*cut)
    return factor_of


def normal_values(rng, shape, spread, reach, cuts=(), kind=jnp.bfloat16):
    array = spread * jax.random.normal(rng, shape, jnp.float32)
    if cuts:
        array = array * steps_of(rng, shape, cuts, -0.22, 0.18)
    return jnp.clip(array, -reach, reach).astype(kind)


def setup_inputs(seed: int = 0) -> dict:
    streams_of = jax.random.split(jax.random.key(seed), 29)
    atom_single = normal_values(streams_of[0], (BATCH, ATOMS, C), 1.0, 6.0, ((0, 4), (1, 8)))
    atom_cond = normal_values(streams_of[1], (BATCH, ATOMS, C), 1.0, 6.0, ((0, 4), (1, 8)))
    atom_pair = normal_values(streams_of[2], (BATCH, CP, ATOMS, KW), 1.0, 6.0, ((0, 4), (2, 8)))
    atom_counts = draw_atom_counts(jax.random.fold_in(streams_of[28], 71), 0)
    cotangent = normal_values(streams_of[4], (BATCH, ATOMS, C), 1.0, 6.0, ((0, 4), (1, 8)))
    first_gain = jnp.clip(1.0 + 0.18 * jax.random.normal(streams_of[5], (C,), jnp.float32), 0.1, 1.9)
    first_scale = normal_values(streams_of[6], (C, C), C ** -0.5, 0.5)
    first_lift = normal_values(streams_of[7], (C,), 1.0, 4.0, (), jnp.float32)
    first_shift = normal_values(streams_of[8], (C, C), C ** -0.5, 0.5)
    query_weight = normal_values(streams_of[9], (C, C), C ** -0.5, 0.5)
    query_bias = normal_values(streams_of[10], (C,), 0.5, 3.0, (), jnp.float32)
    key_weight = normal_values(streams_of[11], (C, C), C ** -0.5, 0.5)
    value_weight = normal_values(streams_of[12], (C, C), C ** -0.5, 0.5)
    gate_weight = normal_values(streams_of[13], (C, C), C ** -0.5, 0.5)
    pair_gain = jnp.clip(1.0 + 0.18 * jax.random.normal(streams_of[14], (CP,), jnp.float32), 0.1, 1.9)
    pair_weight = normal_values(streams_of[15], (CP, H), CP ** -0.5, 1.5, (), jnp.float32)
    output_weight = normal_values(streams_of[16], (C, C), 1 ** -0.5, 6.0)
    branch_gate = normal_values(streams_of[17], (C, C), C ** -0.5, 0.5)
    branch_lift = normal_values(streams_of[18], (C,), 1.0, 4.0, (), jnp.float32)
    second_gain = jnp.clip(1.0 + 0.18 * jax.random.normal(streams_of[19], (C,), jnp.float32), 0.1, 1.9)
    second_scale = normal_values(streams_of[20], (C, C), C ** -0.5, 0.5)
    second_lift = normal_values(streams_of[21], (C,), 1.0, 4.0, (), jnp.float32)
    second_shift = normal_values(streams_of[22], (C, C), C ** -0.5, 0.5)
    hidden_gate = normal_values(streams_of[23], (C, F), C ** -0.5, 0.5)
    hidden_up = normal_values(streams_of[24], (C, F), C ** -0.5, 0.5)
    hidden_down = normal_values(streams_of[25], (F, C), (F // 8) ** -0.5, 1.0)
    closing_gate = normal_values(streams_of[26], (C, C), C ** -0.5, 0.5)
    closing_lift = normal_values(streams_of[27], (C,), 1.0, 4.0, (), jnp.float32)
    return dict(atom_single=atom_single, atom_cond=atom_cond, atom_pair=atom_pair, atom_counts=atom_counts, cotangent=cotangent, first_gain=first_gain, first_scale=first_scale, first_lift=first_lift, first_shift=first_shift, query_weight=query_weight, query_bias=query_bias, key_weight=key_weight, value_weight=value_weight, gate_weight=gate_weight, pair_gain=pair_gain, pair_weight=pair_weight, output_weight=output_weight, branch_gate=branch_gate, branch_lift=branch_lift, second_gain=second_gain, second_scale=second_scale, second_lift=second_lift, second_shift=second_shift, hidden_gate=hidden_gate, hidden_up=hidden_up, hidden_down=hidden_down, closing_gate=closing_gate, closing_lift=closing_lift)


@jax.custom_vjp
def low(v):
    return lax.optimization_barrier(v.astype(jnp.bfloat16)).astype(jnp.float32)

@jax.custom_vjp
def low_back(v):
    return v

def low_keep(v):
    return (low(v), None)

def low_pass(kept, grad):
    return (grad,)

def back_keep(v):
    return (v, None)

def back_low(kept, grad):
    return (low(grad),)
low.defvjp(low_keep, low_pass)
low_back.defvjp(back_keep, back_low)
epsilon = 1e-05
masked_score = -1000000000.0
highest = lax.Precision.HIGHEST

def normalize(values, axis):
    centre = values - lax.optimization_barrier(jnp.mean(values, axis=axis, keepdims=True))
    variance = lax.optimization_barrier(jnp.mean(centre * centre, axis=axis, keepdims=True))
    return centre * lax.rsqrt(variance + epsilon)

def linear(values, weight):
    return low_back(jnp.dot(values, weight, precision=highest))

def adaptive(values, cond, gain, scale_weight, scale_bias, shift_weight):
    cond_low = low(normalize(cond, -1) * gain)
    scaling = jax.nn.sigmoid(linear(cond_low, scale_weight) + scale_bias)
    return low(scaling * normalize(values, -1) + linear(cond_low, shift_weight))

def key_windows(rows_in):
    extended = jnp.pad(rows_in, ((HALO, HALO), (0, 0)))
    blocks = extended.reshape(-1, QW, rows_in.shape[-1])
    windows = rows_in.shape[0] // QW
    return jnp.concatenate([blocks[offset:offset + windows] for offset in range(KW // QW)], axis=1)

def layer(weights, single, cond, pair, count):
    first_gain, first_scale, first_lift, first_shift, query_weight, query_bias, key_weight, value_weight, gate_weight, pair_gain, pair_weight, output_weight, branch_gate, branch_lift, second_gain, second_scale, second_lift, second_shift, hidden_gate, hidden_up, hidden_down, closing_gate, closing_lift = weights
    windows = ATOMS // QW
    positions = jnp.arange(ATOMS, dtype=jnp.int32)
    living = (positions < count).astype(jnp.float32)[:, None]
    key_place = QW * jnp.arange(windows, dtype=jnp.int32)[:, None] - HALO + jnp.arange(KW, dtype=jnp.int32)[None, :]
    key_valid = (key_place >= 0) & (key_place < count)
    first_out = adaptive(single, cond, first_gain, first_scale, first_lift, first_shift)
    query = low(low_back(jnp.dot(first_out, query_weight, precision=highest)) + query_bias)
    key = low(linear(first_out, key_weight))
    value = low(linear(first_out, value_weight))
    gating = jax.nn.sigmoid(linear(first_out, gate_weight))
    pair_normed = normalize(pair, 0) * pair_gain[:, None, None]
    pair_term = jnp.einsum('cak,ch->hak', pair_normed, pair_weight, precision=highest).reshape(H, windows, QW, KW)
    query_win = query.reshape(windows, QW, H, HD)
    key_win = key_windows(key).reshape(windows, KW, H, HD)
    value_win = key_windows(value).reshape(windows, KW, H, HD)
    scores = low_back(jnp.einsum('wqhd,wkhd->hwqk', query_win, key_win, precision=highest) * HD ** (-0.5))
    logits = jnp.where(key_valid[None, :, None, :], scores + pair_term, masked_score)
    probs_low = low(jax.nn.softmax(logits, axis=-1))
    attended = low_back(jnp.einsum('hwqk,wkhd->wqhd', probs_low, value_win, precision=highest).reshape(ATOMS, C))
    gated = low(gating * attended)
    branch = linear(gated, output_weight)
    zero_one = jax.nn.sigmoid(linear(cond, branch_gate) + branch_lift)
    middle = single + living * zero_one * branch
    second_out = adaptive(middle, cond, second_gain, second_scale, second_lift, second_shift)
    hidden = low(jax.nn.silu(linear(second_out, hidden_gate)) * linear(second_out, hidden_up))
    closing = linear(hidden, hidden_down)
    zero_two = jax.nn.sigmoid(linear(cond, closing_gate) + closing_lift)
    return middle + living * zero_two * closing

def reference(atom_single, atom_cond, atom_pair, atom_counts, cotangent, first_gain, first_scale, first_lift, first_shift, query_weight, query_bias, key_weight, value_weight, gate_weight, pair_gain, pair_weight, output_weight, branch_gate, branch_lift, second_gain, second_scale, second_lift, second_shift, hidden_gate, hidden_up, hidden_down, closing_gate, closing_lift):
    weights = tuple((w.astype(jnp.float32) for w in (first_gain, first_scale, first_lift, first_shift, query_weight, query_bias, key_weight, value_weight, gate_weight, pair_gain, pair_weight, output_weight, branch_gate, branch_lift, second_gain, second_scale, second_lift, second_shift, hidden_gate, hidden_up, hidden_down, closing_gate, closing_lift)))
    starting = jax.tree.map(jnp.zeros_like, weights)

    def one_item(totals, item):
        single, cond, pair, count, seed_grad = item

        def forward(params, single_f, cond_f, pair_f):
            return layer(params, single_f, cond_f, pair_f, count)
        result, pullback = jax.vjp(forward, weights, single.astype(jnp.float32), cond.astype(jnp.float32), pair.astype(jnp.float32))
        weight_grads, single_grad, cond_grad, pair_grad = pullback(seed_grad.astype(jnp.float32))
        totals = jax.tree.map(jnp.add, totals, weight_grads)
        return (totals, (result.astype(jnp.bfloat16), single_grad, pair_grad, cond_grad))
    totals, stacked = lax.scan(one_item, starting, (atom_single, atom_cond, atom_pair, atom_counts, cotangent))
    return (stacked[0], stacked[1], stacked[2], stacked[3], totals[0], totals[1], totals[2], totals[3], totals[4], totals[5], totals[6], totals[7], totals[8], totals[9], totals[10], totals[11], totals[12], totals[13], totals[14], totals[15], totals[16], totals[17], totals[18], totals[19], totals[20], totals[21], totals[22])
```

```python
import functools

import jax
import jax.numpy as jnp
from jax import lax
from jax.experimental import pallas as pl
from jax.experimental.pallas import tpu as pltpu
from jax.sharding import PartitionSpec as P

QW = 32
KW = 128
HALO = 48
SPREAD = KW // QW
EPSILON = 1e-05
MASKED = -1000000000.0
HIGHEST = lax.Precision.HIGHEST
MESH = pl.DeviceIdType.MESH
F32 = jnp.float32
BF16 = jnp.bfloat16

GROUP_ONE = (
    "hidden_gate_a",
    "hidden_gate_b",
    "hidden_up_a",
    "hidden_up_b",
    "hidden_down_a",
    "hidden_down_b",
    "output_weight",
    "branch_gate",
    "closing_gate",
    "second_scale",
    "second_shift",
    "gate_weight",
)
GROUP_TWO = ("query_weight", "key_weight", "value_weight", "first_scale", "first_shift")
VECTORS = (
    "first_gain",
    "first_lift",
    "query_bias",
    "branch_lift",
    "second_gain",
    "second_lift",
    "closing_lift",
)


def mm(a, b, precision=None):
    return lax.dot_general(
        a, b, (((1,), (0,)), ((), ())), precision=precision, preferred_element_type=F32
    )


def mm_t(a, b, precision=None):
    return lax.dot_general(
        a, b, (((1,), (1,)), ((), ())), precision=precision, preferred_element_type=F32
    )


def t_mm(a, b):
    return lax.dot_general(a, b, (((0,), (0,)), ((), ())), preferred_element_type=F32)


def sigmoid(v):
    return 1.0 / (1.0 + jnp.exp(-v))


def lane_mean(v):
    return jnp.mean(v, axis=-1, keepdims=True)


def normalize(v):
    centre = v - lane_mean(v)
    inverse = lax.rsqrt(lane_mean(centre * centre) + EPSILON)
    return centre * inverse, jnp.broadcast_to(inverse, v.shape)


def normalize_back(normed, inverse, grads):
    return inverse * (grads - lane_mean(grads) - normed * lane_mean(grads * normed))


def lanes(*parts):
    return jnp.concatenate(parts, axis=1)


def rows(*parts):
    return jnp.concatenate(parts, axis=0)


def col_sum(v):
    return jnp.sum(v, axis=0, keepdims=True)


def iota(shape, axis):
    return lax.broadcasted_iota(jnp.int32, shape, axis)


def shard_rows(total, peers):
    return -(-total // (16 * peers)) * 16


def main_kernel(
    n_a,
    n_d,
    counts,
    single,
    cond,
    cot,
    pair_hbm,
    first_gain,
    first_scale,
    first_lift,
    first_shift,
    query_weight,
    query_bias,
    key_weight,
    value_weight,
    gate_weight,
    pair_gain,
    pair_weight,
    output_weight,
    branch_gate,
    branch_lift,
    second_gain,
    second_scale,
    second_lift,
    second_shift,
    hidden_gate,
    hidden_up,
    hidden_down,
    closing_gate,
    closing_lift,
    layer_o,
    agrad_o,
    cgrad_o,
    dl_o,
    t_o,
    mean_o,
    wide_o,
    red1_o,
    red2_o,
    pair_s,
    kv_s,
    q_s,
    first_s,
    chat_s,
    cinv_s,
    shat_s,
    sinv_s,
    sig_s,
    gating_s,
    term_s,
    probs_s,
    inv_s,
    mean_s,
    att_s,
    mid_grad_s,
    cnorm_s,
    cdir_s,
    dlow_s,
    glow_s,
    dl_s,
    t_s,
    dq_s,
    kvg_s,
    layer_s,
    agrad_s,
    cgrad_s,
    wide_s,
    widet_s,
    headmask_s,
    pacc_s,
    acc1_s,
    acc2_s,
    halo_send,
    halo_recv,
    send1,
    recv1,
    zall1,
    red1_s,
    send2,
    recv2,
    zall2,
    red2_s,
    pair_sem,
    out_sem,
    misc_sem,
    kv_send_sem,
    kv_recv_sem,
    hg_send_sem,
    hg_recv_sem,
    rs1_send,
    rs1_recv,
    z1_send,
    z1_recv,
    ag1_send,
    ag1_recv,
    rs2_send,
    rs2_recv,
    z2_send,
    z2_recv,
    ag2_send,
    ag2_recv,
):
    items, length, width = single.shape
    windows = length // QW
    channels, heads = pair_weight.shape
    head_dim = width // heads
    factor = head_dim ** (-0.5)
    me = lax.axis_index("atoms")
    me_d = lax.axis_index("dp")
    anchor = me * length
    has_left = me > 0
    has_right = me < n_a - 1

    def pair_copy(i):
        return pltpu.make_async_copy(pair_hbm.at[i], pair_s.at[i], pair_sem.at[i])

    for i in range(items):
        pair_copy(i).start()

    kv_s[:, 0:HALO, :] = jnp.zeros((items, HALO, 2 * width), BF16)
    kv_s[:, HALO + length : 2 * HALO + length, :] = jnp.zeros((items, HALO, 2 * width), BF16)
    halo_recv[...] = jnp.zeros(halo_recv.shape, BF16)

    barrier = pltpu.get_barrier_semaphore()

    def greet_atoms(k, carry):
        pl.semaphore_signal(
            barrier, inc=1, device_id={"atoms": lax.rem(me + k, n_a)}, device_id_type=MESH
        )
        return carry

    def greet_dp(k, carry):
        pl.semaphore_signal(
            barrier, inc=1, device_id={"dp": lax.rem(me_d + k, n_d)}, device_id_type=MESH
        )
        return carry

    lax.fori_loop(1, n_a, greet_atoms, 0)
    lax.fori_loop(1, n_d, greet_dp, 0)

    hq = heads * QW
    cq = channels * QW
    headmask_s[...] = jnp.where(
        iota((hq, width), 0) // QW == iota((hq, width), 1) // head_dim, 1.0, 0.0
    ).astype(BF16)
    pick_head = jnp.where(iota((hq, heads), 0) // QW == iota((hq, heads), 1), 1.0, 0.0)
    weighted = mm_t(pick_head, pair_weight[...], HIGHEST) * pair_gain[...]
    weighted = weighted - lane_mean(weighted)
    spread = jnp.where(iota((channels, cq), 0) == iota((channels, cq), 1) // QW, 1.0, 0.0).astype(
        BF16
    )
    same_row = iota((hq, cq), 0) % QW == iota((hq, cq), 1) % QW
    high = weighted.astype(BF16)
    low = (weighted - high.astype(F32)).astype(BF16)
    wide_high = jnp.where(same_row, mm(high, spread), 0.0)
    wide_low = jnp.where(same_row, mm(low, spread), 0.0)
    wide_s[0:hq, :] = wide_high.astype(BF16)
    wide_s[hq : 2 * hq, :] = wide_low.astype(BF16)
    widet_s[:, 0:hq] = wide_high.T.astype(BF16)
    widet_s[:, hq : 2 * hq] = wide_low.T.astype(BF16)
    pltpu.make_async_copy(widet_s, wide_o, misc_sem.at[0]).start()

    acc1_s[...] = jnp.zeros(acc1_s.shape, F32)
    acc2_s[...] = jnp.zeros(acc2_s.shape, F32)
    pacc_s[...] = jnp.zeros(pacc_s.shape, F32)

    def add1(name, value):
        at = GROUP_ONE.index(name) * width
        acc1_s[at : at + value.shape[0], :] += value

    def add2(name, value):
        at = GROUP_TWO.index(name) * width
        acc2_s[at : at + value.shape[0], :] += value

    vector_at = len(GROUP_TWO) * width

    def add_vector(name, value):
        at = vector_at + VECTORS.index(name)
        acc2_s[at : at + 1, :] += value

    pair_at = vector_at + 8

    def alive(i):
        place = anchor + iota((length, width), 0)
        return jnp.where(place < counts[i], 1.0, 0.0)

    def project(i, carry):
        single_hat, single_inv = normalize(single[i].astype(F32))
        cond_hat, cond_inv = normalize(cond[i].astype(F32))
        low1 = (cond_hat * first_gain[...]).astype(BF16)
        pre = mm(low1, lanes(first_scale[...], first_shift[...]))
        scaling = sigmoid(pre[:, :width] + first_lift[...])
        first = (scaling * single_hat + pre[:, width:]).astype(BF16)
        qkvg = mm(
            first, lanes(query_weight[...], key_weight[...], value_weight[...], gate_weight[...])
        )
        q_s[i] = (qkvg[:, :width] + query_bias[...]).astype(BF16)
        kv_s[i, HALO : HALO + length, :] = qkvg[:, width : 3 * width].astype(BF16)
        gating_s[i] = sigmoid(qkvg[:, 3 * width :])
        first_s[i] = first
        shat_s[i] = single_hat
        sinv_s[i] = single_inv
        chat_s[i] = cond_hat
        cinv_s[i] = cond_inv
        sig_s[i] = scaling
        return carry

    lax.fori_loop(0, items, project, 0)

    pl.semaphore_wait(barrier, n_a - 1 + n_d - 1)

    def kv_right():
        return pltpu.make_async_remote_copy(
            src_ref=kv_s.at[:, pl.ds(length, HALO), :],
            dst_ref=kv_s.at[:, pl.ds(0, HALO), :],
            send_sem=kv_send_sem.at[0],
            recv_sem=kv_recv_sem.at[0],
            device_id={"atoms": lax.rem(me + 1, n_a)},
            device_id_type=MESH,
        )

    def kv_left():
        return pltpu.make_async_remote_copy(
            src_ref=kv_s.at[:, pl.ds(HALO, HALO), :],
            dst_ref=kv_s.at[:, pl.ds(HALO + length, HALO), :],
            send_sem=kv_send_sem.at[1],
            recv_sem=kv_recv_sem.at[1],
            device_id={"atoms": lax.rem(me + n_a - 1, n_a)},
            device_id_type=MESH,
        )

    @pl.when(has_right)
    def _():
        kv_right().start()

    @pl.when(has_left)
    def _():
        kv_left().start()

    def pair_rows(i, w):
        return pair_s[i, :, w * QW : (w + 1) * QW, :]

    def pair_forward(i, carry):
        pair_copy(i).wait()
        wide = wide_s[...]
        for w in range(0, windows, 2):
            invs = []
            for v in (w, w + 1):
                block = pair_rows(i, v).astype(F32)
                mean = jnp.mean(block, axis=0)
                centre = block - mean[None]
                inv = lax.rsqrt(jnp.mean(centre * centre, axis=0) + EPSILON)
                mean_s[i, v * QW : (v + 1) * QW, :] = mean
                inv_s[i, v * QW : (v + 1) * QW, :] = inv
                invs.append(inv)
            both = lanes(pair_rows(i, w).reshape(cq, KW), pair_rows(i, w + 1).reshape(cq, KW))
            product = mm(wide, both)
            product = product[:hq] + product[hq:]
            for v in (0, 1):
                part = product[:, v * KW : (v + 1) * KW].reshape(heads, QW, KW)
                term_s[i, w + v] = (part * invs[v][None]).reshape(hq, KW)
        pltpu.make_async_copy(mean_s.at[i], mean_o.at[i], out_sem.at[0, i]).start()
        return carry

    lax.fori_loop(0, items, pair_forward, 0)

    @pl.when(has_right)
    def _():
        kv_right().wait_send()

    @pl.when(has_left)
    def _():
        kv_left().wait_send()

    @pl.when(has_left)
    def _():
        kv_right().wait_recv()

    @pl.when(has_right)
    def _():
        kv_left().wait_recv()

    def spread_heads(block):
        return rows(*([block] * heads)) * headmask_s[...]

    def gather_heads(wide_block):
        lane = iota((QW, width), 1)
        result = wide_block[(heads - 1) * QW :]
        for h in range(heads - 2, -1, -1):
            result = jnp.where(
                lane < (h + 1) * head_dim, wide_block[h * QW : (h + 1) * QW], result
            )
        return result

    def window_rows(w):
        return slice(w * QW, (w + 1) * QW)

    def keys_of(i, w):
        return kv_s[i, w * QW : w * QW + KW, 0:width]

    def values_of(i, w):
        return kv_s[i, w * QW : w * QW + KW, width : 2 * width]

    def attend(i, carry):
        count = counts[i]
        scores = [
            mm_t(spread_heads(q_s[i, window_rows(w), :]), keys_of(i, w)) for w in range(windows)
        ]
        logits = []
        for w in range(windows):
            place = anchor + (w * QW - HALO) + iota((1, KW), 1)
            valid = (place >= 0) & (place < count)
            logits.append(jnp.where(valid, scores[w] * factor + term_s[i, w], MASKED))
        tops = [jnp.max(v, axis=-1, keepdims=True) for v in logits]
        raised = [jnp.exp(v - top) for v, top in zip(logits, tops)]
        totals = [jnp.sum(v, axis=-1, keepdims=True) for v in raised]
        for w in range(windows):
            probs = raised[w] * (1.0 / totals[w])
            probs_s[i, w] = probs
            attended = mm(probs.astype(BF16), values_of(i, w))
            att_s[i, window_rows(w), :] = gather_heads(attended)
        return carry

    lax.fori_loop(0, items, attend, 0)

    def middle(i, carry):
        live = alive(i)
        att = att_s[i]
        gating = gating_s[i]
        cond_hat = chat_s[i]
        cond_rows = cond[i]
        gated = (gating * att).astype(BF16)
        branch = mm(gated, output_weight[...])
        zeros = mm(cond_rows, lanes(branch_gate[...], closing_gate[...]))
        zero_one = sigmoid(zeros[:, :width] + branch_lift[...])
        zero_two = sigmoid(zeros[:, width:] + closing_lift[...])
        mid = single[i].astype(F32) + live * zero_one * branch
        mid_hat, mid_inv = normalize(mid)
        low2 = (cond_hat * second_gain[...]).astype(BF16)
        scale_shift = lanes(second_scale[...], second_shift[...])
        pre = mm(low2, scale_shift)
        scaling = sigmoid(pre[:, :width] + second_lift[...])
        second = (scaling * mid_hat + pre[:, width:]).astype(BF16)
        gate_up = lanes(hidden_gate[...], hidden_up[...])
        pre2 = mm(second, gate_up)
        inner = hidden_gate.shape[1]
        gate_pre, up_pre = pre2[:, :inner], pre2[:, inner:]
        gate_sig = sigmoid(gate_pre)
        hidden = (gate_pre * gate_sig * up_pre).astype(BF16)
        closing = mm(hidden, hidden_down[...])
        layer_s[i] = (mid + live * zero_two * closing).astype(BF16)
        out_grad = cot[i].astype(F32)
        closing_grad = (out_grad * live * zero_two).astype(BF16)
        zero_two_pre = out_grad * live * closing * zero_two * (1.0 - zero_two)
        zero_two_low = zero_two_pre.astype(BF16)
        down_grad = t_mm(hidden, closing_grad)
        add1("hidden_down_a", down_grad)
        add_vector("closing_lift", col_sum(zero_two_pre))
        hidden_grad = mm_t(closing_grad, hidden_down[...])
        gate_pre_grad = (
            hidden_grad * up_pre * gate_sig * (1.0 + gate_pre * (1.0 - gate_sig))
        ).astype(BF16)
        up_pre_grad = (hidden_grad * gate_pre * gate_sig).astype(BF16)
        gate_up_grad = lanes(gate_pre_grad, up_pre_grad)
        wide_grad = t_mm(second, gate_up_grad)
        for k, name in enumerate(GROUP_ONE[:4]):
            add1(name, wide_grad[:, k * width : (k + 1) * width])
        second_grad = mm_t(gate_up_grad, gate_up)
        before = second_grad * mid_hat * scaling * (1.0 - scaling)
        both = lanes(before.astype(BF16), second_grad.astype(BF16))
        both_grad = t_mm(low2, both)
        add1("second_scale", both_grad[:, :width])
        add1("second_shift", both_grad[:, width:])
        add_vector("second_lift", col_sum(before))
        cond_normed = mm_t(both, scale_shift)
        add_vector("second_gain", col_sum(cond_normed * cond_hat))
        cnorm_s[i] = cond_normed * second_gain[...]
        mid_grad = out_grad + normalize_back(mid_hat, mid_inv, second_grad * scaling)
        mid_grad_s[i] = mid_grad
        branch_grad = (mid_grad * live * zero_one).astype(BF16)
        zero_one_pre = mid_grad * live * branch * zero_one * (1.0 - zero_one)
        add_vector("branch_lift", col_sum(zero_one_pre))
        zero_grads = lanes(zero_one_pre.astype(BF16), zero_two_low)
        gate_grads = t_mm(cond_rows, zero_grads)
        add1("branch_gate", gate_grads[:, :width])
        add1("closing_gate", gate_grads[:, width:])
        cdir_s[i] = mm_t(zero_grads, lanes(branch_gate[...], closing_gate[...]))
        add1("output_weight", t_mm(gated, branch_grad))
        gated_grad = mm_t(branch_grad, output_weight[...])
        dlow_s[i] = (gated_grad * gating).astype(BF16)
        gate_low = (gated_grad * att * gating * (1.0 - gating)).astype(BF16)
        glow_s[i] = gate_low
        add1("gate_weight", t_mm(first_s[i], gate_low))
        pltpu.make_async_copy(layer_s.at[i], layer_o.at[i], out_sem.at[1, i]).start()
        return carry

    lax.fori_loop(0, items, middle, 0)

    class Sum:
        def __init__(self, acc, send, recv, zall, red, sems):
            self.acc, self.send, self.recv, self.zall, self.red = acc, send, recv, zall, red
            self.rs_send, self.rs_recv, self.z_send, self.z_recv, self.ag_send, self.ag_recv = sems
            self.shard = send.shape[1]

        def scatter_copy(self, to, at):
            return pltpu.make_async_remote_copy(
                src_ref=self.send.at[to],
                dst_ref=self.recv.at[at],
                send_sem=self.rs_send.at[to],
                recv_sem=self.rs_recv.at[at],
                device_id={"atoms": to},
                device_id_type=MESH,
            )

        def dp_copy(self, to, at):
            return pltpu.make_async_remote_copy(
                src_ref=self.zall.at[me_d],
                dst_ref=self.zall.at[at],
                send_sem=self.z_send.at[to],
                recv_sem=self.z_recv.at[at],
                device_id={"dp": to},
                device_id_type=MESH,
            )

        def gather_copy(self, to, at):
            return pltpu.make_async_remote_copy(
                src_ref=self.red.at[me],
                dst_ref=self.red.at[at],
                send_sem=self.ag_send.at[to],
                recv_sem=self.ag_recv.at[at],
                device_id={"atoms": to},
                device_id_type=MESH,
            )

        def scatter(self):
            self.send[...] = self.acc[...].astype(BF16).reshape(self.send.shape)

            def go(k, carry):
                self.scatter_copy(lax.rem(me + k, n_a), me).start()
                return carry

            lax.fori_loop(1, n_a, go, 0)

        def over_dp(self):
            start = pl.multiple_of(me * self.shard, 16)
            total = self.acc[pl.ds(start, self.shard), :]
            for k in range(1, n_a):
                peer = lax.rem(me + k, n_a)
                self.scatter_copy(peer, peer).wait_recv()
                total = total + self.recv[peer].astype(F32)
            self.zall[me_d] = total.astype(BF16)

            def go(k, carry):
                self.dp_copy(lax.rem(me_d + k, n_d), me_d).start()
                return carry

            lax.fori_loop(1, n_d, go, 0)

        def gather(self):
            def come(k, carry):
                peer = lax.rem(me_d + k, n_d)
                self.dp_copy(peer, peer).wait_recv()
                return carry

            lax.fori_loop(1, n_d, come, 0)
            total = self.zall[0].astype(F32)
            for d in range(1, n_d):
                total = total + self.zall[d].astype(F32)
            self.red[me] = total.astype(BF16)

            def go(k, carry):
                self.gather_copy(lax.rem(me + k, n_a), me).start()
                return carry

            lax.fori_loop(1, n_a, go, 0)

        def finish(self):
            def end(k, carry):
                peer = lax.rem(me + k, n_a)
                self.gather_copy(peer, peer).wait_recv()
                self.gather_copy(peer, peer).wait_send()
                self.scatter_copy(peer, peer).wait_send()
                return carry

            lax.fori_loop(1, n_a, end, 0)

            def end_dp(k, carry):
                peer = lax.rem(me_d + k, n_d)
                self.dp_copy(peer, peer).wait_send()
                return carry

            lax.fori_loop(1, n_d, end_dp, 0)

    sum1 = Sum(
        acc1_s,
        send1,
        recv1,
        zall1,
        red1_s,
        (rs1_send, rs1_recv, z1_send, z1_recv, ag1_send, ag1_recv),
    )
    sum2 = Sum(
        acc2_s,
        send2,
        recv2,
        zall2,
        red2_s,
        (rs2_send, rs2_recv, z2_send, z2_recv, ag2_send, ag2_recv),
    )
    sum1.scatter()

    def halo_right(i):
        return pltpu.make_async_remote_copy(
            src_ref=halo_send.at[i, 1],
            dst_ref=halo_recv.at[i, 0],
            send_sem=hg_send_sem.at[i, 1],
            recv_sem=hg_recv_sem.at[i, 0],
            device_id={"atoms": lax.rem(me + 1, n_a)},
            device_id_type=MESH,
        )

    def halo_left(i):
        return pltpu.make_async_remote_copy(
            src_ref=halo_send.at[i, 0],
            dst_ref=halo_recv.at[i, 1],
            send_sem=hg_send_sem.at[i, 0],
            recv_sem=hg_recv_sem.at[i, 1],
            device_id={"atoms": lax.rem(me + n_a - 1, n_a)},
            device_id_type=MESH,
        )

    def attend_back(i, carry):
        wide_grads = [spread_heads(dlow_s[i, window_rows(w), :]) for w in range(windows)]
        probs_grads = [mm_t(wide_grads[w], values_of(i, w)) for w in range(windows)]
        inners = [
            jnp.sum(probs_grads[w] * probs_s[i, w], axis=-1, keepdims=True) for w in range(windows)
        ]
        value_parts = [t_mm(probs_s[i, w].astype(BF16), wide_grads[w]) for w in range(windows)]
        key_parts = []
        for w in range(windows):
            logits_grad = probs_s[i, w] * (probs_grads[w] - inners[w])
            low = logits_grad.astype(BF16)
            dq_s[i, window_rows(w), :] = gather_heads(mm(low, keys_of(i, w))) * factor
            key_parts.append(t_mm(low, spread_heads(q_s[i, window_rows(w), :])) * factor)
            inv = inv_s[i, window_rows(w), :]
            by_head = logits_grad.reshape(heads, QW, KW)
            dl_s[i, w] = (by_head * inv[None]).astype(BF16).reshape(hq, KW)
            inner = jnp.sum(by_head * term_s[i, w].reshape(heads, QW, KW), axis=0)
            t_s[i, window_rows(w), :] = inner * inv * inv * (1.0 / channels)
        for part, at in ((key_parts, 0), (value_parts, width)):
            for b in range(windows + SPREAD - 1):
                block = None
                for w in range(max(0, b - SPREAD + 1), min(windows - 1, b) + 1):
                    piece = part[w][(b - w) * QW : (b - w + 1) * QW]
                    block = piece if block is None else block + piece
                kvg_s[i, b * QW : (b + 1) * QW, at : at + width] = block
        halo_send[i, 0] = kvg_s[i, 0:HALO, :].astype(BF16)
        halo_send[i, 1] = kvg_s[i, HALO + length : 2 * HALO + length, :].astype(BF16)

        @pl.when(has_right)
        def _():
            halo_right(i).start()

        @pl.when(has_left)
        def _():
            halo_left(i).start()

        pair_all = lanes(*[pair_rows(i, w).reshape(cq, KW) for w in range(windows)])
        grads_all = lanes(*[dl_s[i, w] for w in range(windows)])
        pacc_s[...] += mm_t(pair_all, grads_all)
        pltpu.make_async_copy(dl_s.at[i], dl_o.at[i], out_sem.at[2, i]).start()
        pltpu.make_async_copy(t_s.at[i], t_o.at[i], out_sem.at[3, i]).start()
        return carry

    lax.fori_loop(0, items, attend_back, 0)
    sum1.over_dp()

    diagonal = jnp.where(iota((cq, hq), 0) % QW == iota((cq, hq), 1) % QW, pacc_s[...], 0.0)
    by_channel = jnp.sum(diagonal.reshape(channels, QW, hq), axis=1)
    fold = jnp.where(iota((hq, width), 0) // QW == iota((hq, width), 1), 1.0, 0.0)
    pair_sums = mm(by_channel, fold, HIGHEST)
    acc2_s[pair_at : pair_at + channels, :] = pair_sums - jnp.mean(
        pair_sums, axis=0, keepdims=True
    )

    def finish_rows(i, carry):
        @pl.when(has_left)
        def _():
            halo_right(i).wait_recv()

        @pl.when(has_right)
        def _():
            halo_left(i).wait_recv()

        kvg_s[i, HALO : 2 * HALO, :] += halo_recv[i, 0].astype(F32)
        kvg_s[i, length : length + HALO, :] += halo_recv[i, 1].astype(F32)
        dq = dq_s[i]
        add_vector("query_bias", col_sum(dq))
        grads = lanes(
            dq.astype(BF16), kvg_s[i, HALO : HALO + length, :].astype(BF16), glow_s[i]
        )
        first = first_s[i]
        weight_grads = t_mm(first, grads[:, : 3 * width])
        for k, name in enumerate(GROUP_TWO[:3]):
            add2(name, weight_grads[:, k * width : (k + 1) * width])
        first_grad = mm_t(
            grads, lanes(query_weight[...], key_weight[...], value_weight[...], gate_weight[...])
        )
        scaling = sig_s[i]
        single_hat = shat_s[i]
        cond_hat = chat_s[i]
        before = first_grad * single_hat * scaling * (1.0 - scaling)
        both = lanes(before.astype(BF16), first_grad.astype(BF16))
        low1 = (cond_hat * first_gain[...]).astype(BF16)
        both_grad = t_mm(low1, both)
        add2("first_scale", both_grad[:, :width])
        add2("first_shift", both_grad[:, width:])
        add_vector("first_lift", col_sum(before))
        cond_normed = mm_t(both, lanes(first_scale[...], first_shift[...]))
        add_vector("first_gain", col_sum(cond_normed * cond_hat))
        agrad_s[i] = mid_grad_s[i] + normalize_back(single_hat, sinv_s[i], first_grad * scaling)
        cond_grad = cond_normed * first_gain[...] + cnorm_s[i]
        cgrad_s[i] = normalize_back(cond_hat, cinv_s[i], cond_grad) + cdir_s[i]
        pltpu.make_async_copy(agrad_s.at[i], agrad_o.at[i], out_sem.at[4, i]).start()
        pltpu.make_async_copy(cgrad_s.at[i], cgrad_o.at[i], out_sem.at[5, i]).start()
        return carry

    lax.fori_loop(0, items, finish_rows, 0)
    sum2.scatter()
    sum1.gather()
    sum2.over_dp()
    sum2.gather()
    sum1.finish()
    red1_out = pltpu.make_async_copy(red1_s, red1_o, misc_sem.at[1])
    red1_out.start()
    sum2.finish()
    red2_out = pltpu.make_async_copy(red2_s, red2_o, misc_sem.at[2])
    red2_out.start()

    def drain(i, carry):
        pltpu.make_async_copy(mean_s.at[i], mean_o.at[i], out_sem.at[0, i]).wait()
        pltpu.make_async_copy(layer_s.at[i], layer_o.at[i], out_sem.at[1, i]).wait()
        pltpu.make_async_copy(dl_s.at[i], dl_o.at[i], out_sem.at[2, i]).wait()
        pltpu.make_async_copy(t_s.at[i], t_o.at[i], out_sem.at[3, i]).wait()
        pltpu.make_async_copy(agrad_s.at[i], agrad_o.at[i], out_sem.at[4, i]).wait()
        pltpu.make_async_copy(cgrad_s.at[i], cgrad_o.at[i], out_sem.at[5, i]).wait()

        @pl.when(has_right)
        def _():
            halo_right(i).wait_send()

        @pl.when(has_left)
        def _():
            halo_left(i).wait_send()

        return carry

    lax.fori_loop(0, items, drain, 0)
    pltpu.make_async_copy(widet_s, wide_o, misc_sem.at[0]).wait()
    red1_out.wait()
    red2_out.wait()


GRADS = (
    "first_gain",
    "first_scale",
    "first_lift",
    "first_shift",
    "query_weight",
    "query_bias",
    "key_weight",
    "value_weight",
    "gate_weight",
    "pair_gain",
    "pair_weight",
    "output_weight",
    "branch_gate",
    "branch_lift",
    "second_gain",
    "second_scale",
    "second_lift",
    "second_shift",
    "hidden_gate",
    "hidden_up",
    "hidden_down",
    "closing_gate",
    "closing_lift",
)
SPLIT = {
    "hidden_gate": ("hidden_gate_a", "hidden_gate_b"),
    "hidden_up": ("hidden_up_a", "hidden_up_b"),
}


def pair_kernel(
    steps,
    pair,
    dl,
    t,
    mean,
    wide,
    red1,
    red2,
    pair_gain,
    pair_weight,
    layer_in,
    agrad_in,
    cgrad_in,
    pgrad,
    layer_o,
    agrad_o,
    cgrad_o,
    *rest,
):
    grads = dict(zip(GRADS, rest[: len(GRADS)]))
    (sem,) = rest[len(GRADS) :]
    step = pl.program_id(0)
    copies = [
        pltpu.make_async_copy(layer_in, layer_o, sem.at[0]),
        pltpu.make_async_copy(agrad_in, agrad_o, sem.at[1]),
        pltpu.make_async_copy(cgrad_in, cgrad_o, sem.at[2]),
    ]

    @pl.when(step == 0)
    def _():
        for copy in copies:
            copy.start()
        width = red1.shape[1]

        def one(name):
            at = GROUP_ONE.index(name) * width
            return red1[at : at + width, :].astype(F32)

        vector_at = len(GROUP_TWO) * width
        tail = red2[vector_at : vector_at + 32, :].astype(F32)
        for name in GRADS:
            ref = grads[name]
            if name in SPLIT:
                for k, part in enumerate(SPLIT[name]):
                    ref[:, k * width : (k + 1) * width] = one(part)
            elif name == "hidden_down":
                ref[0:width, :] = one("hidden_down_a")
                ref[width : 2 * width, :] = one("hidden_down_b")
            elif name in GROUP_ONE:
                ref[...] = one(name)
            elif name in GROUP_TWO:
                at = GROUP_TWO.index(name) * width
                ref[...] = red2[at : at + width, :].astype(F32)
            elif name in VECTORS:
                at = VECTORS.index(name)
                ref[...] = tail[at : at + 1, :]
        channels, heads = pair_weight.shape
        sums = tail[8 : 8 + channels, 0:heads]
        eye = jnp.where(
            iota((channels, channels), 0) == iota((channels, channels), 1), 1.0, 0.0
        )
        gain_column = jnp.sum(eye * pair_gain[...], axis=1, keepdims=True)
        grads["pair_weight"][...] = gain_column * sums
        gain_grad = jnp.sum(pair_weight[...] * sums, axis=1, keepdims=True)
        grads["pair_gain"][...] = jnp.sum(eye * gain_grad, axis=0, keepdims=True)

    channels, span, _ = pair.shape[1:]
    wide_v = wide[...]
    for w in range(0, span // QW, 2):
        both = lanes(dl[0, w], dl[0, w + 1])
        product = mm(wide_v, rows(both, both))
        for v in (0, 1):
            at = slice((w + v) * QW, (w + v + 1) * QW)
            block = pair[0, :, at, :].astype(F32)
            part = product[:, v * KW : (v + 1) * KW].reshape(channels, QW, KW)
            pgrad[0, :, at, :] = part - (block - mean[0, at, :][None]) * t[0, at, :][None]

    @pl.when(step == steps - 1)
    def _():
        for copy in copies:
            copy.wait()


def shards(
    n_a,
    n_d,
    atom_single,
    atom_cond,
    atom_pair,
    atom_counts,
    cotangent,
    *params,
):
    items, length, width = atom_single.shape
    windows = length // QW
    channels = atom_pair.shape[1]
    named = dict(zip(GRADS, params))
    flat = [v.reshape(1, -1) if v.ndim == 1 else v for v in params]
    heads = named["pair_weight"].shape[1]
    hq, cq = heads * QW, channels * QW
    rows1 = len(GROUP_ONE) * width
    rows2 = len(GROUP_TWO) * width + 8 + channels
    shard1, shard2 = shard_rows(rows1, n_a), shard_rows(rows2, n_a)

    vmem = pl.BlockSpec(memory_space=pltpu.VMEM)
    anywhere = pl.BlockSpec(memory_space=pl.ANY)
    by_rows = (items, length, width)
    by_keys = (items, length, KW)
    ext = length + 2 * HALO
    dma = pltpu.SemaphoreType.DMA

    def sds(shape, dtype):
        return jax.ShapeDtypeStruct(shape, dtype)

    outs = pl.pallas_call(
        functools.partial(main_kernel, n_a, n_d),
        out_shape=[
            sds(by_rows, BF16),
            sds(by_rows, F32),
            sds(by_rows, F32),
            sds((items, windows, hq, KW), BF16),
            sds(by_keys, F32),
            sds(by_keys, F32),
            sds((cq, 2 * hq), BF16),
            sds((n_a, shard1, width), BF16),
            sds((n_a, shard2, width), BF16),
        ],
        in_specs=[pl.BlockSpec(memory_space=pltpu.SMEM), vmem, vmem, vmem, anywhere]
        + [vmem] * len(flat),
        out_specs=[anywhere] * 9,
        scratch_shapes=[
            pltpu.VMEM((items, channels, length, KW), BF16),
            pltpu.VMEM((items, ext, 2 * width), BF16),
            pltpu.VMEM(by_rows, BF16),
            pltpu.VMEM(by_rows, BF16),
            pltpu.VMEM(by_rows, F32),
            pltpu.VMEM(by_rows, F32),
            pltpu.VMEM(by_rows, F32),
            pltpu.VMEM(by_rows, F32),
            pltpu.VMEM(by_rows, F32),
            pltpu.VMEM(by_rows, F32),
            pltpu.VMEM((items, windows, hq, KW), F32),
            pltpu.VMEM((items, windows, hq, KW), F32),
            pltpu.VMEM(by_keys, F32),
            pltpu.VMEM(by_keys, F32),
            pltpu.VMEM(by_rows, F32),
            pltpu.VMEM(by_rows, F32),
            pltpu.VMEM(by_rows, F32),
            pltpu.VMEM(by_rows, F32),
            pltpu.VMEM(by_rows, BF16),
            pltpu.VMEM(by_rows, BF16),
            pltpu.VMEM((items, windows, hq, KW), BF16),
            pltpu.VMEM(by_keys, F32),
            pltpu.VMEM(by_rows, F32),
            pltpu.VMEM((items, ext, 2 * width), F32),
            pltpu.VMEM(by_rows, BF16),
            pltpu.VMEM(by_rows, F32),
            pltpu.VMEM(by_rows, F32),
            pltpu.VMEM((2 * hq, cq), BF16),
            pltpu.VMEM((cq, 2 * hq), BF16),
            pltpu.VMEM((hq, width), BF16),
            pltpu.VMEM((cq, hq), F32),
            pltpu.VMEM((n_a * shard1, width), F32),
            pltpu.VMEM((n_a * shard2, width), F32),
            pltpu.VMEM((items, 2, HALO, 2 * width), BF16),
            pltpu.VMEM((items, 2, HALO, 2 * width), BF16),
            pltpu.VMEM((n_a, shard1, width), BF16),
            pltpu.VMEM((n_a, shard1, width), BF16),
            pltpu.VMEM((n_d, shard1, width), BF16),
            pltpu.VMEM((n_a, shard1, width), BF16),
            pltpu.VMEM((n_a, shard2, width), BF16),
            pltpu.VMEM((n_a, shard2, width), BF16),
            pltpu.VMEM((n_d, shard2, width), BF16),
            pltpu.VMEM((n_a, shard2, width), BF16),
            dma((items,)),
            dma((6, items)),
            dma((3,)),
            dma((2,)),
            dma((2,)),
            dma((items, 2)),
            dma((items, 2)),
            dma((n_a,)),
            dma((n_a,)),
            dma((n_d,)),
            dma((n_d,)),
            dma((n_a,)),
            dma((n_a,)),
            dma((n_a,)),
            dma((n_a,)),
            dma((n_d,)),
            dma((n_d,)),
            dma((n_a,)),
            dma((n_a,)),
        ],
        compiler_params=pltpu.CompilerParams(
            collective_id=0, has_side_effects=True, vmem_limit_bytes=56 * 1024 * 1024
        ),
        name="block",
    )(atom_counts, atom_single, atom_cond, cotangent, atom_pair, *flat)
    layer, agrad, cgrad, dl, t, mean, wide, red1, red2 = outs

    parts = 2 if windows % 4 == 0 else 1
    span = length // parts
    steps = items * parts

    def whole(shape):
        return pl.BlockSpec(shape, lambda s: (0,) * len(shape))

    grad_shapes = [
        (1, v.shape[0]) if v.ndim == 1 else v.shape for v in (named[name] for name in GRADS)
    ]
    red1 = red1.reshape(n_a * shard1, width)
    red2 = red2.reshape(n_a * shard2, width)
    pair_spec = pl.BlockSpec((1, channels, span, KW), lambda s: (s // parts, 0, s % parts, 0))
    rows_spec = pl.BlockSpec((1, span, KW), lambda s: (s // parts, s % parts, 0))
    finals = pl.pallas_call(
        functools.partial(pair_kernel, steps),
        grid=(steps,),
        out_shape=[
            sds(atom_pair.shape, F32),
            sds(by_rows, BF16),
            sds(by_rows, F32),
            sds(by_rows, F32),
        ]
        + [sds(shape, F32) for shape in grad_shapes],
        in_specs=[
            pair_spec,
            pl.BlockSpec((1, span // QW, hq, KW), lambda s: (s // parts, s % parts, 0, 0)),
            rows_spec,
            rows_spec,
            whole(wide.shape),
            whole(red1.shape),
            whole(red2.shape),
            whole((1, channels)),
            whole((channels, heads)),
            anywhere,
            anywhere,
            anywhere,
        ],
        out_specs=[pair_spec, anywhere, anywhere, anywhere] + [whole(s) for s in grad_shapes],
        scratch_shapes=[dma((3,))],
        compiler_params=pltpu.CompilerParams(
            dimension_semantics=("arbitrary",), vmem_limit_bytes=40 * 1024 * 1024
        ),
        name="pair_grad",
    )(
        atom_pair,
        dl,
        t,
        mean,
        wide,
        red1,
        red2,
        named["pair_gain"].reshape(1, -1),
        named["pair_weight"],
        layer,
        agrad,
        cgrad,
    )
    pgrad, layer, agrad, cgrad, *weight_grads = finals
    weight_grads = [g.reshape(named[n].shape) for g, n in zip(weight_grads, GRADS)]
    return (layer, agrad, pgrad, cgrad, *weight_grads)


def solution(mesh):
    atoms = P("dp", "atoms", None)
    pair = P("dp", None, "atoms", None)
    return jax.shard_map(
        functools.partial(shards, mesh.shape["atoms"], mesh.shape["dp"]),
        mesh=mesh,
        in_specs=(atoms, atoms, pair, P("dp"), atoms) + (P(),) * len(GRADS),
        out_specs=(atoms, atoms, pair, atoms) + (P(),) * len(GRADS),
        check_vma=False,
    )
```

```python
import functools

import jax
import jax.numpy as jnp
from jax import lax
from jax.experimental import pallas as pl
from jax.experimental.pallas import tpu as pltpu
from jax.sharding import PartitionSpec as P

QW = 32
KW = 128
HALO = 48
SPREAD = KW // QW
EPSILON = 1e-05
MASKED = -1000000000.0
HIGHEST = lax.Precision.HIGHEST
MESH = pl.DeviceIdType.MESH
PROJECT_ITEMS = 2
PAIR_ITEMS = 1
ATTEND_ITEMS = 2
MIDDLE_ITEMS = 2
BACK_ITEMS = 1
FINISH_ITEMS = 2
F32 = jnp.float32
BF16 = jnp.bfloat16

GROUP_ONE = (
    "hidden_gate_a",
    "hidden_gate_b",
    "hidden_up_a",
    "hidden_up_b",
    "hidden_down_a",
    "hidden_down_b",
    "output_weight",
    "branch_gate",
    "closing_gate",
    "second_scale",
    "second_shift",
    "gate_weight",
)
GROUP_TWO = ("query_weight", "key_weight", "value_weight", "first_scale", "first_shift")
VECTORS = (
    "first_gain",
    "first_lift",
    "query_bias",
    "branch_lift",
    "second_gain",
    "second_lift",
    "closing_lift",
)


def mm(a, b, precision=None):
    return lax.dot_general(
        a, b, (((1,), (0,)), ((), ())), precision=precision, preferred_element_type=F32
    )


def mm_t(a, b, precision=None):
    return lax.dot_general(
        a, b, (((1,), (1,)), ((), ())), precision=precision, preferred_element_type=F32
    )


def t_mm(a, b):
    return lax.dot_general(a, b, (((0,), (0,)), ((), ())), preferred_element_type=F32)


def sigmoid(v):
    return 0.5 * jnp.tanh(0.5 * v) + 0.5


def lane_mean(v):
    return jnp.mean(v, axis=-1, keepdims=True)


def normalize(v):
    centre = v - lane_mean(v)
    inverse = lax.rsqrt(lane_mean(centre * centre) + EPSILON)
    return centre * inverse, jnp.broadcast_to(inverse, v.shape)


def normalize_back(normed, inverse, grads):
    return inverse * (grads - lane_mean(grads) - normed * lane_mean(grads * normed))


def lanes(*parts):
    return jnp.concatenate(parts, axis=1)


def rows(*parts):
    return jnp.concatenate(parts, axis=0)


def col_sum(v):
    return jnp.sum(v, axis=0, keepdims=True)


def iota(shape, axis):
    return lax.broadcasted_iota(jnp.int32, shape, axis)


def shard_rows(total, peers):
    return -(-total // (16 * peers)) * 16


def main_kernel(
    n_a,
    n_d,
    counts,
    single,
    cond,
    cot,
    pair_hbm,
    first_gain,
    first_scale,
    first_lift,
    first_shift,
    query_weight,
    query_bias,
    key_weight,
    value_weight,
    gate_weight,
    pair_gain,
    pair_weight,
    output_weight,
    branch_gate,
    branch_lift,
    second_gain,
    second_scale,
    second_lift,
    second_shift,
    hidden_gate,
    hidden_up,
    hidden_down,
    closing_gate,
    closing_lift,
    layer_o,
    agrad_o,
    cgrad_o,
    pgrad_o,
    red1_s,
    red2_s,
    pair_s,
    kv_s,
    q_s,
    first_s,
    chat_s,
    cinv_s,
    shat_s,
    sinv_s,
    sig_s,
    gating_s,
    term_s,
    probs_s,
    inv_s,
    mean_s,
    att_s,
    mid_grad_s,
    cnorm_s,
    cdir_s,
    dlow_s,
    glow_s,
    dl_s,
    t_s,
    dq_s,
    kvg_s,
    wide_s,
    widet_s,
    headmask_s,
    pacc_s,
    acc1_s,
    acc2_s,
    halo_send,
    halo_recv,
    send1,
    recv1,
    zall1,
    send2,
    recv2,
    zall2,
    pair_sem,
    kv_send_sem,
    kv_recv_sem,
    hg_send_sem,
    hg_recv_sem,
    rs1_send,
    rs1_recv,
    z1_send,
    z1_recv,
    ag1_send,
    ag1_recv,
    rs2_send,
    rs2_recv,
    z2_send,
    z2_recv,
    ag2_send,
    ag2_recv,
):
    items, length, width = single.shape
    windows = length // QW
    heads, channels = pair_weight.shape
    head_dim = width // heads
    factor = head_dim ** (-0.5)
    me = lax.axis_index("atoms")
    me_d = lax.axis_index("dp")
    anchor = me * length
    has_left = me > 0
    has_right = me < n_a - 1

    def pair_copy(i):
        return pltpu.make_async_copy(pair_hbm.at[i], pair_s.at[i], pair_sem.at[i])

    for i in range(items):
        pair_copy(i).start()

    kv_s[:, 0:HALO, :] = jnp.zeros((items, HALO, 2 * width), BF16)
    kv_s[:, HALO + length : 2 * HALO + length, :] = jnp.zeros((items, HALO, 2 * width), BF16)
    halo_recv[...] = jnp.zeros(halo_recv.shape, BF16)

    barrier = pltpu.get_barrier_semaphore()

    def greet_atoms(k, carry):
        pl.semaphore_signal(
            barrier, inc=1, device_id={"atoms": lax.rem(me + k, n_a)}, device_id_type=MESH
        )
        return carry

    def greet_dp(k, carry):
        pl.semaphore_signal(
            barrier, inc=1, device_id={"dp": lax.rem(me_d + k, n_d)}, device_id_type=MESH
        )
        return carry

    lax.fori_loop(1, n_a, greet_atoms, 0)
    lax.fori_loop(1, n_d, greet_dp, 0)

    hq = heads * QW
    cq = channels * QW
    headmask_s[...] = jnp.where(
        iota((hq, width), 0) // QW == iota((hq, width), 1) // head_dim, 1.0, 0.0
    ).astype(BF16)
    pick_head = jnp.where(iota((hq, heads), 0) // QW == iota((hq, heads), 1), 1.0, 0.0)
    weighted = mm(pick_head, pair_weight[...], HIGHEST) * pair_gain[...]
    weighted = weighted - lane_mean(weighted)
    spread = jnp.where(iota((channels, cq), 0) == iota((channels, cq), 1) // QW, 1.0, 0.0).astype(
        BF16
    )
    same_row = iota((hq, cq), 0) % QW == iota((hq, cq), 1) % QW
    high = weighted.astype(BF16)
    low = (weighted - high.astype(F32)).astype(BF16)
    wide_high = jnp.where(same_row, mm(high, spread), 0.0)
    wide_low = jnp.where(same_row, mm(low, spread), 0.0)
    wide_s[0:hq, :] = wide_high.astype(BF16)
    wide_s[hq : 2 * hq, :] = wide_low.astype(BF16)
    widet_s[:, 0:hq] = wide_high.T.astype(BF16)
    widet_s[:, hq : 2 * hq] = wide_low.T.astype(BF16)

    acc1_s[...] = jnp.zeros(acc1_s.shape, F32)
    acc2_s[...] = jnp.zeros(acc2_s.shape, F32)
    pacc_s[...] = jnp.zeros(pacc_s.shape, F32)

    def add1(name, value):
        at = GROUP_ONE.index(name) * width
        acc1_s[at : at + value.shape[0], :] += value

    def add2(name, value):
        at = GROUP_TWO.index(name) * width
        acc2_s[at : at + value.shape[0], :] += value

    vector_at = len(GROUP_TWO) * width

    def add_vector(name, value):
        at = vector_at + VECTORS.index(name)
        acc2_s[at : at + 1, :] += value

    pair_at = vector_at + 8

    def steps(count, body):
        def step(s, carry):
            body(s * count)
            return carry

        lax.fori_loop(0, items // count, step, 0)

    def of_items(ref, i, count):
        return ref[pl.ds(i, count)].reshape(count * length, ref.shape[-1])

    def rows_of(i, count):
        return pl.ds(pl.multiple_of(i * length, length), count * length)

    def alive(i, count):
        place = anchor + iota((length, width), 0)
        return rows(*[jnp.where(place < counts[i + k], 1.0, 0.0) for k in range(count)])

    def project(i):
        n = PROJECT_ITEMS
        at = rows_of(i, n)
        single_hat, single_inv = normalize(of_items(single, i, n).astype(F32))
        cond_hat, cond_inv = normalize(of_items(cond, i, n).astype(F32))
        low1 = (cond_hat * first_gain[...]).astype(BF16)
        pre = mm(low1, lanes(first_scale[...], first_shift[...]))
        scaling = sigmoid(pre[:, :width] + first_lift[...])
        first = (scaling * single_hat + pre[:, width:]).astype(BF16)
        qkvg = mm(
            first, lanes(query_weight[...], key_weight[...], value_weight[...], gate_weight[...])
        )
        q_s[at, :] = (qkvg[:, :width] + query_bias[...]).astype(BF16)
        for k in range(n):
            kv_s[i + k, HALO : HALO + length, :] = qkvg[
                k * length : (k + 1) * length, width : 3 * width
            ].astype(BF16)
        gating_s[at, :] = sigmoid(qkvg[:, 3 * width :])
        first_s[at, :] = first
        shat_s[at, :] = single_hat
        sinv_s[at, :] = single_inv
        chat_s[at, :] = cond_hat
        cinv_s[at, :] = cond_inv
        sig_s[at, :] = scaling

    steps(PROJECT_ITEMS, project)

    pl.semaphore_wait(barrier, n_a - 1 + n_d - 1)

    def kv_right():
        return pltpu.make_async_remote_copy(
            src_ref=kv_s.at[:, pl.ds(length, HALO), :],
            dst_ref=kv_s.at[:, pl.ds(0, HALO), :],
            send_sem=kv_send_sem.at[0],
            recv_sem=kv_recv_sem.at[0],
            device_id={"atoms": lax.rem(me + 1, n_a)},
            device_id_type=MESH,
        )

    def kv_left():
        return pltpu.make_async_remote_copy(
            src_ref=kv_s.at[:, pl.ds(HALO, HALO), :],
            dst_ref=kv_s.at[:, pl.ds(HALO + length, HALO), :],
            send_sem=kv_send_sem.at[1],
            recv_sem=kv_recv_sem.at[1],
            device_id={"atoms": lax.rem(me + n_a - 1, n_a)},
            device_id_type=MESH,
        )

    @pl.when(has_right)
    def _():
        kv_right().start()

    @pl.when(has_left)
    def _():
        kv_left().start()

    def window_at(i, w):
        return pl.ds(pl.multiple_of(i * length + w * QW, QW), QW)

    def pair_rows(i, w):
        return pair_s[i, :, w * QW : (w + 1) * QW, :]

    def pair_forward(i):
        for k in range(PAIR_ITEMS):
            pair_copy(i + k).wait()
        wide = wide_s[...]
        for k in range(PAIR_ITEMS):
            for w in range(0, windows, 2):
                invs = []
                for v in (w, w + 1):
                    block = pair_rows(i + k, v).astype(F32)
                    mean = jnp.mean(block, axis=0)
                    centre = block - mean[None]
                    inv = lax.rsqrt(jnp.mean(centre * centre, axis=0) + EPSILON)
                    mean_s[window_at(i + k, v), :] = mean
                    inv_s[window_at(i + k, v), :] = inv
                    invs.append(inv)
                both = lanes(
                    pair_rows(i + k, w).reshape(cq, KW), pair_rows(i + k, w + 1).reshape(cq, KW)
                )
                product = mm(wide, both)
                product = product[:hq] + product[hq:]
                for v in (0, 1):
                    part = product[:, v * KW : (v + 1) * KW].reshape(heads, QW, KW)
                    term_s[i + k, w + v] = (part * invs[v][None]).reshape(hq, KW)

    steps(PAIR_ITEMS, pair_forward)

    @pl.when(has_right)
    def _():
        kv_right().wait_send()

    @pl.when(has_left)
    def _():
        kv_left().wait_send()

    @pl.when(has_left)
    def _():
        kv_right().wait_recv()

    @pl.when(has_right)
    def _():
        kv_left().wait_recv()

    def spread_heads(block):
        return rows(*([block] * heads)) * headmask_s[...]

    def gather_heads(wide_block):
        lane = iota((QW, width), 1)
        result = wide_block[(heads - 1) * QW :]
        for h in range(heads - 2, -1, -1):
            result = jnp.where(
                lane < (h + 1) * head_dim, wide_block[h * QW : (h + 1) * QW], result
            )
        return result

    def keys_of(i, w):
        return kv_s[i, w * QW : w * QW + KW, 0:width]

    def values_of(i, w):
        return kv_s[i, w * QW : w * QW + KW, width : 2 * width]

    def windows_of(i, count):
        return [(i + k, w) for k in range(count) for w in range(windows)]

    def attend(i):
        here = windows_of(i, ATTEND_ITEMS)
        scores = [mm_t(spread_heads(q_s[window_at(*a), :]), keys_of(*a)) for a in here]
        logits = []
        for a, score in zip(here, scores):
            place = anchor + (a[1] * QW - HALO) + iota((1, KW), 1)
            valid = (place >= 0) & (place < counts[a[0]])
            logits.append(jnp.where(valid, score * factor + term_s[a], MASKED))
        tops = [jnp.max(v, axis=-1, keepdims=True) for v in logits]
        raised = [jnp.exp(v - top) for v, top in zip(logits, tops)]
        totals = [jnp.sum(v, axis=-1, keepdims=True) for v in raised]
        for a, up, total in zip(here, raised, totals):
            probs = up * (1.0 / total)
            probs_s[a] = probs
            att_s[window_at(*a), :] = gather_heads(mm(probs.astype(BF16), values_of(*a)))

    steps(ATTEND_ITEMS, attend)

    def middle(i):
        n = MIDDLE_ITEMS
        at = rows_of(i, n)
        live = alive(i, n)
        att = att_s[at, :]
        gating = gating_s[at, :]
        cond_hat = chat_s[at, :]
        cond_rows = of_items(cond, i, n)
        gated = (gating * att).astype(BF16)
        branch = mm(gated, output_weight[...])
        zeros = mm(cond_rows, lanes(branch_gate[...], closing_gate[...]))
        zero_one = sigmoid(zeros[:, :width] + branch_lift[...])
        zero_two = sigmoid(zeros[:, width:] + closing_lift[...])
        live_one = live * zero_one
        live_two = live * zero_two
        mid = of_items(single, i, n).astype(F32) + live_one * branch
        mid_hat, mid_inv = normalize(mid)
        low2 = (cond_hat * second_gain[...]).astype(BF16)
        scale_shift = lanes(second_scale[...], second_shift[...])
        pre = mm(low2, scale_shift)
        scaling = sigmoid(pre[:, :width] + second_lift[...])
        second = (scaling * mid_hat + pre[:, width:]).astype(BF16)
        gate_up = lanes(hidden_gate[...], hidden_up[...])
        pre2 = mm(second, gate_up)
        inner = hidden_gate.shape[1]
        gate_pre, up_pre = pre2[:, :inner], pre2[:, inner:]
        gate_sig = sigmoid(gate_pre)
        gate_silu = gate_pre * gate_sig
        hidden = (gate_silu * up_pre).astype(BF16)
        closing = mm(hidden, hidden_down[...])
        layer_o[pl.ds(i, n)] = (
            (mid + live_two * closing).astype(BF16).reshape(n, length, width)
        )
        out_grad = of_items(cot, i, n).astype(F32)
        closing_full = out_grad * live_two
        closing_grad = closing_full.astype(BF16)
        zero_two_pre = closing_full * closing * (1.0 - zero_two)
        zero_two_low = zero_two_pre.astype(BF16)
        add1("hidden_down_a", t_mm(hidden, closing_grad))
        add_vector("closing_lift", col_sum(zero_two_pre))
        hidden_grad = mm_t(closing_grad, hidden_down[...])
        gate_pre_grad = (hidden_grad * up_pre * (gate_sig + gate_silu * (1.0 - gate_sig))).astype(
            BF16
        )
        up_pre_grad = (hidden_grad * gate_silu).astype(BF16)
        gate_up_grad = lanes(gate_pre_grad, up_pre_grad)
        wide_grad = t_mm(second, gate_up_grad)
        for k, name in enumerate(GROUP_ONE[:4]):
            add1(name, wide_grad[:, k * width : (k + 1) * width])
        second_grad = mm_t(gate_up_grad, gate_up)
        scaled_grad = second_grad * scaling
        before = scaled_grad * mid_hat * (1.0 - scaling)
        both = lanes(before.astype(BF16), second_grad.astype(BF16))
        both_grad = t_mm(low2, both)
        add1("second_scale", both_grad[:, :width])
        add1("second_shift", both_grad[:, width:])
        add_vector("second_lift", col_sum(before))
        cond_normed = mm_t(both, scale_shift)
        add_vector("second_gain", col_sum(cond_normed * cond_hat))
        cnorm_s[at, :] = cond_normed * second_gain[...]
        mid_grad = out_grad + normalize_back(mid_hat, mid_inv, scaled_grad)
        mid_grad_s[at, :] = mid_grad
        branch_full = mid_grad * live_one
        branch_grad = branch_full.astype(BF16)
        zero_one_pre = branch_full * branch * (1.0 - zero_one)
        add_vector("branch_lift", col_sum(zero_one_pre))
        zero_grads = lanes(zero_one_pre.astype(BF16), zero_two_low)
        gate_grads = t_mm(cond_rows, zero_grads)
        add1("branch_gate", gate_grads[:, :width])
        add1("closing_gate", gate_grads[:, width:])
        cdir_s[at, :] = mm_t(zero_grads, lanes(branch_gate[...], closing_gate[...]))
        add1("output_weight", t_mm(gated, branch_grad))
        attended_grad = mm_t(branch_grad, output_weight[...]) * gating
        dlow_s[at, :] = attended_grad.astype(BF16)
        gate_low = (attended_grad * att * (1.0 - gating)).astype(BF16)
        glow_s[at, :] = gate_low
        add1("gate_weight", t_mm(first_s[at, :], gate_low))

    steps(MIDDLE_ITEMS, middle)

    class Sum:
        def __init__(self, acc, send, recv, zall, red, sems):
            self.acc, self.send, self.recv, self.zall, self.red = acc, send, recv, zall, red
            self.rs_send, self.rs_recv, self.z_send, self.z_recv, self.ag_send, self.ag_recv = sems
            self.shard = send.shape[1]

        def scatter_copy(self, to, at):
            return pltpu.make_async_remote_copy(
                src_ref=self.send.at[to],
                dst_ref=self.recv.at[at],
                send_sem=self.rs_send.at[to],
                recv_sem=self.rs_recv.at[at],
                device_id={"atoms": to},
                device_id_type=MESH,
            )

        def dp_copy(self, to, at):
            return pltpu.make_async_remote_copy(
                src_ref=self.zall.at[me_d],
                dst_ref=self.zall.at[at],
                send_sem=self.z_send.at[to],
                recv_sem=self.z_recv.at[at],
                device_id={"dp": to},
                device_id_type=MESH,
            )

        def gather_copy(self, to, at):
            return pltpu.make_async_remote_copy(
                src_ref=self.red.at[me],
                dst_ref=self.red.at[at],
                send_sem=self.ag_send.at[to],
                recv_sem=self.ag_recv.at[at],
                device_id={"atoms": to},
                device_id_type=MESH,
            )

        def scatter(self):
            self.send[...] = self.acc[...].astype(BF16).reshape(self.send.shape)

            def go(k, carry):
                self.scatter_copy(lax.rem(me + k, n_a), me).start()
                return carry

            lax.fori_loop(1, n_a, go, 0)

        def over_dp(self):
            start = pl.multiple_of(me * self.shard, 16)
            total = self.acc[pl.ds(start, self.shard), :]
            for k in range(1, n_a):
                peer = lax.rem(me + k, n_a)
                self.scatter_copy(peer, peer).wait_recv()
                total = total + self.recv[peer].astype(F32)
            self.zall[me_d] = total.astype(BF16)

            def go(k, carry):
                self.dp_copy(lax.rem(me_d + k, n_d), me_d).start()
                return carry

            lax.fori_loop(1, n_d, go, 0)

        def gather(self):
            def come(k, carry):
                peer = lax.rem(me_d + k, n_d)
                self.dp_copy(peer, peer).wait_recv()
                return carry

            lax.fori_loop(1, n_d, come, 0)
            total = self.zall[0].astype(F32)
            for d in range(1, n_d):
                total = total + self.zall[d].astype(F32)
            self.red[me] = total.astype(BF16)

            def go(k, carry):
                self.gather_copy(lax.rem(me + k, n_a), me).start()
                return carry

            lax.fori_loop(1, n_a, go, 0)

        def finish(self):
            def end(k, carry):
                peer = lax.rem(me + k, n_a)
                self.gather_copy(peer, peer).wait_recv()
                self.gather_copy(peer, peer).wait_send()
                self.scatter_copy(peer, peer).wait_send()
                return carry

            lax.fori_loop(1, n_a, end, 0)

            def end_dp(k, carry):
                peer = lax.rem(me_d + k, n_d)
                self.dp_copy(peer, peer).wait_send()
                return carry

            lax.fori_loop(1, n_d, end_dp, 0)

    sum1 = Sum(
        acc1_s,
        send1,
        recv1,
        zall1,
        red1_s,
        (rs1_send, rs1_recv, z1_send, z1_recv, ag1_send, ag1_recv),
    )
    sum2 = Sum(
        acc2_s,
        send2,
        recv2,
        zall2,
        red2_s,
        (rs2_send, rs2_recv, z2_send, z2_recv, ag2_send, ag2_recv),
    )
    sum1.scatter()

    def halo_right(i):
        return pltpu.make_async_remote_copy(
            src_ref=halo_send.at[i, 1],
            dst_ref=halo_recv.at[i, 0],
            send_sem=hg_send_sem.at[i, 1],
            recv_sem=hg_recv_sem.at[i, 0],
            device_id={"atoms": lax.rem(me + 1, n_a)},
            device_id_type=MESH,
        )

    def halo_left(i):
        return pltpu.make_async_remote_copy(
            src_ref=halo_send.at[i, 0],
            dst_ref=halo_recv.at[i, 1],
            send_sem=hg_send_sem.at[i, 0],
            recv_sem=hg_recv_sem.at[i, 1],
            device_id={"atoms": lax.rem(me + n_a - 1, n_a)},
            device_id_type=MESH,
        )

    def attend_back(i):
        here = windows_of(i, BACK_ITEMS)
        wide_grads = [spread_heads(dlow_s[window_at(*a), :]) for a in here]
        probs_grads = [mm_t(wide, values_of(*a)) for a, wide in zip(here, wide_grads)]
        inners = [
            jnp.sum(grad * probs_s[a], axis=-1, keepdims=True)
            for a, grad in zip(here, probs_grads)
        ]
        value_parts = [t_mm(probs_s[a].astype(BF16), wide) for a, wide in zip(here, wide_grads)]
        key_parts = []
        for a, grad, inner in zip(here, probs_grads, inners):
            at = window_at(*a)
            logits_grad = probs_s[a] * (grad - inner)
            low = logits_grad.astype(BF16)
            dq_s[at, :] = gather_heads(mm(low, keys_of(*a))) * factor
            key_parts.append(t_mm(low, spread_heads(q_s[at, :])) * factor)
            inv = inv_s[at, :]
            by_head = logits_grad.reshape(heads, QW, KW)
            dl_s[a] = (by_head * inv[None]).astype(BF16).reshape(hq, KW)
            dot = jnp.sum(by_head * term_s[a].reshape(heads, QW, KW), axis=0)
            t_s[at, :] = dot * inv * inv * (1.0 / channels)
        for k in range(BACK_ITEMS):
            for parts, at in ((key_parts, 0), (value_parts, width)):
                part = parts[k * windows : (k + 1) * windows]
                for b in range(windows + SPREAD - 1):
                    block = None
                    for w in range(max(0, b - SPREAD + 1), min(windows - 1, b) + 1):
                        piece = part[w][(b - w) * QW : (b - w + 1) * QW]
                        block = piece if block is None else block + piece
                    kvg_s[i + k, b * QW : (b + 1) * QW, at : at + width] = block
            halo_send[i + k, 0] = kvg_s[i + k, 0:HALO, :].astype(BF16)
            halo_send[i + k, 1] = kvg_s[i + k, HALO + length : 2 * HALO + length, :].astype(BF16)

            @pl.when(has_right)
            def _(k=k):
                halo_right(i + k).start()

            @pl.when(has_left)
            def _(k=k):
                halo_left(i + k).start()

        pair_all = lanes(*[pair_rows(*a).reshape(cq, KW) for a in here])
        grads_all = lanes(*[dl_s[a] for a in here])
        pacc_s[...] += mm_t(pair_all, grads_all)

    steps(BACK_ITEMS, attend_back)

    diagonal = jnp.where(iota((cq, hq), 0) % QW == iota((cq, hq), 1) % QW, pacc_s[...], 0.0)
    by_channel = jnp.sum(diagonal.reshape(channels, QW, hq), axis=1)
    fold = jnp.where(iota((hq, width), 0) // QW == iota((hq, width), 1), 1.0, 0.0)
    pair_sums = mm(by_channel, fold, HIGHEST)
    acc2_s[pair_at : pair_at + channels, :] = pair_sums - jnp.mean(
        pair_sums, axis=0, keepdims=True
    )

    def finish_rows(i):
        n = FINISH_ITEMS
        at = rows_of(i, n)
        for k in range(n):

            @pl.when(has_left)
            def _(k=k):
                halo_right(i + k).wait_recv()

            @pl.when(has_right)
            def _(k=k):
                halo_left(i + k).wait_recv()

        owned = []
        for k in range(n):
            kvg_s[i + k, HALO : 2 * HALO, :] += halo_recv[i + k, 0].astype(F32)
            kvg_s[i + k, length : length + HALO, :] += halo_recv[i + k, 1].astype(F32)
            owned.append(kvg_s[i + k, HALO : HALO + length, :].astype(BF16))
        dq = dq_s[at, :]
        add_vector("query_bias", col_sum(dq))
        grads = lanes(dq.astype(BF16), rows(*owned), glow_s[at, :])
        first = first_s[at, :]
        weight_grads = t_mm(first, grads[:, : 3 * width])
        for k, name in enumerate(GROUP_TWO[:3]):
            add2(name, weight_grads[:, k * width : (k + 1) * width])
        first_grad = mm_t(
            grads, lanes(query_weight[...], key_weight[...], value_weight[...], gate_weight[...])
        )
        scaling = sig_s[at, :]
        single_hat = shat_s[at, :]
        cond_hat = chat_s[at, :]
        scaled_grad = first_grad * scaling
        before = scaled_grad * single_hat * (1.0 - scaling)
        both = lanes(before.astype(BF16), first_grad.astype(BF16))
        low1 = (cond_hat * first_gain[...]).astype(BF16)
        both_grad = t_mm(low1, both)
        add2("first_scale", both_grad[:, :width])
        add2("first_shift", both_grad[:, width:])
        add_vector("first_lift", col_sum(before))
        cond_normed = mm_t(both, lanes(first_scale[...], first_shift[...]))
        add_vector("first_gain", col_sum(cond_normed * cond_hat))
        atom_grad = mid_grad_s[at, :] + normalize_back(single_hat, sinv_s[at, :], scaled_grad)
        agrad_o[pl.ds(i, n)] = atom_grad.reshape(n, length, width)
        cond_grad = cond_normed * first_gain[...] + cnorm_s[at, :]
        cond_grad = normalize_back(cond_hat, cinv_s[at, :], cond_grad) + cdir_s[at, :]
        cgrad_o[pl.ds(i, n)] = cond_grad.reshape(n, length, width)

    steps(FINISH_ITEMS, finish_rows)

    def pair_back(i):
        wide = widet_s[...]
        for w in range(0, windows, 2):
            both = lanes(dl_s[i, w], dl_s[i, w + 1])
            product = mm(wide, rows(both, both))
            for v in (0, 1):
                at = window_at(i, w + v)
                block = pair_rows(i, w + v).astype(F32)
                part = product[:, v * KW : (v + 1) * KW].reshape(channels, QW, KW)
                pgrad_o[i, :, (w + v) * QW : (w + v + 1) * QW, :] = (
                    part - (block - mean_s[at, :][None]) * t_s[at, :][None]
                )

    def pair_part(part):
        low, high = part * items // 4, (part + 1) * items // 4

        def step(i, carry):
            pair_back(i)
            return carry

        lax.fori_loop(low, high, step, 0)

    sum2.scatter()
    sum1.over_dp()
    pair_part(0)
    sum2.over_dp()
    pair_part(1)
    sum1.gather()
    pair_part(2)
    sum2.gather()
    pair_part(3)
    sum1.finish()
    sum2.finish()

    def drain(i, carry):
        @pl.when(has_right)
        def _():
            halo_right(i).wait_send()

        @pl.when(has_left)
        def _():
            halo_left(i).wait_send()

        return carry

    lax.fori_loop(0, items, drain, 0)


GRADS = (
    "first_gain",
    "first_scale",
    "first_lift",
    "first_shift",
    "query_weight",
    "query_bias",
    "key_weight",
    "value_weight",
    "gate_weight",
    "pair_gain",
    "pair_weight",
    "output_weight",
    "branch_gate",
    "branch_lift",
    "second_gain",
    "second_scale",
    "second_lift",
    "second_shift",
    "hidden_gate",
    "hidden_up",
    "hidden_down",
    "closing_gate",
    "closing_lift",
)
SPLIT = {
    "hidden_gate": ("hidden_gate_a", "hidden_gate_b"),
    "hidden_up": ("hidden_up_a", "hidden_up_b"),
}


def results_kernel(
    pgrad_in,
    layer_in,
    agrad_in,
    cgrad_in,
    red1,
    red2,
    pair_gain,
    pair_weight,
    pgrad_o,
    layer_o,
    agrad_o,
    cgrad_o,
    *rest,
):
    grads = dict(zip(GRADS, rest[: len(GRADS)]))
    (sem,) = rest[len(GRADS) :]
    copies = [
        pltpu.make_async_copy(src, dst, sem.at[k])
        for k, (src, dst) in enumerate(
            (
                (pgrad_in, pgrad_o),
                (agrad_in, agrad_o),
                (cgrad_in, cgrad_o),
                (layer_in, layer_o),
            )
        )
    ]
    for copy in copies:
        copy.start()
    width = red1.shape[1]

    def one(name):
        at = GROUP_ONE.index(name) * width
        return red1[at : at + width, :].astype(F32)

    vector_at = len(GROUP_TWO) * width
    tail = red2[vector_at : vector_at + 32, :].astype(F32)
    for name in GRADS:
        ref = grads[name]
        if name in SPLIT:
            for k, part in enumerate(SPLIT[name]):
                ref[:, k * width : (k + 1) * width] = one(part)
        elif name == "hidden_down":
            ref[0:width, :] = one("hidden_down_a")
            ref[width : 2 * width, :] = one("hidden_down_b")
        elif name in GROUP_ONE:
            ref[...] = one(name)
        elif name in GROUP_TWO:
            at = GROUP_TWO.index(name) * width
            ref[...] = red2[at : at + width, :].astype(F32)
        elif name in VECTORS:
            at = VECTORS.index(name)
            ref[...] = tail[at : at + 1, :]
    heads, channels = pair_weight.shape
    eye = jnp.where(iota((channels, channels), 0) == iota((channels, channels), 1), 1.0, 0.0)
    sums = tail[8 : 8 + channels, :]
    pick = jnp.where(iota((heads, width), 0) == iota((heads, width), 1), 1.0, 0.0)
    turned = mm_t(pick, sums, HIGHEST)
    grads["pair_weight"][...] = turned * pair_gain[...]
    grads["pair_gain"][...] = jnp.sum(pair_weight[...] * turned, axis=0, keepdims=True)
    for copy in copies:
        copy.wait()


def shards(
    n_a,
    n_d,
    atom_single,
    atom_cond,
    atom_pair,
    atom_counts,
    cotangent,
    *params,
):
    items, length, width = atom_single.shape
    windows = length // QW
    channels = atom_pair.shape[1]
    named = dict(zip(GRADS, params))
    named["pair_weight"] = named["pair_weight"].T
    flat = [v.reshape(1, -1) if v.ndim == 1 else v for v in named.values()]
    heads = named["pair_weight"].shape[0]
    hq, cq = heads * QW, channels * QW
    rows1 = len(GROUP_ONE) * width
    rows2 = len(GROUP_TWO) * width + 8 + channels
    shard1, shard2 = shard_rows(rows1, n_a), shard_rows(rows2, n_a)

    vmem = pl.BlockSpec(memory_space=pltpu.VMEM)
    anywhere = pl.BlockSpec(memory_space=pl.ANY)
    by_items = (items, length, width)
    by_rows = (items * length, width)
    by_keys = (items * length, KW)
    ext = length + 2 * HALO
    dma = pltpu.SemaphoreType.DMA

    def in_hbm(value):
        return pltpu.with_memory_space_constraint(value, pltpu.HBM)

    def sds(shape, dtype):
        return jax.ShapeDtypeStruct(shape, dtype)

    outs = pl.pallas_call(
        functools.partial(main_kernel, n_a, n_d),
        out_shape=[
            pltpu.VMEM(by_items, BF16),
            pltpu.VMEM(by_items, F32),
            pltpu.VMEM(by_items, F32),
            pltpu.VMEM((items, channels, length, KW), F32),
            pltpu.VMEM((n_a, shard1, width), BF16),
            pltpu.VMEM((n_a, shard2, width), BF16),
        ],
        in_specs=[pl.BlockSpec(memory_space=pltpu.SMEM), vmem, vmem, vmem, anywhere]
        + [vmem] * len(flat),
        out_specs=[vmem] * 6,
        scratch_shapes=[
            pltpu.VMEM((items, channels, length, KW), BF16),
            pltpu.VMEM((items, ext, 2 * width), BF16),
            pltpu.VMEM(by_rows, BF16),
            pltpu.VMEM(by_rows, BF16),
            pltpu.VMEM(by_rows, F32),
            pltpu.VMEM(by_rows, F32),
            pltpu.VMEM(by_rows, F32),
            pltpu.VMEM(by_rows, F32),
            pltpu.VMEM(by_rows, F32),
            pltpu.VMEM(by_rows, F32),
            pltpu.VMEM((items, windows, hq, KW), F32),
            pltpu.VMEM((items, windows, hq, KW), F32),
            pltpu.VMEM(by_keys, F32),
            pltpu.VMEM(by_keys, F32),
            pltpu.VMEM(by_rows, F32),
            pltpu.VMEM(by_rows, F32),
            pltpu.VMEM(by_rows, F32),
            pltpu.VMEM(by_rows, F32),
            pltpu.VMEM(by_rows, BF16),
            pltpu.VMEM(by_rows, BF16),
            pltpu.VMEM((items, windows, hq, KW), BF16),
            pltpu.VMEM(by_keys, F32),
            pltpu.VMEM(by_rows, F32),
            pltpu.VMEM((items, ext, 2 * width), F32),
            pltpu.VMEM((2 * hq, cq), BF16),
            pltpu.VMEM((cq, 2 * hq), BF16),
            pltpu.VMEM((hq, width), BF16),
            pltpu.VMEM((cq, hq), F32),
            pltpu.VMEM((n_a * shard1, width), F32),
            pltpu.VMEM((n_a * shard2, width), F32),
            pltpu.VMEM((items, 2, HALO, 2 * width), BF16),
            pltpu.VMEM((items, 2, HALO, 2 * width), BF16),
            pltpu.VMEM((n_a, shard1, width), BF16),
            pltpu.VMEM((n_a, shard1, width), BF16),
            pltpu.VMEM((n_d, shard1, width), BF16),
            pltpu.VMEM((n_a, shard2, width), BF16),
            pltpu.VMEM((n_a, shard2, width), BF16),
            pltpu.VMEM((n_d, shard2, width), BF16),
            dma((items,)),
            dma((2,)),
            dma((2,)),
            dma((items, 2)),
            dma((items, 2)),
            dma((n_a,)),
            dma((n_a,)),
            dma((n_d,)),
            dma((n_d,)),
            dma((n_a,)),
            dma((n_a,)),
            dma((n_a,)),
            dma((n_a,)),
            dma((n_d,)),
            dma((n_d,)),
            dma((n_a,)),
            dma((n_a,)),
        ],
        compiler_params=pltpu.CompilerParams(
            collective_id=0, has_side_effects=True, vmem_limit_bytes=44 * 1024 * 1024
        ),
        name="block",
    )(*[in_hbm(v) for v in (atom_counts, atom_single, atom_cond, cotangent, atom_pair, *flat)])
    layer, agrad, cgrad, pgrad, red1, red2 = outs
    red1 = red1.reshape(n_a * shard1, width)
    red2 = red2.reshape(n_a * shard2, width)
    grad_shapes = [
        (1, v.shape[0]) if v.ndim == 1 else v.shape for v in (named[name] for name in GRADS)
    ]
    finals = pl.pallas_call(
        results_kernel,
        out_shape=[
            sds(atom_pair.shape, F32),
            sds(by_items, BF16),
            sds(by_items, F32),
            sds(by_items, F32),
        ]
        + [sds(shape, F32) for shape in grad_shapes],
        in_specs=[anywhere] * 4 + [vmem] * 4,
        out_specs=[anywhere] * 4 + [vmem] * len(GRADS),
        scratch_shapes=[dma((4,))],
        compiler_params=pltpu.CompilerParams(vmem_limit_bytes=16 * 1024 * 1024),
        name="results",
    )(
        pgrad,
        layer,
        agrad,
        cgrad,
        red1,
        red2,
        in_hbm(named["pair_gain"].reshape(1, -1)),
        in_hbm(named["pair_weight"]),
    )
    pgrad, layer, agrad, cgrad, *weight_grads = finals
    weight_grads = [
        g.T if n == "pair_weight" else g.reshape(named[n].shape)
        for g, n in zip(weight_grads, GRADS)
    ]
    return (layer, agrad, pgrad, cgrad, *weight_grads)


def solution(mesh):
    atoms = P("dp", "atoms", None)
    pair = P("dp", None, "atoms", None)
    return jax.shard_map(
        functools.partial(shards, mesh.shape["atoms"], mesh.shape["dp"]),
        mesh=mesh,
        in_specs=(atoms, atoms, pair, P("dp"), atoms) + (P(),) * len(GRADS),
        out_specs=(atoms, atoms, pair, atoms) + (P(),) * len(GRADS),
        check_vma=False,
    )
```

```python
import functools
from typing import Any, NamedTuple

import jax
import jax.numpy as jnp
from jax import lax
from jax.experimental import pallas as pl
from jax.experimental.pallas import tpu as pltpu
from jax.sharding import PartitionSpec as P

QW = 32
KW = 128
HALO = 48
SPREAD = KW // QW
EPSILON = 1e-05
MASKED = -1000000000.0
HIGHEST = lax.Precision.HIGHEST
MESH = pl.DeviceIdType.MESH
F32 = jnp.float32
BF16 = jnp.bfloat16
PROJECT_START = 4
PAIR_START = 1
ATTEND_START = 16
MIDDLE_START = 4
BACK_START = 16
FINISH_START = 4

HIDDEN_GATE, HIDDEN_UP, HIDDEN_DOWN = (0, 0), (0, 2), (0, 4)
OUTPUT, BRANCH, CLOSING, SECOND_SCALE, SECOND_SHIFT, GATE = [(1, k) for k in range(6)]
QUERY, KEY, VALUE = [(2, k) for k in range(3)]
FIRST_SCALE, FIRST_SHIFT = [(3, k) for k in range(2)]
BLOCKS = (6, 6, 3, 2)
SUMS = len(BLOCKS)
(
    V_FIRST_GAIN,
    V_FIRST_LIFT,
    V_QUERY_BIAS,
    V_BRANCH_LIFT,
    V_SECOND_GAIN,
    V_SECOND_LIFT,
    V_CLOSING_LIFT,
) = range(7)
VECTOR_ROWS = 8


class Params(NamedTuple):
    first_gain: Any
    first_scale: Any
    first_lift: Any
    first_shift: Any
    query_weight: Any
    query_bias: Any
    key_weight: Any
    value_weight: Any
    gate_weight: Any
    pair_gain: Any
    pair_weight: Any
    output_weight: Any
    branch_gate: Any
    branch_lift: Any
    second_gain: Any
    second_scale: Any
    second_lift: Any
    second_shift: Any
    hidden_gate: Any
    hidden_up: Any
    hidden_down: Any
    closing_gate: Any
    closing_lift: Any


EARLY_PARAMS = 11


class Inputs(NamedTuple):
    counts: Any
    pair: Any
    single: Any
    cond: Any
    cot: Any


class Outputs(NamedTuple):
    layer: Any
    agrad: Any
    cgrad: Any
    pgrad: Any
    gain: Any
    weight: Any


class Scratch(NamedTuple):
    counts: Any
    single: Any
    cond: Any
    cot: Any
    pair: Any
    keys: Any
    keys_grad: Any
    query: Any
    first: Any
    attended_low: Any
    gate_low: Any
    cond_hat: Any
    cond_inv: Any
    single_hat: Any
    single_inv: Any
    scaling: Any
    gating: Any
    attended: Any
    mid_grad: Any
    cond_normed: Any
    cond_direct: Any
    row_grad: Any
    pair_inv: Any
    pair_mean: Any
    term: Any
    probs: Any
    slopes: Any
    wide: Any
    wide_turned: Any
    head_mask: Any
    pair_sums: Any
    halo_send: Any
    halo_recv: Any
    in_sem: Any
    pair_sem: Any
    kv_send: Any
    kv_recv: Any
    hg_send: Any
    hg_recv: Any
    rs_send: Any
    rs_recv: Any
    ag_send: Any
    ag_recv: Any
    z_send: Any
    z_recv: Any


class SumScratch(NamedTuple):
    acc: Any
    send: Any
    recv: Any
    zall: Any


def mm(a, b, precision=None):
    return lax.dot_general(
        a, b, (((1,), (0,)), ((), ())), precision=precision, preferred_element_type=F32
    )


def mm_t(a, b, precision=None):
    return lax.dot_general(
        a, b, (((1,), (1,)), ((), ())), precision=precision, preferred_element_type=F32
    )


def t_mm(a, b):
    return lax.dot_general(a, b, (((0,), (0,)), ((), ())), preferred_element_type=F32)


def sigmoid(v):
    return 0.5 * jnp.tanh(0.5 * v) + 0.5


def lane_mean(v):
    return jnp.mean(v, axis=-1, keepdims=True)


def normalize(v):
    centre = v - lane_mean(v)
    inverse = lax.rsqrt(lane_mean(centre * centre) + EPSILON)
    return centre * inverse, jnp.broadcast_to(inverse, v.shape)


def normalize_back(normed, inverse, grads):
    return inverse * (grads - lane_mean(grads) - normed * lane_mean(grads * normed))


def lanes(*parts):
    return jnp.concatenate(parts, axis=1)


def rows(*parts):
    return jnp.concatenate(parts, axis=0)


def col_sum(v):
    return jnp.sum(v, axis=0, keepdims=True)


def iota(shape, axis):
    return lax.broadcasted_iota(jnp.int32, shape, axis)


def shard_rows(total, peers):
    return -(-total // (16 * peers)) * 16


def weave(parts, start):
    waiting, active = list(parts), []
    while waiting or active:
        active, waiting = active + waiting[:start], waiting[start:]
        going = []
        for part in active:
            try:
                next(part)
                going.append(part)
            except StopIteration:
                pass
        active = going


class Sum:
    def __init__(self, k, n_a, n_d, bufs, red, v):
        self.n_a, self.n_d = n_a, n_d
        self.me, self.me_d = lax.axis_index("atoms"), lax.axis_index("dp")
        self.acc, self.send, self.recv, self.zall = bufs
        self.red = red
        self.rs_send, self.rs_recv = v.rs_send.at[k], v.rs_recv.at[k]
        self.z_send, self.z_recv = v.z_send.at[k], v.z_recv.at[k]
        self.ag_send, self.ag_recv = v.ag_send.at[k], v.ag_recv.at[k]
        self.shard = self.send.shape[1]
        self.written = set()

    def add(self, block, value):
        at = slice(block * value.shape[1], block * value.shape[1] + value.shape[0])
        if block in self.written:
            self.acc[at, :] += value
        else:
            self.written.add(block)
            self.acc[at, :] = value

    def scatter_copy(self, to, at):
        return pltpu.make_async_remote_copy(
            src_ref=self.send.at[to],
            dst_ref=self.recv.at[at],
            send_sem=self.rs_send.at[to],
            recv_sem=self.rs_recv.at[at],
            device_id={"atoms": to},
            device_id_type=MESH,
        )

    def dp_copy(self, to, at):
        return pltpu.make_async_remote_copy(
            src_ref=self.zall.at[self.me_d],
            dst_ref=self.zall.at[at],
            send_sem=self.z_send.at[to],
            recv_sem=self.z_recv.at[at],
            device_id={"dp": to},
            device_id_type=MESH,
        )

    def gather_copy(self, to, at):
        return pltpu.make_async_remote_copy(
            src_ref=self.red.at[self.me],
            dst_ref=self.red.at[at],
            send_sem=self.ag_send.at[to],
            recv_sem=self.ag_recv.at[at],
            device_id={"atoms": to},
            device_id_type=MESH,
        )

    def each_atoms(self, body):
        def go(k, carry):
            body(lax.rem(self.me + k, self.n_a))
            return carry

        lax.fori_loop(1, self.n_a, go, 0)

    def each_dp(self, body):
        def go(k, carry):
            body(lax.rem(self.me_d + k, self.n_d))
            return carry

        lax.fori_loop(1, self.n_d, go, 0)

    def scatter(self):
        self.send[...] = self.acc[...].astype(BF16).reshape(self.send.shape)
        self.each_atoms(lambda peer: self.scatter_copy(peer, self.me).start())

    def over_dp(self):
        start = pl.multiple_of(self.me * self.shard, 16)
        total = self.acc[pl.ds(start, self.shard), :]
        for k in range(1, self.n_a):
            peer = lax.rem(self.me + k, self.n_a)
            self.scatter_copy(peer, peer).wait_recv()
            total = total + self.recv[peer].astype(F32)
        self.zall[self.me_d] = total.astype(BF16)
        self.each_dp(lambda peer: self.dp_copy(peer, self.me_d).start())
        self.each_atoms(lambda peer: self.scatter_copy(peer, peer).wait_send())

    def gather(self):
        self.each_dp(lambda peer: self.dp_copy(peer, peer).wait_recv())
        total = self.zall[0].astype(F32)
        for d in range(1, self.n_d):
            total = total + self.zall[d].astype(F32)
        self.red[self.me] = total.astype(BF16)
        self.each_atoms(lambda peer: self.gather_copy(peer, self.me).start())
        self.each_dp(lambda peer: self.dp_copy(peer, peer).wait_send())

    def finish(self):
        self.each_atoms(lambda peer: self.gather_copy(peer, peer).wait_recv())
        self.each_atoms(lambda peer: self.gather_copy(peer, peer).wait_send())


def main_kernel(n_a, n_d, *refs):
    def take(kind):
        nonlocal refs
        count = len(kind._fields)
        head, refs = refs[:count], refs[count:]
        return kind(*head)

    ins, params_in, out = take(Inputs), take(Params), take(Outputs)
    reds, refs = refs[:SUMS], refs[SUMS:]
    v, w_ = take(Scratch), take(Params)
    sums = [Sum(k, n_a, n_d, take(SumScratch), reds[k], v) for k in range(SUMS)]
    hidden_sum, middle_sum, qkv_sum, first_sum = sums

    items, length, width = v.single.shape
    windows = length // QW
    heads, channels = w_.pair_weight.shape
    head_dim = width // heads
    factor = head_dim ** (-0.5)
    me = lax.axis_index("atoms")
    me_d = lax.axis_index("dp")
    anchor = me * length
    has_left = me > 0
    has_right = me < n_a - 1

    pairs = [(ins.single, v.single), (ins.cond, v.cond)] + list(zip(params_in, w_))
    pairs += [(ins.cot, v.cot), (ins.counts, v.counts)]
    loads = [pltpu.make_async_copy(a, b, v.in_sem.at[k]) for k, (a, b) in enumerate(pairs)]
    early, late = loads[: 2 + EARLY_PARAMS], loads[2 + EARLY_PARAMS :]

    def pair_copy(i):
        return pltpu.make_async_copy(ins.pair.at[i], v.pair.at[i], v.pair_sem.at[i])

    for load in early:
        load.start()
    for i in range(items):
        pair_copy(i).start()
    for load in late:
        load.start()

    v.keys[:, 0:HALO, :] = jnp.zeros((items, HALO, 2 * width), BF16)
    v.keys[:, HALO + length : 2 * HALO + length, :] = jnp.zeros((items, HALO, 2 * width), BF16)
    v.halo_recv[...] = jnp.zeros(v.halo_recv.shape, BF16)

    barrier = pltpu.get_barrier_semaphore()

    def greet(axis, peer):
        pl.semaphore_signal(barrier, inc=1, device_id={axis: peer}, device_id_type=MESH)

    hidden_sum.each_atoms(functools.partial(greet, "atoms"))
    hidden_sum.each_dp(functools.partial(greet, "dp"))

    hq = heads * QW
    cq = channels * QW
    v.head_mask[...] = jnp.where(
        iota((hq, width), 0) // QW == iota((hq, width), 1) // head_dim, 1.0, 0.0
    ).astype(BF16)
    pick_head = jnp.where(iota((hq, heads), 0) // QW == iota((hq, heads), 1), 1.0, 0.0)
    spread = jnp.where(iota((channels, cq), 0) == iota((channels, cq), 1) // QW, 1.0, 0.0).astype(
        BF16
    )
    same_row = iota((hq, cq), 0) % QW == iota((hq, cq), 1) % QW
    for group, count in zip(sums, BLOCKS):
        unused = slice(0 if group is first_sum else count * width, group.acc.shape[0])
        if unused.start < unused.stop:
            group.acc[unused, :] = jnp.zeros((unused.stop - unused.start, width), F32)
    v.pair_sums[...] = jnp.zeros(v.pair_sums.shape, F32)
    for load in early:
        load.wait()
    out.gain[...] = w_.pair_gain[...]
    out.weight[...] = w_.pair_weight[...]
    weighted = mm(pick_head, w_.pair_weight[...], HIGHEST) * w_.pair_gain[...]
    weighted = weighted - lane_mean(weighted)
    high = weighted.astype(BF16)
    low = (weighted - high.astype(F32)).astype(BF16)
    wide_high = jnp.where(same_row, mm(high, spread), 0.0)
    wide_low = jnp.where(same_row, mm(low, spread), 0.0)
    v.wide[0:hq, :] = wide_high.astype(BF16)
    v.wide[hq : 2 * hq, :] = wide_low.astype(BF16)
    v.wide_turned[:, 0:hq] = wide_high.T.astype(BF16)
    v.wide_turned[:, hq : 2 * hq] = wide_low.T.astype(BF16)

    def add(place, value):
        sums[place[0]].add(place[1], value)

    vectors_at = BLOCKS[-1] * width
    pair_at = vectors_at + VECTOR_ROWS

    def add_vector(k, value):
        first_sum.acc[vectors_at + k : vectors_at + k + 1, :] += value

    def rows_of(i):
        return slice(i * length, (i + 1) * length)

    def alive(i):
        place = anchor + iota((length, width), 0)
        return jnp.where(place < v.counts[i], 1.0, 0.0)

    def project(i):
        at = rows_of(i)
        cond_hat, cond_inv = normalize(v.cond[i].astype(F32))
        v.cond_hat[at, :] = cond_hat
        v.cond_inv[at, :] = cond_inv
        low1 = (cond_hat * w_.first_gain[...]).astype(BF16)
        yield
        pre = mm(low1, lanes(w_.first_scale[...], w_.first_shift[...]))
        single_hat, single_inv = normalize(v.single[i].astype(F32))
        v.single_hat[at, :] = single_hat
        v.single_inv[at, :] = single_inv
        yield
        scaling = sigmoid(pre[:, :width] + w_.first_lift[...])
        v.scaling[at, :] = scaling
        first = (scaling * single_hat + pre[:, width:]).astype(BF16)
        v.first[at, :] = first
        yield
        key_value = mm(first, lanes(w_.key_weight[...], w_.value_weight[...]))
        query_gate = mm(first, lanes(w_.query_weight[...], w_.gate_weight[...]))
        yield
        v.keys[i, HALO : HALO + length, :] = key_value.astype(BF16)
        v.query[at, :] = (query_gate[:, :width] + w_.query_bias[...]).astype(BF16)
        v.gating[at, :] = sigmoid(query_gate[:, width:])

    weave([project(i) for i in range(items)], PROJECT_START)

    pl.semaphore_wait(barrier, n_a - 1 + n_d - 1)
    right, left = lax.rem(me + 1, n_a), lax.rem(me + n_a - 1, n_a)

    def to_right(src, dst, send_sem, recv_sem):
        return pltpu.make_async_remote_copy(
            src, dst, send_sem, recv_sem, device_id={"atoms": right}, device_id_type=MESH
        )

    def to_left(src, dst, send_sem, recv_sem):
        return pltpu.make_async_remote_copy(
            src, dst, send_sem, recv_sem, device_id={"atoms": left}, device_id_type=MESH
        )

    kv_right = to_right(
        v.keys.at[:, pl.ds(length, HALO), :],
        v.keys.at[:, pl.ds(0, HALO), :],
        v.kv_send.at[0],
        v.kv_recv.at[0],
    )
    kv_left = to_left(
        v.keys.at[:, pl.ds(HALO, HALO), :],
        v.keys.at[:, pl.ds(HALO + length, HALO), :],
        v.kv_send.at[1],
        v.kv_recv.at[1],
    )

    def where_right(*actions):
        @pl.when(has_right)
        def _():
            for action in actions:
                action()

    def where_left(*actions):
        @pl.when(has_left)
        def _():
            for action in actions:
                action()

    where_right(kv_right.start)
    where_left(kv_left.start)

    def window_at(i, w):
        at = i * length + w * QW
        return slice(at, at + QW)

    def pair_rows(i, w):
        return v.pair[i, :, w * QW : (w + 1) * QW, :]

    def pair_forward(i, w):
        both = lanes(pair_rows(i, w).reshape(cq, KW), pair_rows(i, w + 1).reshape(cq, KW))
        product = mm(v.wide[...], both)
        invs = []
        for u in (w, w + 1):
            block = pair_rows(i, u).astype(F32)
            mean = jnp.mean(block, axis=0)
            centre = block - mean[None]
            inv = lax.rsqrt(jnp.mean(centre * centre, axis=0) + EPSILON)
            v.pair_mean[window_at(i, u), :] = mean
            v.pair_inv[window_at(i, u), :] = inv
            invs.append(inv)
        yield
        product = product[:hq] + product[hq:]
        for u in (0, 1):
            part = product[:, u * KW : (u + 1) * KW].reshape(heads, QW, KW)
            v.term[i, w + u] = (part * invs[u][None]).reshape(hq, KW)

    for i in range(items):
        pair_copy(i).wait()
        weave([pair_forward(i, w) for w in range(0, windows, 2)], PAIR_START)

    inner = [w for w in range(windows) if w * QW >= HALO and (w + 1) * QW + HALO <= length]
    outer = [w for w in range(windows) if w not in inner]

    def every(ws):
        return [(i, w) for i in range(items) for w in ws]

    def spread_heads(block):
        return rows(*([block] * heads)) * v.head_mask[...]

    def gather_heads(wide_block):
        lane = iota((QW, width), 1)
        result = wide_block[(heads - 1) * QW :]
        for h in range(heads - 2, -1, -1):
            result = jnp.where(
                lane < (h + 1) * head_dim, wide_block[h * QW : (h + 1) * QW], result
            )
        return result

    def keys_of(i, w):
        return v.keys[i, w * QW : w * QW + KW, 0:width]

    def values_of(i, w):
        return v.keys[i, w * QW : w * QW + KW, width : 2 * width]

    def attend(i, w):
        at = window_at(i, w)
        scores = mm_t(spread_heads(v.query[at, :]), keys_of(i, w))
        yield
        place = anchor + (w * QW - HALO) + iota((1, KW), 1)
        valid = (place >= 0) & (place < v.counts[i])
        logits = jnp.where(valid, scores * factor + v.term[i, w], MASKED)
        top = jnp.max(logits, axis=-1, keepdims=True)
        yield
        raised = jnp.exp(logits - top)
        total = jnp.sum(raised, axis=-1, keepdims=True)
        yield
        probs = raised * (1.0 / total)
        v.probs[i, w] = probs
        attended = mm(probs.astype(BF16), values_of(i, w))
        yield
        v.attended[at, :] = gather_heads(attended)

    for load in late:
        load.wait()
    weave([attend(*a) for a in every(inner)], ATTEND_START)
    where_left(kv_right.wait_recv)
    where_right(kv_left.wait_recv)
    weave([attend(*a) for a in every(outer)], ATTEND_START)
    where_right(kv_right.wait_send)
    where_left(kv_left.wait_send)

    def middle(i):
        at = rows_of(i)
        cond_rows = v.cond[i]
        att = v.attended[at, :]
        gating = v.gating[at, :]
        gated = (gating * att).astype(BF16)
        branch = mm(gated, w_.output_weight[...])
        zeros = mm(cond_rows, lanes(w_.branch_gate[...], w_.closing_gate[...]))
        low2 = (v.cond_hat[at, :] * w_.second_gain[...]).astype(BF16)
        pre = mm(low2, lanes(w_.second_scale[...], w_.second_shift[...]))
        yield
        live = alive(i)
        zero_one = sigmoid(zeros[:, :width] + w_.branch_lift[...])
        zero_two = sigmoid(zeros[:, width:] + w_.closing_lift[...])
        live_one = live * zero_one
        live_two = live * zero_two
        mid = v.single[i].astype(F32) + live_one * branch
        mid_hat, mid_inv = normalize(mid)
        scaling = sigmoid(pre[:, :width] + w_.second_lift[...])
        second = (scaling * mid_hat + pre[:, width:]).astype(BF16)
        yield
        pre = mm(second, lanes(w_.hidden_gate[...], w_.hidden_up[...]))
        half = pre.shape[1] // 2
        gate_pre, up_pre = pre[:, :half], pre[:, half:]
        yield
        gate_sig = sigmoid(gate_pre)
        gate_silu = gate_pre * gate_sig
        hidden = (gate_silu * up_pre).astype(BF16)
        out_grad = v.cot[i].astype(F32)
        closing_full = out_grad * live_two
        closing_grad = closing_full.astype(BF16)
        yield
        closing = mm(hidden, w_.hidden_down[...])
        hidden_grad = mm_t(closing_grad, w_.hidden_down[...])
        add(HIDDEN_DOWN, t_mm(hidden, closing_grad))
        yield
        gate_slope = gate_sig + gate_silu * (1.0 - gate_sig)
        gate_pre_grad = (hidden_grad * up_pre * gate_slope).astype(BF16)
        up_pre_grad = (hidden_grad * gate_silu).astype(BF16)
        gate_up_grad = lanes(gate_pre_grad, up_pre_grad)
        yield
        second_grad = mm_t(gate_up_grad, lanes(w_.hidden_gate[...], w_.hidden_up[...]))
        wide_grad = t_mm(second, gate_up_grad)
        for k in range(4):
            add((0, k), wide_grad[:, k * width : (k + 1) * width])
        out.layer[i] = (mid + live_two * closing).astype(BF16)
        zero_two_pre = closing_full * closing * (1.0 - zero_two)
        add_vector(V_CLOSING_LIFT, col_sum(zero_two_pre))
        if i == items - 1:
            hidden_sum.scatter()
        yield
        scaled_grad = second_grad * scaling
        mid_grad = out_grad + normalize_back(mid_hat, mid_inv, scaled_grad)
        v.mid_grad[at, :] = mid_grad
        branch_full = mid_grad * live_one
        branch_grad = branch_full.astype(BF16)
        yield
        attended_grad = mm_t(branch_grad, w_.output_weight[...]) * gating
        v.attended_low[at, :] = attended_grad.astype(BF16)
        add(OUTPUT, t_mm(gated, branch_grad))
        before = scaled_grad * mid_hat * (1.0 - scaling)
        both = lanes(before.astype(BF16), second_grad.astype(BF16))
        add_vector(V_SECOND_LIFT, col_sum(before))
        both_grad = t_mm(low2, both)
        add(SECOND_SCALE, both_grad[:, :width])
        add(SECOND_SHIFT, both_grad[:, width:])
        cond_normed = mm_t(both, lanes(w_.second_scale[...], w_.second_shift[...]))
        yield
        gate_low = (attended_grad * att * (1.0 - gating)).astype(BF16)
        v.gate_low[at, :] = gate_low
        zero_one_pre = branch_full * branch * (1.0 - zero_one)
        add_vector(V_BRANCH_LIFT, col_sum(zero_one_pre))
        zero_grads = lanes(zero_one_pre.astype(BF16), zero_two_pre.astype(BF16))
        add(GATE, t_mm(v.first[at, :], gate_low))
        gate_grads = t_mm(cond_rows, zero_grads)
        add(BRANCH, gate_grads[:, :width])
        add(CLOSING, gate_grads[:, width:])
        v.cond_direct[at, :] = mm_t(zero_grads, lanes(w_.branch_gate[...], w_.closing_gate[...]))
        add_vector(V_SECOND_GAIN, col_sum(cond_normed * v.cond_hat[at, :]))
        v.cond_normed[at, :] = cond_normed * w_.second_gain[...]

    weave([middle(i) for i in range(items)], MIDDLE_START)

    def halo_right(i):
        return to_right(
            v.halo_send.at[i, 1], v.halo_recv.at[i, 0], v.hg_send.at[i, 1], v.hg_recv.at[i, 0]
        )

    def halo_left(i):
        return to_left(
            v.halo_send.at[i, 0], v.halo_recv.at[i, 1], v.hg_send.at[i, 0], v.hg_recv.at[i, 1]
        )

    folded = {}

    def attend_back(i, w):
        at = window_at(i, w)
        wide_grad = spread_heads(v.attended_low[at, :])
        probs_grad = mm_t(wide_grad, values_of(i, w))
        probs = v.probs[i, w]
        value_grad = t_mm(probs.astype(BF16), wide_grad)
        yield
        inner_sum = jnp.sum(probs_grad * probs, axis=-1, keepdims=True)
        yield
        logits_grad = probs * (probs_grad - inner_sum)
        low = logits_grad.astype(BF16)
        by_head = logits_grad.reshape(heads, QW, KW)
        v.slopes[i, w] = (by_head * v.pair_inv[at, :][None]).astype(BF16).reshape(hq, KW)
        v.probs[i, w] = logits_grad
        query_grad = mm(low, keys_of(i, w))
        key_grad = t_mm(low, spread_heads(v.query[at, :]))
        yield
        v.row_grad[at, :] = gather_heads(query_grad) * factor
        for k in range(SPREAD):
            piece = slice(k * QW, (k + 1) * QW)
            piece = (key_grad[piece], value_grad[piece])
            if (i, w + k) in folded:
                piece = [a + b for a, b in zip(folded[i, w + k], piece)]
            folded[i, w + k] = piece

    def fold(i, blocks):
        for b in blocks:
            key_grad, value_grad = folded.pop((i, b))
            v.keys_grad[i, b * QW : (b + 1) * QW, :width] = key_grad * factor
            v.keys_grad[i, b * QW : (b + 1) * QW, width:] = value_grad

    blocks = range(windows + SPREAD - 1)
    ends = -(-HALO // QW)
    weave([attend_back(*a) for a in every(outer)], BACK_START)
    for i in range(items):
        for side, at in ((0, blocks[:ends]), (1, blocks[-ends:])):
            for k in (0, 1):
                edge = rows(*[folded[i, b][k] for b in at])
                edge = edge[:HALO] if side == 0 else edge[-HALO:]
                if k == 0:
                    edge = edge * factor
                v.halo_send[i, side, :, k * width : (k + 1) * width] = edge.astype(BF16)
    where_right(*[halo_right(i).start for i in range(items)])
    where_left(*[halo_left(i).start for i in range(items)])
    middle_sum.scatter()
    weave([attend_back(*a) for a in every(inner)], BACK_START)
    for i in range(items):
        fold(i, blocks)
    for i in range(items):
        if i == items // 2:
            hidden_sum.over_dp()
        pair_all = lanes(*[pair_rows(i, w).reshape(cq, KW) for w in range(windows)])
        slopes_all = lanes(*[v.slopes[i, w] for w in range(windows)])
        for k in (0, 1):
            half = slice(k * cq // 2, (k + 1) * cq // 2)
            v.pair_sums[half, :] += mm_t(pair_all[half], slopes_all)

    diagonal = jnp.where(iota((cq, hq), 0) % QW == iota((cq, hq), 1) % QW, v.pair_sums[...], 0.0)
    by_channel = jnp.sum(diagonal.reshape(channels, QW, hq), axis=1)
    gather = jnp.where(iota((hq, width), 0) // QW == iota((hq, width), 1), 1.0, 0.0)
    channel_sums = mm(by_channel, gather, HIGHEST)
    first_sum.acc[pair_at : pair_at + channels, :] = channel_sums - jnp.mean(
        channel_sums, axis=0, keepdims=True
    )

    where_left(*[halo_right(i).wait_recv for i in range(items)])
    where_right(*[halo_left(i).wait_recv for i in range(items)])

    def finish_rows(i):
        at = rows_of(i)
        v.keys_grad[i, HALO : 2 * HALO, :] += v.halo_recv[i, 0].astype(F32)
        v.keys_grad[i, length : length + HALO, :] += v.halo_recv[i, 1].astype(F32)
        query_grad = v.row_grad[at, :]
        add_vector(V_QUERY_BIAS, col_sum(query_grad))
        key_value = v.keys_grad[i, HALO : HALO + length, :].astype(BF16)
        grads = lanes(query_grad.astype(BF16), key_value, v.gate_low[at, :])
        yield
        weight_grads = t_mm(v.first[at, :], grads[:, : 3 * width])
        for k in range(3):
            add((2, k), weight_grads[:, k * width : (k + 1) * width])
        if i == items - 1:
            qkv_sum.scatter()
        first_grad = mm_t(
            grads,
            lanes(
                w_.query_weight[...],
                w_.key_weight[...],
                w_.value_weight[...],
                w_.gate_weight[...],
            ),
        )
        yield
        scaling = v.scaling[at, :]
        scaled_grad = first_grad * scaling
        before = scaled_grad * v.single_hat[at, :] * (1.0 - scaling)
        both = lanes(before.astype(BF16), first_grad.astype(BF16))
        add_vector(V_FIRST_LIFT, col_sum(before))
        v.row_grad[at, :] = scaled_grad
        yield
        cond_hat = v.cond_hat[at, :]
        low1 = (cond_hat * w_.first_gain[...]).astype(BF16)
        both_grad = t_mm(low1, both)
        add(FIRST_SCALE, both_grad[:, :width])
        add(FIRST_SHIFT, both_grad[:, width:])
        cond_normed = mm_t(both, lanes(w_.first_scale[...], w_.first_shift[...]))
        add_vector(V_FIRST_GAIN, col_sum(cond_normed * cond_hat))
        v.cond_normed[at, :] += cond_normed * w_.first_gain[...]

    weave([finish_rows(i) for i in range(items)], FINISH_START)

    def close_rows(i):
        at = rows_of(i)
        atom_grad = normalize_back(v.single_hat[at, :], v.single_inv[at, :], v.row_grad[at, :])
        out.agrad[i] = v.mid_grad[at, :] + atom_grad
        cond_grad = normalize_back(v.cond_hat[at, :], v.cond_inv[at, :], v.cond_normed[at, :])
        out.cgrad[i] = cond_grad + v.cond_direct[at, :]

    def pair_back(i):
        wide = v.wide_turned[...]
        for w in range(0, windows, 2):
            both = lanes(v.slopes[i, w], v.slopes[i, w + 1])
            both = rows(both, both)
            half = cq // 2
            product = rows(mm(wide[:half], both), mm(wide[half:], both))
            for u in (0, 1):
                at = window_at(i, w + u)
                grad = v.probs[i, w + u] * v.term[i, w + u]
                dot = jnp.sum(grad.reshape(heads, QW, KW), axis=0)
                inv = v.pair_inv[at, :]
                slope = dot * inv * inv * (1.0 / channels)
                block = pair_rows(i, w + u).astype(F32)
                part = product[:, u * KW : (u + 1) * KW].reshape(channels, QW, KW)
                out.pgrad[i, :, (w + u) * QW : (w + u + 1) * QW, :] = (
                    part - (block - v.pair_mean[at, :][None]) * slope[None]
                )

    def close_part(part):
        for i in range(part * items // 4, (part + 1) * items // 4):
            close_rows(i)
            pair_back(i)

    first_sum.scatter()
    close_part(0)
    middle_sum.over_dp()
    close_part(1)
    close_part(2)
    hidden_sum.gather()
    qkv_sum.over_dp()
    first_sum.over_dp()
    close_part(3)
    where_right(*[halo_right(i).wait_send for i in range(items)])
    where_left(*[halo_left(i).wait_send for i in range(items)])
    middle_sum.gather()
    qkv_sum.gather()
    first_sum.gather()
    for group in sums:
        group.finish()


def results_kernel(*refs):
    ins = Outputs(*refs[:6])
    reds, refs = refs[6 : 6 + SUMS], refs[6 + SUMS :]
    (pgrad, layer, agrad, cgrad), refs = refs[:4], refs[4:]
    count = len(Params._fields)
    grads, stages = Params(*refs[:count]), refs[count : count + SUMS]
    vectors, weight_s, gain_s, sem = refs[count + SUMS :]
    copies = []

    def send(src, dst):
        copy = pltpu.make_async_copy(src, dst, sem.at[len(copies)])
        copy.start()
        copies.append(copy)

    send(ins.pgrad, pgrad)
    send(ins.agrad, agrad)
    send(ins.cgrad, cgrad)
    send(ins.layer, layer)
    for stage, red in zip(stages, reds):
        stage[...] = red[...].astype(F32)
    width = layer.shape[-1]

    def block(place, n=1):
        return stages[place[0]].at[pl.ds(place[1] * width, n * width), :]

    for place, ref in (
        (OUTPUT, grads.output_weight),
        (BRANCH, grads.branch_gate),
        (CLOSING, grads.closing_gate),
        (SECOND_SCALE, grads.second_scale),
        (SECOND_SHIFT, grads.second_shift),
        (GATE, grads.gate_weight),
        (QUERY, grads.query_weight),
        (KEY, grads.key_weight),
        (VALUE, grads.value_weight),
        (FIRST_SCALE, grads.first_scale),
        (FIRST_SHIFT, grads.first_shift),
    ):
        send(block(place), ref)
    send(block(HIDDEN_DOWN, 2), grads.hidden_down)
    for place, ref in ((HIDDEN_GATE, grads.hidden_gate), (HIDDEN_UP, grads.hidden_up)):
        for k in (0, 1):
            send(block((place[0], place[1] + k)), ref.at[:, pl.ds(k * width, width)])
    tail = stages[-1]
    vectors_at = BLOCKS[-1] * width
    for k, ref in (
        (V_FIRST_GAIN, grads.first_gain),
        (V_FIRST_LIFT, grads.first_lift),
        (V_QUERY_BIAS, grads.query_bias),
        (V_BRANCH_LIFT, grads.branch_lift),
        (V_SECOND_GAIN, grads.second_gain),
        (V_SECOND_LIFT, grads.second_lift),
        (V_CLOSING_LIFT, grads.closing_lift),
    ):
        vectors[k] = tail[vectors_at + k : vectors_at + k + 1, :]
        send(vectors.at[k], ref)
    heads, channels = ins.weight.shape
    pair_at = vectors_at + VECTOR_ROWS
    pick = jnp.where(iota((heads, width), 0) == iota((heads, width), 1), 1.0, 0.0)
    turned = mm_t(pick, tail[pair_at : pair_at + channels, :], HIGHEST)
    weight_s[...] = turned * ins.gain[...]
    gain_s[...] = jnp.sum(ins.weight[...] * turned, axis=0, keepdims=True)
    send(weight_s, grads.pair_weight)
    send(gain_s, grads.pair_gain)
    for copy in copies:
        copy.wait()


def shards(n_a, n_d, single, cond, pair, counts, cot, *params):
    items, length, width = single.shape
    windows = length // QW
    channels = pair.shape[1]
    params = Params(*params)
    flat = Params(
        *[p.reshape(1, -1) if p.ndim == 1 else p for p in params._replace(pair_weight=params.pair_weight.T)]
    )
    heads = flat.pair_weight.shape[0]
    hq, cq = heads * QW, channels * QW
    totals = [count * width for count in BLOCKS]
    totals[-1] += VECTOR_ROWS + channels
    shard = [shard_rows(total, n_a) for total in totals]

    vmem = pl.BlockSpec(memory_space=pltpu.VMEM)
    anywhere = pl.BlockSpec(memory_space=pl.ANY)
    by_items = (items, length, width)
    ext = length + 2 * HALO
    dma = pltpu.SemaphoreType.DMA

    def f32(*shape):
        return pltpu.VMEM(shape, F32)

    def bf16(*shape):
        return pltpu.VMEM(shape, BF16)

    by_rows = f32(items * length, width)
    by_rows_low = bf16(items * length, width)
    by_keys = f32(items * length, KW)
    by_window = f32(items, windows, hq, KW)
    scratch = Scratch(
        counts=pltpu.SMEM(counts.shape, counts.dtype),
        single=bf16(*by_items),
        cond=bf16(*by_items),
        cot=bf16(*by_items),
        pair=bf16(*pair.shape),
        keys=bf16(items, ext, 2 * width),
        keys_grad=f32(items, ext, 2 * width),
        query=by_rows_low,
        first=by_rows_low,
        attended_low=by_rows_low,
        gate_low=by_rows_low,
        cond_hat=by_rows,
        cond_inv=by_rows,
        single_hat=by_rows,
        single_inv=by_rows,
        scaling=by_rows,
        gating=by_rows,
        attended=by_rows,
        mid_grad=by_rows,
        cond_normed=by_rows,
        cond_direct=by_rows,
        row_grad=by_rows,
        pair_inv=by_keys,
        pair_mean=by_keys,
        term=by_window,
        probs=by_window,
        slopes=bf16(items, windows, hq, KW),
        wide=bf16(2 * hq, cq),
        wide_turned=bf16(cq, 2 * hq),
        head_mask=bf16(hq, width),
        pair_sums=f32(cq, hq),
        halo_send=bf16(items, 2, HALO, 2 * width),
        halo_recv=bf16(items, 2, HALO, 2 * width),
        in_sem=dma((4 + len(params),)),
        pair_sem=dma((items,)),
        kv_send=dma((2,)),
        kv_recv=dma((2,)),
        hg_send=dma((items, 2)),
        hg_recv=dma((items, 2)),
        rs_send=dma((SUMS, n_a)),
        rs_recv=dma((SUMS, n_a)),
        ag_send=dma((SUMS, n_a)),
        ag_recv=dma((SUMS, n_a)),
        z_send=dma((SUMS, n_d)),
        z_recv=dma((SUMS, n_d)),
    )
    sum_scratch = [
        SumScratch(
            acc=f32(n_a * size, width),
            send=bf16(n_a, size, width),
            recv=bf16(n_a, size, width),
            zall=bf16(n_d, size, width),
        )
        for size in shard
    ]

    def in_hbm(value):
        return pltpu.with_memory_space_constraint(value, pltpu.HBM)

    outs = pl.pallas_call(
        functools.partial(main_kernel, n_a, n_d),
        out_shape=[
            *Outputs(
                layer=bf16(*by_items),
                agrad=f32(*by_items),
                cgrad=f32(*by_items),
                pgrad=f32(*pair.shape),
                gain=f32(1, channels),
                weight=f32(heads, channels),
            ),
            *[bf16(n_a, size, width) for size in shard],
        ],
        in_specs=[anywhere] * (5 + len(params)),
        out_specs=[vmem] * (6 + SUMS),
        scratch_shapes=[
            *scratch,
            *[pltpu.VMEM(p.shape, p.dtype) for p in flat],
            *[buf for bufs in sum_scratch for buf in bufs],
        ],
        compiler_params=pltpu.CompilerParams(
            collective_id=0, has_side_effects=True, vmem_limit_bytes=48 * 1024 * 1024
        ),
        name="block",
    )(*[in_hbm(x) for x in (counts, pair, single, cond, cot, *flat)])
    kept = Outputs(*outs[:6])
    reds = [red.reshape(-1, width) for red in outs[6:]]

    def sds(shape, dtype):
        return jax.ShapeDtypeStruct(shape, dtype)

    pgrad, layer, agrad, cgrad, *grads = pl.pallas_call(
        results_kernel,
        out_shape=[
            sds(pair.shape, F32),
            sds(by_items, BF16),
            sds(by_items, F32),
            sds(by_items, F32),
            *[sds(p.shape, F32) for p in flat],
        ],
        in_specs=[anywhere] * 4 + [vmem] * (2 + SUMS),
        out_specs=[anywhere] * (4 + len(params)),
        scratch_shapes=[
            *[f32(n_a * size, width) for size in shard],
            f32(VECTOR_ROWS, 1, width),
            f32(heads, channels),
            f32(1, channels),
            dma((6 + len(params),)),
        ],
        compiler_params=pltpu.CompilerParams(vmem_limit_bytes=16 * 1024 * 1024),
        name="results",
    )(*kept, *reds)
    grads = Params(*grads)
    grads = grads._replace(pair_weight=grads.pair_weight.T)
    return (layer, agrad, pgrad, cgrad, *[g.reshape(p.shape) for g, p in zip(grads, params)])


def solution(mesh):
    atoms = P("dp", "atoms", None)
    pair = P("dp", None, "atoms", None)
    count = len(Params._fields)
    return jax.shard_map(
        functools.partial(shards, mesh.shape["atoms"], mesh.shape["dp"]),
        mesh=mesh,
        in_specs=(atoms, atoms, pair, P("dp"), atoms) + (P(),) * count,
        out_specs=(atoms, atoms, pair, atoms) + (P(),) * count,
        check_vma=False,
    )
```

```python
import functools
from typing import Any, NamedTuple

import jax
import jax.numpy as jnp
from jax import lax
from jax.experimental import pallas as pl
from jax.experimental.pallas import tpu as pltpu
from jax.sharding import PartitionSpec as P

QW = 32
KW = 128
HALO = 48
SPREAD = KW // QW
EPSILON = 1e-05
MASKED = -1000000000.0
HIGHEST = lax.Precision.HIGHEST
MESH = pl.DeviceIdType.MESH
F32 = jnp.float32
BF16 = jnp.bfloat16
PROJECT_START = 4
PAIR_START = 1
ATTEND_START = 16
MIDDLE_STEPS = 9
BACK_START = 16
FINISH_START = 4

HIDDEN_GATE, HIDDEN_UP, HIDDEN_DOWN = (0, 0), (0, 2), (0, 4)
OUTPUT, BRANCH, CLOSING, SECOND_SCALE, SECOND_SHIFT, GATE = [(1, k) for k in range(6)]
QUERY, KEY, VALUE = [(2, k) for k in range(3)]
FIRST_SCALE, FIRST_SHIFT = [(3, k) for k in range(2)]
BLOCKS = (6, 6, 3, 2)
SUMS = len(BLOCKS)
(
    V_FIRST_GAIN,
    V_FIRST_LIFT,
    V_QUERY_BIAS,
    V_BRANCH_LIFT,
    V_SECOND_GAIN,
    V_SECOND_LIFT,
    V_CLOSING_LIFT,
) = range(7)
VECTOR_ROWS = 8


class Params(NamedTuple):
    first_gain: Any
    first_scale: Any
    first_lift: Any
    first_shift: Any
    query_weight: Any
    query_bias: Any
    key_weight: Any
    value_weight: Any
    gate_weight: Any
    pair_gain: Any
    pair_weight: Any
    output_weight: Any
    branch_gate: Any
    branch_lift: Any
    second_gain: Any
    second_scale: Any
    second_lift: Any
    second_shift: Any
    hidden_gate: Any
    hidden_up: Any
    hidden_down: Any
    closing_gate: Any
    closing_lift: Any


EARLY_PARAMS = 11


class Inputs(NamedTuple):
    counts: Any
    pair: Any
    single: Any
    cond: Any
    cot: Any


class Outputs(NamedTuple):
    layer: Any
    agrad: Any
    cgrad: Any
    pgrad: Any
    gain: Any
    weight: Any


class Scratch(NamedTuple):
    counts: Any
    single: Any
    cond: Any
    cot: Any
    pair: Any
    keys: Any
    keys_grad: Any
    query: Any
    first: Any
    attended_low: Any
    gate_low: Any
    cond_hat: Any
    cond_inv: Any
    single_hat: Any
    single_inv: Any
    scaling: Any
    gating: Any
    attended: Any
    mid_grad: Any
    cond_normed: Any
    cond_direct: Any
    row_grad: Any
    pair_inv: Any
    pair_mean: Any
    term: Any
    probs: Any
    slopes: Any
    wide: Any
    wide_turned: Any
    head_mask: Any
    pair_sums: Any
    halo_send: Any
    halo_recv: Any
    in_sem: Any
    pair_sem: Any
    kv_send: Any
    kv_recv: Any
    hg_send: Any
    hg_recv: Any
    rs_send: Any
    rs_recv: Any
    ag_send: Any
    ag_recv: Any
    z_send: Any
    z_recv: Any


class SumScratch(NamedTuple):
    acc: Any
    send: Any
    recv: Any
    zall: Any


def mm(a, b, precision=None):
    return lax.dot_general(
        a, b, (((1,), (0,)), ((), ())), precision=precision, preferred_element_type=F32
    )


def mm_t(a, b, precision=None):
    return lax.dot_general(
        a, b, (((1,), (1,)), ((), ())), precision=precision, preferred_element_type=F32
    )


def t_mm(a, b):
    return lax.dot_general(a, b, (((0,), (0,)), ((), ())), preferred_element_type=F32)


def sigmoid(v):
    return 0.5 * jnp.tanh(0.5 * v) + 0.5


def lane_mean(v):
    return jnp.mean(v, axis=-1, keepdims=True)


def normalize(v):
    centre = v - lane_mean(v)
    inverse = lax.rsqrt(lane_mean(centre * centre) + EPSILON)
    return centre * inverse, jnp.broadcast_to(inverse, v.shape)


def normalize_back(normed, inverse, grads):
    return inverse * (grads - lane_mean(grads) - normed * lane_mean(grads * normed))


def lanes(*parts):
    return jnp.concatenate(parts, axis=1)


def rows(*parts):
    return jnp.concatenate(parts, axis=0)


def col_sum(v):
    return jnp.sum(v, axis=0, keepdims=True)


def iota(shape, axis):
    return lax.broadcasted_iota(jnp.int32, shape, axis)


def shard_rows(total, peers):
    return -(-total // (16 * peers)) * 16


def weave(parts, start):
    waiting, active = list(parts), []
    while waiting or active:
        active, waiting = active + waiting[:start], waiting[start:]
        going = []
        for part in active:
            try:
                next(part)
                going.append(part)
            except StopIteration:
                pass
        active = going


class Sum:
    def __init__(self, k, n_a, n_d, bufs, red, v):
        self.n_a, self.n_d = n_a, n_d
        self.me, self.me_d = lax.axis_index("atoms"), lax.axis_index("dp")
        self.acc, self.send, self.recv, self.zall = bufs
        self.red = red
        self.rs_send, self.rs_recv = v.rs_send.at[k], v.rs_recv.at[k]
        self.z_send, self.z_recv = v.z_send.at[k], v.z_recv.at[k]
        self.ag_send, self.ag_recv = v.ag_send.at[k], v.ag_recv.at[k]
        self.shard = self.send.shape[1]
        self.written = set()

    def add(self, block, value):
        at = slice(block * value.shape[1], block * value.shape[1] + value.shape[0])
        if block in self.written:
            self.acc[at, :] += value
        else:
            self.written.add(block)
            self.acc[at, :] = value

    def scatter_copy(self, to, at):
        return pltpu.make_async_remote_copy(
            src_ref=self.send.at[to],
            dst_ref=self.recv.at[at],
            send_sem=self.rs_send.at[to],
            recv_sem=self.rs_recv.at[at],
            device_id={"atoms": to},
            device_id_type=MESH,
        )

    def dp_copy(self, to, at):
        return pltpu.make_async_remote_copy(
            src_ref=self.zall.at[self.me_d],
            dst_ref=self.zall.at[at],
            send_sem=self.z_send.at[to],
            recv_sem=self.z_recv.at[at],
            device_id={"dp": to},
            device_id_type=MESH,
        )

    def gather_copy(self, to, at):
        return pltpu.make_async_remote_copy(
            src_ref=self.red.at[self.me],
            dst_ref=self.red.at[at],
            send_sem=self.ag_send.at[to],
            recv_sem=self.ag_recv.at[at],
            device_id={"atoms": to},
            device_id_type=MESH,
        )

    def each_atoms(self, body):
        def go(k, carry):
            body(lax.rem(self.me + k, self.n_a))
            return carry

        lax.fori_loop(1, self.n_a, go, 0)

    def each_dp(self, body):
        def go(k, carry):
            body(lax.rem(self.me_d + k, self.n_d))
            return carry

        lax.fori_loop(1, self.n_d, go, 0)

    def scatter(self):
        self.send[...] = self.acc[...].astype(BF16).reshape(self.send.shape)
        self.each_atoms(lambda peer: self.scatter_copy(peer, self.me).start())

    def over_dp(self):
        start = pl.multiple_of(self.me * self.shard, 16)
        total = self.acc[pl.ds(start, self.shard), :]
        for k in range(1, self.n_a):
            peer = lax.rem(self.me + k, self.n_a)
            self.scatter_copy(peer, peer).wait_recv()
            total = total + self.recv[peer].astype(F32)
        self.zall[self.me_d] = total.astype(BF16)
        self.each_dp(lambda peer: self.dp_copy(peer, self.me_d).start())
        self.each_atoms(lambda peer: self.scatter_copy(peer, peer).wait_send())

    def gather(self):
        self.each_dp(lambda peer: self.dp_copy(peer, peer).wait_recv())
        total = self.zall[0].astype(F32)
        for d in range(1, self.n_d):
            total = total + self.zall[d].astype(F32)
        self.red[self.me] = total.astype(BF16)
        self.each_atoms(lambda peer: self.gather_copy(peer, self.me).start())
        self.each_dp(lambda peer: self.dp_copy(peer, peer).wait_send())

    def finish(self):
        self.each_atoms(lambda peer: self.gather_copy(peer, peer).wait_recv())
        self.each_atoms(lambda peer: self.gather_copy(peer, peer).wait_send())


def main_kernel(n_a, n_d, *refs):
    def take(kind):
        nonlocal refs
        count = len(kind._fields)
        head, refs = refs[:count], refs[count:]
        return kind(*head)

    ins, params_in, out = take(Inputs), take(Params), take(Outputs)
    reds, refs = refs[:SUMS], refs[SUMS:]
    v, w_ = take(Scratch), take(Params)
    sums = [Sum(k, n_a, n_d, take(SumScratch), reds[k], v) for k in range(SUMS)]
    hidden_sum, middle_sum, qkv_sum, first_sum = sums

    items, length, width = v.single.shape
    windows = length // QW
    heads, channels = w_.pair_weight.shape
    head_dim = width // heads
    factor = head_dim ** (-0.5)
    me = lax.axis_index("atoms")
    me_d = lax.axis_index("dp")
    anchor = me * length
    has_left = me > 0
    has_right = me < n_a - 1

    pairs = [(ins.single, v.single), (ins.cond, v.cond)] + list(zip(params_in, w_))
    pairs += [(ins.cot, v.cot), (ins.counts, v.counts)]
    loads = [pltpu.make_async_copy(a, b, v.in_sem.at[k]) for k, (a, b) in enumerate(pairs)]
    early, late = loads[: 2 + EARLY_PARAMS], loads[2 + EARLY_PARAMS :]

    def pair_copy(i):
        return pltpu.make_async_copy(ins.pair.at[i], v.pair.at[i], v.pair_sem.at[i])

    for load in early:
        load.start()
    for i in range(items):
        pair_copy(i).start()
    for load in late:
        load.start()

    v.keys[:, 0:HALO, :] = jnp.zeros((items, HALO, 2 * width), BF16)
    v.keys[:, HALO + length : 2 * HALO + length, :] = jnp.zeros((items, HALO, 2 * width), BF16)
    v.halo_recv[...] = jnp.zeros(v.halo_recv.shape, BF16)

    barrier = pltpu.get_barrier_semaphore()

    def greet(axis, peer):
        pl.semaphore_signal(barrier, inc=1, device_id={axis: peer}, device_id_type=MESH)

    hidden_sum.each_atoms(functools.partial(greet, "atoms"))
    hidden_sum.each_dp(functools.partial(greet, "dp"))

    hq = heads * QW
    cq = channels * QW
    v.head_mask[...] = jnp.where(
        iota((hq, width), 0) // QW == iota((hq, width), 1) // head_dim, 1.0, 0.0
    ).astype(BF16)
    pick_head = jnp.where(iota((hq, heads), 0) // QW == iota((hq, heads), 1), 1.0, 0.0)
    spread = jnp.where(iota((channels, cq), 0) == iota((channels, cq), 1) // QW, 1.0, 0.0).astype(
        BF16
    )
    same_row = iota((hq, cq), 0) % QW == iota((hq, cq), 1) % QW
    for group, count in zip(sums, BLOCKS):
        unused = slice(0 if group is first_sum else count * width, group.acc.shape[0])
        if unused.start < unused.stop:
            group.acc[unused, :] = jnp.zeros((unused.stop - unused.start, width), F32)
    v.pair_sums[...] = jnp.zeros(v.pair_sums.shape, F32)
    for load in early:
        load.wait()
    out.gain[...] = w_.pair_gain[...]
    out.weight[...] = w_.pair_weight[...]
    weighted = mm(pick_head, w_.pair_weight[...], HIGHEST) * w_.pair_gain[...]
    weighted = weighted - lane_mean(weighted)
    high = weighted.astype(BF16)
    low = (weighted - high.astype(F32)).astype(BF16)
    wide_high = jnp.where(same_row, mm(high, spread), 0.0)
    wide_low = jnp.where(same_row, mm(low, spread), 0.0)
    v.wide[0:hq, :] = wide_high.astype(BF16)
    v.wide[hq : 2 * hq, :] = wide_low.astype(BF16)
    v.wide_turned[:, 0:hq] = wide_high.T.astype(BF16)
    v.wide_turned[:, hq : 2 * hq] = wide_low.T.astype(BF16)

    def add(place, value):
        sums[place[0]].add(place[1], value)

    vectors_at = BLOCKS[-1] * width
    pair_at = vectors_at + VECTOR_ROWS

    def add_vector(k, value):
        first_sum.acc[vectors_at + k : vectors_at + k + 1, :] += value

    def rows_of(i):
        return slice(i * length, (i + 1) * length)

    def alive(i):
        place = anchor + iota((length, width), 0)
        return jnp.where(place < v.counts[i], 1.0, 0.0)

    def project(i):
        at = rows_of(i)
        cond_hat, cond_inv = normalize(v.cond[i].astype(F32))
        v.cond_hat[at, :] = cond_hat
        v.cond_inv[at, :] = cond_inv
        low1 = (cond_hat * w_.first_gain[...]).astype(BF16)
        yield
        pre = mm(low1, lanes(w_.first_scale[...], w_.first_shift[...]))
        single_hat, single_inv = normalize(v.single[i].astype(F32))
        v.single_hat[at, :] = single_hat
        v.single_inv[at, :] = single_inv
        yield
        scaling = sigmoid(pre[:, :width] + w_.first_lift[...])
        v.scaling[at, :] = scaling
        first = (scaling * single_hat + pre[:, width:]).astype(BF16)
        v.first[at, :] = first
        yield
        key_value = mm(first, lanes(w_.key_weight[...], w_.value_weight[...]))
        query_gate = mm(first, lanes(w_.query_weight[...], w_.gate_weight[...]))
        yield
        v.keys[i, HALO : HALO + length, :] = key_value.astype(BF16)
        v.query[at, :] = (query_gate[:, :width] + w_.query_bias[...]).astype(BF16)
        v.gating[at, :] = sigmoid(query_gate[:, width:])

    weave([project(i) for i in range(items)], PROJECT_START)

    pl.semaphore_wait(barrier, n_a - 1 + n_d - 1)
    right, left = lax.rem(me + 1, n_a), lax.rem(me + n_a - 1, n_a)

    def to_right(src, dst, send_sem, recv_sem):
        return pltpu.make_async_remote_copy(
            src, dst, send_sem, recv_sem, device_id={"atoms": right}, device_id_type=MESH
        )

    def to_left(src, dst, send_sem, recv_sem):
        return pltpu.make_async_remote_copy(
            src, dst, send_sem, recv_sem, device_id={"atoms": left}, device_id_type=MESH
        )

    kv_right = to_right(
        v.keys.at[:, pl.ds(length, HALO), :],
        v.keys.at[:, pl.ds(0, HALO), :],
        v.kv_send.at[0],
        v.kv_recv.at[0],
    )
    kv_left = to_left(
        v.keys.at[:, pl.ds(HALO, HALO), :],
        v.keys.at[:, pl.ds(HALO + length, HALO), :],
        v.kv_send.at[1],
        v.kv_recv.at[1],
    )

    def where_right(*actions):
        @pl.when(has_right)
        def _():
            for action in actions:
                action()

    def where_left(*actions):
        @pl.when(has_left)
        def _():
            for action in actions:
                action()

    where_right(kv_right.start)
    where_left(kv_left.start)

    def window_at(i, w):
        at = i * length + w * QW
        return slice(at, at + QW)

    def pair_rows(i, w):
        return v.pair[i, :, w * QW : (w + 1) * QW, :]

    def pair_forward(i, w):
        both = lanes(pair_rows(i, w).reshape(cq, KW), pair_rows(i, w + 1).reshape(cq, KW))
        product = mm(v.wide[...], both)
        invs = []
        for u in (w, w + 1):
            block = pair_rows(i, u).astype(F32)
            mean = jnp.mean(block, axis=0)
            centre = block - mean[None]
            inv = lax.rsqrt(jnp.mean(centre * centre, axis=0) + EPSILON)
            v.pair_mean[window_at(i, u), :] = mean
            v.pair_inv[window_at(i, u), :] = inv
            invs.append(inv)
        yield
        product = product[:hq] + product[hq:]
        for u in (0, 1):
            part = product[:, u * KW : (u + 1) * KW].reshape(heads, QW, KW)
            v.term[i, w + u] = (part * invs[u][None]).reshape(hq, KW)

    for i in range(items):
        pair_copy(i).wait()
        weave([pair_forward(i, w) for w in range(0, windows, 2)], PAIR_START)

    inner = [w for w in range(windows) if w * QW >= HALO and (w + 1) * QW + HALO <= length]
    outer = [w for w in range(windows) if w not in inner]

    def every(ws):
        return [(i, w) for i in range(items) for w in ws]

    def spread_heads(block):
        return rows(*([block] * heads)) * v.head_mask[...]

    def gather_heads(wide_block):
        lane = iota((QW, width), 1)
        result = wide_block[(heads - 1) * QW :]
        for h in range(heads - 2, -1, -1):
            result = jnp.where(
                lane < (h + 1) * head_dim, wide_block[h * QW : (h + 1) * QW], result
            )
        return result

    def keys_of(i, w):
        return v.keys[i, w * QW : w * QW + KW, 0:width]

    def values_of(i, w):
        return v.keys[i, w * QW : w * QW + KW, width : 2 * width]

    def attend(i, w):
        at = window_at(i, w)
        scores = mm_t(spread_heads(v.query[at, :]), keys_of(i, w))
        yield
        place = anchor + (w * QW - HALO) + iota((1, KW), 1)
        valid = (place >= 0) & (place < v.counts[i])
        logits = jnp.where(valid, scores * factor + v.term[i, w], MASKED)
        top = jnp.max(logits, axis=-1, keepdims=True)
        yield
        raised = jnp.exp(logits - top)
        total = jnp.sum(raised, axis=-1, keepdims=True)
        yield
        probs = raised * (1.0 / total)
        v.probs[i, w] = probs
        attended = mm(probs.astype(BF16), values_of(i, w))
        yield
        v.attended[at, :] = gather_heads(attended)

    for load in late:
        load.wait()
    weave([attend(*a) for a in every(inner)], ATTEND_START)
    where_left(kv_right.wait_recv)
    where_right(kv_left.wait_recv)
    weave([attend(*a) for a in every(outer)], ATTEND_START)
    where_right(kv_right.wait_send)
    where_left(kv_left.wait_send)

    def middle(i):
        at = rows_of(i)
        cond_rows = v.cond[i]
        att = v.attended[at, :]
        gating = v.gating[at, :]
        gated = (gating * att).astype(BF16)
        branch = mm(gated, w_.output_weight[...])
        zeros = mm(cond_rows, lanes(w_.branch_gate[...], w_.closing_gate[...]))
        low2 = (v.cond_hat[at, :] * w_.second_gain[...]).astype(BF16)
        pre = mm(low2, lanes(w_.second_scale[...], w_.second_shift[...]))
        yield
        live = alive(i)
        zero_one = sigmoid(zeros[:, :width] + w_.branch_lift[...])
        zero_two = sigmoid(zeros[:, width:] + w_.closing_lift[...])
        live_one = live * zero_one
        live_two = live * zero_two
        mid = v.single[i].astype(F32) + live_one * branch
        mid_hat, mid_inv = normalize(mid)
        scaling = sigmoid(pre[:, :width] + w_.second_lift[...])
        second = (scaling * mid_hat + pre[:, width:]).astype(BF16)
        yield
        pre = mm(second, lanes(w_.hidden_gate[...], w_.hidden_up[...]))
        half = pre.shape[1] // 2
        gate_pre, up_pre = pre[:, :half], pre[:, half:]
        yield
        gate_sig = sigmoid(gate_pre)
        gate_silu = gate_pre * gate_sig
        hidden = (gate_silu * up_pre).astype(BF16)
        out_grad = v.cot[i].astype(F32)
        closing_full = out_grad * live_two
        closing_grad = closing_full.astype(BF16)
        yield
        closing = mm(hidden, w_.hidden_down[...])
        hidden_grad = mm_t(closing_grad, w_.hidden_down[...])
        add(HIDDEN_DOWN, t_mm(hidden, closing_grad))
        yield
        gate_slope = gate_sig + gate_silu * (1.0 - gate_sig)
        gate_pre_grad = (hidden_grad * up_pre * gate_slope).astype(BF16)
        up_pre_grad = (hidden_grad * gate_silu).astype(BF16)
        gate_up_grad = lanes(gate_pre_grad, up_pre_grad)
        yield
        second_grad = mm_t(gate_up_grad, lanes(w_.hidden_gate[...], w_.hidden_up[...]))
        wide_grad = t_mm(second, gate_up_grad)
        for k in range(4):
            add((0, k), wide_grad[:, k * width : (k + 1) * width])
        out.layer[i] = (mid + live_two * closing).astype(BF16)
        zero_two_pre = closing_full * closing * (1.0 - zero_two)
        add_vector(V_CLOSING_LIFT, col_sum(zero_two_pre))
        if i == items - 1:
            hidden_sum.scatter()
        yield
        scaled_grad = second_grad * scaling
        mid_grad = out_grad + normalize_back(mid_hat, mid_inv, scaled_grad)
        v.mid_grad[at, :] = mid_grad
        branch_full = mid_grad * live_one
        branch_grad = branch_full.astype(BF16)
        yield
        attended_grad = mm_t(branch_grad, w_.output_weight[...]) * gating
        v.attended_low[at, :] = attended_grad.astype(BF16)
        yield
        add(OUTPUT, t_mm(gated, branch_grad))
        before = scaled_grad * mid_hat * (1.0 - scaling)
        both = lanes(before.astype(BF16), second_grad.astype(BF16))
        add_vector(V_SECOND_LIFT, col_sum(before))
        both_grad = t_mm(low2, both)
        add(SECOND_SCALE, both_grad[:, :width])
        add(SECOND_SHIFT, both_grad[:, width:])
        cond_normed = mm_t(both, lanes(w_.second_scale[...], w_.second_shift[...]))
        yield
        gate_low = (attended_grad * att * (1.0 - gating)).astype(BF16)
        v.gate_low[at, :] = gate_low
        zero_one_pre = branch_full * branch * (1.0 - zero_one)
        add_vector(V_BRANCH_LIFT, col_sum(zero_one_pre))
        zero_grads = lanes(zero_one_pre.astype(BF16), zero_two_pre.astype(BF16))
        add(GATE, t_mm(v.first[at, :], gate_low))
        gate_grads = t_mm(cond_rows, zero_grads)
        add(BRANCH, gate_grads[:, :width])
        add(CLOSING, gate_grads[:, width:])
        v.cond_direct[at, :] = mm_t(zero_grads, lanes(w_.branch_gate[...], w_.closing_gate[...]))
        add_vector(V_SECOND_GAIN, col_sum(cond_normed * v.cond_hat[at, :]))
        v.cond_normed[at, :] = cond_normed * w_.second_gain[...]

    middles = [middle(i) for i in range(items)]
    for _ in range(MIDDLE_STEPS):
        for part in middles:
            next(part)

    def halo_right(i):
        return to_right(
            v.halo_send.at[i, 1], v.halo_recv.at[i, 0], v.hg_send.at[i, 1], v.hg_recv.at[i, 0]
        )

    def halo_left(i):
        return to_left(
            v.halo_send.at[i, 0], v.halo_recv.at[i, 1], v.hg_send.at[i, 0], v.hg_recv.at[i, 1]
        )

    folded = {}

    def attend_back(i, w):
        at = window_at(i, w)
        wide_grad = spread_heads(v.attended_low[at, :])
        probs_grad = mm_t(wide_grad, values_of(i, w))
        probs = v.probs[i, w]
        value_grad = t_mm(probs.astype(BF16), wide_grad)
        yield
        inner_sum = jnp.sum(probs_grad * probs, axis=-1, keepdims=True)
        yield
        logits_grad = probs * (probs_grad - inner_sum)
        low = logits_grad.astype(BF16)
        by_head = logits_grad.reshape(heads, QW, KW)
        v.slopes[i, w] = (by_head * v.pair_inv[at, :][None]).astype(BF16).reshape(hq, KW)
        v.probs[i, w] = logits_grad
        query_grad = mm(low, keys_of(i, w))
        key_grad = t_mm(low, spread_heads(v.query[at, :]))
        yield
        v.row_grad[at, :] = gather_heads(query_grad) * factor
        for k in range(SPREAD):
            piece = slice(k * QW, (k + 1) * QW)
            piece = (key_grad[piece], value_grad[piece])
            if (i, w + k) in folded:
                piece = [a + b for a, b in zip(folded[i, w + k], piece)]
            folded[i, w + k] = piece

    def fold(i, blocks):
        for b in blocks:
            key_grad, value_grad = folded.pop((i, b))
            v.keys_grad[i, b * QW : (b + 1) * QW, :width] = key_grad * factor
            v.keys_grad[i, b * QW : (b + 1) * QW, width:] = value_grad

    blocks = range(windows + SPREAD - 1)
    ends = -(-HALO // QW)
    for group in (range(items // 2), range(items // 2, items)):
        weave([attend_back(i, w) for i in group for w in outer], BACK_START)
        for i in group:
            for side, at in ((0, blocks[:ends]), (1, blocks[-ends:])):
                for k in (0, 1):
                    edge = rows(*[folded[i, b][k] for b in at])
                    edge = edge[:HALO] if side == 0 else edge[-HALO:]
                    if k == 0:
                        edge = edge * factor
                    v.halo_send[i, side, :, k * width : (k + 1) * width] = edge.astype(BF16)
        where_right(*[halo_right(i).start for i in group])
        where_left(*[halo_left(i).start for i in group])
    weave([attend_back(*a) for a in every(inner)], BACK_START)
    weave(middles, items)
    middle_sum.scatter()
    for i in range(items):
        fold(i, blocks)
    for i in range(items):
        if i == items // 2:
            hidden_sum.over_dp()
        pair_all = lanes(*[pair_rows(i, w).reshape(cq, KW) for w in range(windows)])
        slopes_all = lanes(*[v.slopes[i, w] for w in range(windows)])
        for k in (0, 1):
            half = slice(k * cq // 2, (k + 1) * cq // 2)
            v.pair_sums[half, :] += mm_t(pair_all[half], slopes_all)

    diagonal = jnp.where(iota((cq, hq), 0) % QW == iota((cq, hq), 1) % QW, v.pair_sums[...], 0.0)
    by_channel = jnp.sum(diagonal.reshape(channels, QW, hq), axis=1)
    gather = jnp.where(iota((hq, width), 0) // QW == iota((hq, width), 1), 1.0, 0.0)
    channel_sums = mm(by_channel, gather, HIGHEST)
    first_sum.acc[pair_at : pair_at + channels, :] = channel_sums - jnp.mean(
        channel_sums, axis=0, keepdims=True
    )

    def finish_rows(parts, last):
        def read(ref):
            return rows(*[ref[i * length + a : i * length + b, :] for i, a, b in parts])

        def write(ref, value):
            done = 0
            for i, a, b in parts:
                ref[i * length + a : i * length + b, :] = value[done : done + b - a]
                done += b - a

        query_grad = read(v.row_grad)
        add_vector(V_QUERY_BIAS, col_sum(query_grad))
        key_value = rows(*[v.keys_grad[i, HALO + a : HALO + b, :] for i, a, b in parts])
        grads = lanes(query_grad.astype(BF16), key_value.astype(BF16), read(v.gate_low))
        yield
        weight_grads = t_mm(read(v.first), grads[:, : 3 * width])
        for k in range(3):
            add((2, k), weight_grads[:, k * width : (k + 1) * width])
        if last:
            qkv_sum.scatter()
        first_grad = mm_t(
            grads,
            lanes(
                w_.query_weight[...],
                w_.key_weight[...],
                w_.value_weight[...],
                w_.gate_weight[...],
            ),
        )
        yield
        scaling = read(v.scaling)
        scaled_grad = first_grad * scaling
        before = scaled_grad * read(v.single_hat) * (1.0 - scaling)
        both = lanes(before.astype(BF16), first_grad.astype(BF16))
        add_vector(V_FIRST_LIFT, col_sum(before))
        write(v.row_grad, scaled_grad)
        yield
        cond_hat = read(v.cond_hat)
        low1 = (cond_hat * w_.first_gain[...]).astype(BF16)
        both_grad = t_mm(low1, both)
        add(FIRST_SCALE, both_grad[:, :width])
        add(FIRST_SHIFT, both_grad[:, width:])
        cond_normed = mm_t(both, lanes(w_.first_scale[...], w_.first_shift[...]))
        add_vector(V_FIRST_GAIN, col_sum(cond_normed * cond_hat))
        write(v.cond_normed, read(v.cond_normed) + cond_normed * w_.first_gain[...])

    weave(
        [finish_rows([(i, HALO, length - HALO)], False) for i in range(items)], FINISH_START
    )
    where_left(*[halo_right(i).wait_recv for i in range(items)])
    where_right(*[halo_left(i).wait_recv for i in range(items)])
    rim = []
    for i in range(items):
        v.keys_grad[i, HALO : 2 * HALO, :] += v.halo_recv[i, 0].astype(F32)
        v.keys_grad[i, length : length + HALO, :] += v.halo_recv[i, 1].astype(F32)
        rim += [(i, 0, HALO), (i, length - HALO, length)]
    weave([finish_rows(rim, True)], FINISH_START)

    def close_rows(i):
        at = rows_of(i)
        atom_grad = normalize_back(v.single_hat[at, :], v.single_inv[at, :], v.row_grad[at, :])
        out.agrad[i] = v.mid_grad[at, :] + atom_grad
        cond_grad = normalize_back(v.cond_hat[at, :], v.cond_inv[at, :], v.cond_normed[at, :])
        out.cgrad[i] = cond_grad + v.cond_direct[at, :]

    def pair_back(i):
        wide = v.wide_turned[...]
        for w in range(0, windows, 2):
            both = lanes(v.slopes[i, w], v.slopes[i, w + 1])
            both = rows(both, both)
            half = cq // 2
            product = rows(mm(wide[:half], both), mm(wide[half:], both))
            for u in (0, 1):
                at = window_at(i, w + u)
                grad = v.probs[i, w + u] * v.term[i, w + u]
                dot = jnp.sum(grad.reshape(heads, QW, KW), axis=0)
                inv = v.pair_inv[at, :]
                slope = dot * inv * inv * (1.0 / channels)
                block = pair_rows(i, w + u).astype(F32)
                part = product[:, u * KW : (u + 1) * KW].reshape(channels, QW, KW)
                out.pgrad[i, :, (w + u) * QW : (w + u + 1) * QW, :] = (
                    part - (block - v.pair_mean[at, :][None]) * slope[None]
                )

    def close_part(part):
        for i in range(part * items // 4, (part + 1) * items // 4):
            close_rows(i)
            pair_back(i)

    first_sum.scatter()
    close_part(0)
    middle_sum.over_dp()
    close_part(1)
    close_part(2)
    hidden_sum.gather()
    qkv_sum.over_dp()
    first_sum.over_dp()
    close_part(3)
    where_right(*[halo_right(i).wait_send for i in range(items)])
    where_left(*[halo_left(i).wait_send for i in range(items)])
    middle_sum.gather()
    qkv_sum.gather()
    first_sum.gather()
    for group in sums:
        group.finish()


def results_kernel(*refs):
    ins = Outputs(*refs[:6])
    reds, refs = refs[6 : 6 + SUMS], refs[6 + SUMS :]
    (pgrad, layer, agrad, cgrad), refs = refs[:4], refs[4:]
    count = len(Params._fields)
    grads, stages = Params(*refs[:count]), refs[count : count + SUMS]
    vectors, weight_s, gain_s, sem = refs[count + SUMS :]
    copies = []

    def send(src, dst):
        copy = pltpu.make_async_copy(src, dst, sem.at[len(copies)])
        copy.start()
        copies.append(copy)

    send(ins.pgrad, pgrad)
    send(ins.agrad, agrad)
    send(ins.cgrad, cgrad)
    send(ins.layer, layer)
    for stage, red in zip(stages, reds):
        stage[...] = red[...].astype(F32)
    width = layer.shape[-1]

    def block(place, n=1):
        return stages[place[0]].at[pl.ds(place[1] * width, n * width), :]

    for place, ref in (
        (OUTPUT, grads.output_weight),
        (BRANCH, grads.branch_gate),
        (CLOSING, grads.closing_gate),
        (SECOND_SCALE, grads.second_scale),
        (SECOND_SHIFT, grads.second_shift),
        (GATE, grads.gate_weight),
        (QUERY, grads.query_weight),
        (KEY, grads.key_weight),
        (VALUE, grads.value_weight),
        (FIRST_SCALE, grads.first_scale),
        (FIRST_SHIFT, grads.first_shift),
    ):
        send(block(place), ref)
    send(block(HIDDEN_DOWN, 2), grads.hidden_down)
    for place, ref in ((HIDDEN_GATE, grads.hidden_gate), (HIDDEN_UP, grads.hidden_up)):
        for k in (0, 1):
            send(block((place[0], place[1] + k)), ref.at[:, pl.ds(k * width, width)])
    tail = stages[-1]
    vectors_at = BLOCKS[-1] * width
    for k, ref in (
        (V_FIRST_GAIN, grads.first_gain),
        (V_FIRST_LIFT, grads.first_lift),
        (V_QUERY_BIAS, grads.query_bias),
        (V_BRANCH_LIFT, grads.branch_lift),
        (V_SECOND_GAIN, grads.second_gain),
        (V_SECOND_LIFT, grads.second_lift),
        (V_CLOSING_LIFT, grads.closing_lift),
    ):
        vectors[k] = tail[vectors_at + k : vectors_at + k + 1, :]
        send(vectors.at[k], ref)
    heads, channels = ins.weight.shape
    pair_at = vectors_at + VECTOR_ROWS
    pick = jnp.where(iota((heads, width), 0) == iota((heads, width), 1), 1.0, 0.0)
    turned = mm_t(pick, tail[pair_at : pair_at + channels, :], HIGHEST)
    weight_s[...] = turned * ins.gain[...]
    gain_s[...] = jnp.sum(ins.weight[...] * turned, axis=0, keepdims=True)
    send(weight_s, grads.pair_weight)
    send(gain_s, grads.pair_gain)
    for copy in copies:
        copy.wait()


def shards(n_a, n_d, single, cond, pair, counts, cot, *params):
    items, length, width = single.shape
    windows = length // QW
    channels = pair.shape[1]
    params = Params(*params)
    flat = Params(
        *[p.reshape(1, -1) if p.ndim == 1 else p for p in params._replace(pair_weight=params.pair_weight.T)]
    )
    heads = flat.pair_weight.shape[0]
    hq, cq = heads * QW, channels * QW
    totals = [count * width for count in BLOCKS]
    totals[-1] += VECTOR_ROWS + channels
    shard = [shard_rows(total, n_a) for total in totals]

    vmem = pl.BlockSpec(memory_space=pltpu.VMEM)
    anywhere = pl.BlockSpec(memory_space=pl.ANY)
    by_items = (items, length, width)
    ext = length + 2 * HALO
    dma = pltpu.SemaphoreType.DMA

    def f32(*shape):
        return pltpu.VMEM(shape, F32)

    def bf16(*shape):
        return pltpu.VMEM(shape, BF16)

    by_rows = f32(items * length, width)
    by_rows_low = bf16(items * length, width)
    by_keys = f32(items * length, KW)
    by_window = f32(items, windows, hq, KW)
    scratch = Scratch(
        counts=pltpu.SMEM(counts.shape, counts.dtype),
        single=bf16(*by_items),
        cond=bf16(*by_items),
        cot=bf16(*by_items),
        pair=bf16(*pair.shape),
        keys=bf16(items, ext, 2 * width),
        keys_grad=f32(items, ext, 2 * width),
        query=by_rows_low,
        first=by_rows_low,
        attended_low=by_rows_low,
        gate_low=by_rows_low,
        cond_hat=by_rows,
        cond_inv=by_rows,
        single_hat=by_rows,
        single_inv=by_rows,
        scaling=by_rows,
        gating=by_rows,
        attended=by_rows,
        mid_grad=by_rows,
        cond_normed=by_rows,
        cond_direct=by_rows,
        row_grad=by_rows,
        pair_inv=by_keys,
        pair_mean=by_keys,
        term=by_window,
        probs=by_window,
        slopes=bf16(items, windows, hq, KW),
        wide=bf16(2 * hq, cq),
        wide_turned=bf16(cq, 2 * hq),
        head_mask=bf16(hq, width),
        pair_sums=f32(cq, hq),
        halo_send=bf16(items, 2, HALO, 2 * width),
        halo_recv=bf16(items, 2, HALO, 2 * width),
        in_sem=dma((4 + len(params),)),
        pair_sem=dma((items,)),
        kv_send=dma((2,)),
        kv_recv=dma((2,)),
        hg_send=dma((items, 2)),
        hg_recv=dma((items, 2)),
        rs_send=dma((SUMS, n_a)),
        rs_recv=dma((SUMS, n_a)),
        ag_send=dma((SUMS, n_a)),
        ag_recv=dma((SUMS, n_a)),
        z_send=dma((SUMS, n_d)),
        z_recv=dma((SUMS, n_d)),
    )
    sum_scratch = [
        SumScratch(
            acc=f32(n_a * size, width),
            send=bf16(n_a, size, width),
            recv=bf16(n_a, size, width),
            zall=bf16(n_d, size, width),
        )
        for size in shard
    ]

    def in_hbm(value):
        return pltpu.with_memory_space_constraint(value, pltpu.HBM)

    outs = pl.pallas_call(
        functools.partial(main_kernel, n_a, n_d),
        out_shape=[
            *Outputs(
                layer=bf16(*by_items),
                agrad=f32(*by_items),
                cgrad=f32(*by_items),
                pgrad=f32(*pair.shape),
                gain=f32(1, channels),
                weight=f32(heads, channels),
            ),
            *[bf16(n_a, size, width) for size in shard],
        ],
        in_specs=[anywhere] * (5 + len(params)),
        out_specs=[vmem] * (6 + SUMS),
        scratch_shapes=[
            *scratch,
            *[pltpu.VMEM(p.shape, p.dtype) for p in flat],
            *[buf for bufs in sum_scratch for buf in bufs],
        ],
        compiler_params=pltpu.CompilerParams(
            collective_id=0, has_side_effects=True, vmem_limit_bytes=48 * 1024 * 1024
        ),
        name="block",
    )(*[in_hbm(x) for x in (counts, pair, single, cond, cot, *flat)])
    kept = Outputs(*outs[:6])
    reds = [red.reshape(-1, width) for red in outs[6:]]

    def sds(shape, dtype):
        return jax.ShapeDtypeStruct(shape, dtype)

    pgrad, layer, agrad, cgrad, *grads = pl.pallas_call(
        results_kernel,
        out_shape=[
            sds(pair.shape, F32),
            sds(by_items, BF16),
            sds(by_items, F32),
            sds(by_items, F32),
            *[sds(p.shape, F32) for p in flat],
        ],
        in_specs=[anywhere] * 4 + [vmem] * (2 + SUMS),
        out_specs=[anywhere] * (4 + len(params)),
        scratch_shapes=[
            *[f32(n_a * size, width) for size in shard],
            f32(VECTOR_ROWS, 1, width),
            f32(heads, channels),
            f32(1, channels),
            dma((6 + len(params),)),
        ],
        compiler_params=pltpu.CompilerParams(vmem_limit_bytes=16 * 1024 * 1024),
        name="results",
    )(*kept, *reds)
    grads = Params(*grads)
    grads = grads._replace(pair_weight=grads.pair_weight.T)
    return (layer, agrad, pgrad, cgrad, *[g.reshape(p.shape) for g, p in zip(grads, params)])


def solution(mesh):
    atoms = P("dp", "atoms", None)
    pair = P("dp", None, "atoms", None)
    count = len(Params._fields)
    return jax.shard_map(
        functools.partial(shards, mesh.shape["atoms"], mesh.shape["dp"]),
        mesh=mesh,
        in_specs=(atoms, atoms, pair, P("dp"), atoms) + (P(),) * count,
        out_specs=(atoms, atoms, pair, atoms) + (P(),) * count,
        check_vma=False,
    )
```

```python
import functools
from typing import Any, NamedTuple

import jax
import jax.numpy as jnp
from jax import lax
from jax.experimental import pallas as pl
from jax.experimental.pallas import tpu as pltpu
from jax.sharding import PartitionSpec as P

QW = 32
KW = 128
HALO = 48
SPREAD = KW // QW
EPSILON = 1e-05
MASKED = -1000000000.0
HIGHEST = lax.Precision.HIGHEST
MESH = pl.DeviceIdType.MESH
F32 = jnp.float32
BF16 = jnp.bfloat16
PROJECT_START = 4
PAIR_START = 1
ATTEND_START = 16
MIDDLE_STEPS = 9
BACK_START = 16
FINISH_START = 4
UNROLLED = 8

HIDDEN_GATE, HIDDEN_UP, HIDDEN_DOWN = (0, 0), (0, 2), (0, 4)
OUTPUT, BRANCH, CLOSING, SECOND_SCALE, SECOND_SHIFT, GATE = [(1, k) for k in range(6)]
QUERY, KEY, VALUE = [(2, k) for k in range(3)]
FIRST_SCALE, FIRST_SHIFT = [(3, k) for k in range(2)]
BLOCKS = (6, 6, 3, 2)
SUMS = len(BLOCKS)
(
    V_FIRST_GAIN,
    V_FIRST_LIFT,
    V_QUERY_BIAS,
    V_BRANCH_LIFT,
    V_SECOND_GAIN,
    V_SECOND_LIFT,
    V_CLOSING_LIFT,
) = range(7)
VECTOR_ROWS = 8


class Params(NamedTuple):
    first_gain: Any
    first_scale: Any
    first_lift: Any
    first_shift: Any
    query_weight: Any
    query_bias: Any
    key_weight: Any
    value_weight: Any
    gate_weight: Any
    pair_gain: Any
    pair_weight: Any
    output_weight: Any
    branch_gate: Any
    branch_lift: Any
    second_gain: Any
    second_scale: Any
    second_lift: Any
    second_shift: Any
    hidden_gate: Any
    hidden_up: Any
    hidden_down: Any
    closing_gate: Any
    closing_lift: Any


EARLY_PARAMS = 11


class Inputs(NamedTuple):
    counts: Any
    pair: Any
    single: Any
    cond: Any
    cot: Any


class Outputs(NamedTuple):
    layer: Any
    agrad: Any
    cgrad: Any
    pgrad: Any
    gain: Any
    weight: Any


class Scratch(NamedTuple):
    counts: Any
    single: Any
    cond: Any
    cot: Any
    pair: Any
    keys: Any
    keys_grad: Any
    query: Any
    first: Any
    attended_low: Any
    gate_low: Any
    cond_hat: Any
    cond_inv: Any
    single_hat: Any
    single_inv: Any
    scaling: Any
    gating: Any
    attended: Any
    mid_grad: Any
    cond_normed: Any
    cond_direct: Any
    row_grad: Any
    pair_inv: Any
    pair_mean: Any
    term: Any
    probs: Any
    slopes: Any
    wide: Any
    wide_turned: Any
    head_mask: Any
    pair_sums: Any
    halo_send: Any
    halo_recv: Any
    in_sem: Any
    pair_sem: Any
    kv_send: Any
    kv_recv: Any
    hg_send: Any
    hg_recv: Any
    rs_send: Any
    rs_recv: Any
    ag_send: Any
    ag_recv: Any
    z_send: Any
    z_recv: Any


class SumScratch(NamedTuple):
    acc: Any
    send: Any
    recv: Any
    zall: Any


def mm(a, b, precision=None):
    return lax.dot_general(
        a, b, (((1,), (0,)), ((), ())), precision=precision, preferred_element_type=F32
    )


def mm_t(a, b, precision=None):
    return lax.dot_general(
        a, b, (((1,), (1,)), ((), ())), precision=precision, preferred_element_type=F32
    )


def t_mm(a, b):
    return lax.dot_general(a, b, (((0,), (0,)), ((), ())), preferred_element_type=F32)


def sigmoid(v):
    return 0.5 * jnp.tanh(0.5 * v) + 0.5


def lane_mean(v):
    return jnp.mean(v, axis=-1, keepdims=True)


def normalize(v):
    centre = v - lane_mean(v)
    inverse = lax.rsqrt(lane_mean(centre * centre) + EPSILON)
    return centre * inverse, jnp.broadcast_to(inverse, v.shape)


def normalize_back(normed, inverse, grads):
    return inverse * (grads - lane_mean(grads) - normed * lane_mean(grads * normed))


def lanes(*parts):
    return jnp.concatenate(parts, axis=1)


def rows(*parts):
    return jnp.concatenate(parts, axis=0)


def col_sum(v):
    return jnp.sum(v, axis=0, keepdims=True)


def iota(shape, axis):
    return lax.broadcasted_iota(jnp.int32, shape, axis)


def shard_rows(total, peers):
    return -(-total // (16 * peers)) * 16


def weave(parts, start):
    waiting, active = list(parts), []
    while waiting or active:
        active, waiting = active + waiting[:start], waiting[start:]
        going = []
        for part in active:
            try:
                next(part)
                going.append(part)
            except StopIteration:
                pass
        active = going


class Sum:
    def __init__(self, k, n_a, n_d, bufs, red, v):
        self.n_a, self.n_d = n_a, n_d
        self.me, self.me_d = lax.axis_index("atoms"), lax.axis_index("dp")
        self.acc, self.send, self.recv, self.zall = bufs
        self.red = red
        self.rs_send, self.rs_recv = v.rs_send.at[k], v.rs_recv.at[k]
        self.z_send, self.z_recv = v.z_send.at[k], v.z_recv.at[k]
        self.ag_send, self.ag_recv = v.ag_send.at[k], v.ag_recv.at[k]
        self.shard = self.send.shape[1]
        self.written = set()

    def add(self, block, value):
        at = slice(block * value.shape[1], block * value.shape[1] + value.shape[0])
        if block in self.written:
            self.acc[at, :] += value
        else:
            self.written.add(block)
            self.acc[at, :] = value

    def scatter_copy(self, to, at):
        return pltpu.make_async_remote_copy(
            src_ref=self.send.at[to],
            dst_ref=self.recv.at[at],
            send_sem=self.rs_send.at[to],
            recv_sem=self.rs_recv.at[at],
            device_id={"atoms": to},
            device_id_type=MESH,
        )

    def dp_copy(self, to, at):
        return pltpu.make_async_remote_copy(
            src_ref=self.zall.at[self.me_d],
            dst_ref=self.zall.at[at],
            send_sem=self.z_send.at[to],
            recv_sem=self.z_recv.at[at],
            device_id={"dp": to},
            device_id_type=MESH,
        )

    def gather_copy(self, to, at):
        return pltpu.make_async_remote_copy(
            src_ref=self.red.at[self.me],
            dst_ref=self.red.at[at],
            send_sem=self.ag_send.at[to],
            recv_sem=self.ag_recv.at[at],
            device_id={"atoms": to},
            device_id_type=MESH,
        )

    def each(self, me, count, body):
        if count <= UNROLLED:
            for k in range(1, count):
                body(lax.rem(me + k, count))
            return

        def go(k, carry):
            body(lax.rem(me + k, count))
            return carry

        lax.fori_loop(1, count, go, 0)

    def each_atoms(self, body):
        self.each(self.me, self.n_a, body)

    def each_dp(self, body):
        self.each(self.me_d, self.n_d, body)

    def scatter(self):
        self.send[...] = self.acc[...].astype(BF16).reshape(self.send.shape)
        self.each_atoms(lambda peer: self.scatter_copy(peer, self.me).start())

    def over_dp(self):
        start = pl.multiple_of(self.me * self.shard, 16)
        total = self.acc[pl.ds(start, self.shard), :]
        for k in range(1, self.n_a):
            peer = lax.rem(self.me + k, self.n_a)
            self.scatter_copy(peer, peer).wait_recv()
            total = total + self.recv[peer].astype(F32)
        self.zall[self.me_d] = total.astype(BF16)
        self.each_dp(lambda peer: self.dp_copy(peer, self.me_d).start())
        self.each_atoms(lambda peer: self.scatter_copy(peer, peer).wait_send())

    def gather(self):
        self.each_dp(lambda peer: self.dp_copy(peer, peer).wait_recv())
        total = self.zall[0].astype(F32)
        for d in range(1, self.n_d):
            total = total + self.zall[d].astype(F32)
        self.red[self.me] = total.astype(BF16)
        self.each_atoms(lambda peer: self.gather_copy(peer, self.me).start())
        self.each_dp(lambda peer: self.dp_copy(peer, peer).wait_send())

    def finish(self):
        self.each_atoms(lambda peer: self.gather_copy(peer, peer).wait_recv())
        self.each_atoms(lambda peer: self.gather_copy(peer, peer).wait_send())


def main_kernel(n_a, n_d, *refs):
    def take(kind):
        nonlocal refs
        count = len(kind._fields)
        head, refs = refs[:count], refs[count:]
        return kind(*head)

    ins, params_in, out = take(Inputs), take(Params), take(Outputs)
    reds, refs = refs[:SUMS], refs[SUMS:]
    v, w_ = take(Scratch), take(Params)
    sums = [Sum(k, n_a, n_d, take(SumScratch), reds[k], v) for k in range(SUMS)]
    hidden_sum, middle_sum, qkv_sum, first_sum = sums

    items, length, width = v.single.shape
    windows = length // QW
    heads, channels = w_.pair_weight.shape
    head_dim = width // heads
    factor = head_dim ** (-0.5)
    me = lax.axis_index("atoms")
    me_d = lax.axis_index("dp")
    anchor = me * length
    has_left = me > 0
    has_right = me < n_a - 1

    pairs = [(ins.single, v.single), (ins.cond, v.cond)] + list(zip(params_in, w_))
    pairs += [(ins.cot, v.cot), (ins.counts, v.counts)]
    loads = [pltpu.make_async_copy(a, b, v.in_sem.at[k]) for k, (a, b) in enumerate(pairs)]
    early, late = loads[: 2 + EARLY_PARAMS], loads[2 + EARLY_PARAMS :]

    def pair_copy(i):
        return pltpu.make_async_copy(ins.pair.at[i], v.pair.at[i], v.pair_sem.at[i])

    for load in early:
        load.start()
    for i in range(items):
        pair_copy(i).start()
    for load in late:
        load.start()

    v.keys[:, 0:HALO, :] = jnp.zeros((items, HALO, 2 * width), BF16)
    v.keys[:, HALO + length : 2 * HALO + length, :] = jnp.zeros((items, HALO, 2 * width), BF16)
    v.halo_recv[...] = jnp.zeros(v.halo_recv.shape, BF16)

    barrier = pltpu.get_barrier_semaphore()

    def greet(axis, peer):
        pl.semaphore_signal(barrier, inc=1, device_id={axis: peer}, device_id_type=MESH)

    hidden_sum.each_atoms(functools.partial(greet, "atoms"))
    hidden_sum.each_dp(functools.partial(greet, "dp"))

    hq = heads * QW
    cq = channels * QW
    v.head_mask[...] = jnp.where(
        iota((hq, width), 0) // QW == iota((hq, width), 1) // head_dim, 1.0, 0.0
    ).astype(BF16)
    pick_head = jnp.where(iota((hq, heads), 0) // QW == iota((hq, heads), 1), 1.0, 0.0)
    spread = jnp.where(iota((channels, cq), 0) == iota((channels, cq), 1) // QW, 1.0, 0.0).astype(
        BF16
    )
    same_row = iota((hq, cq), 0) % QW == iota((hq, cq), 1) % QW
    for group, count in zip(sums, BLOCKS):
        unused = slice(0 if group is first_sum else count * width, group.acc.shape[0])
        if unused.start < unused.stop:
            group.acc[unused, :] = jnp.zeros((unused.stop - unused.start, width), F32)
    v.pair_sums[...] = jnp.zeros(v.pair_sums.shape, F32)
    for load in early:
        load.wait()
    out.gain[...] = w_.pair_gain[...]
    out.weight[...] = w_.pair_weight[...]
    weighted = mm(pick_head, w_.pair_weight[...], HIGHEST) * w_.pair_gain[...]
    weighted = weighted - lane_mean(weighted)
    high = weighted.astype(BF16)
    low = (weighted - high.astype(F32)).astype(BF16)
    wide_high = jnp.where(same_row, mm(high, spread), 0.0)
    wide_low = jnp.where(same_row, mm(low, spread), 0.0)
    v.wide[0:hq, :] = wide_high.astype(BF16)
    v.wide[hq : 2 * hq, :] = wide_low.astype(BF16)
    v.wide_turned[:, 0:hq] = wide_high.T.astype(BF16)
    v.wide_turned[:, hq : 2 * hq] = wide_low.T.astype(BF16)

    def add(place, value):
        sums[place[0]].add(place[1], value)

    vectors_at = BLOCKS[-1] * width
    pair_at = vectors_at + VECTOR_ROWS

    def add_vector(k, value):
        first_sum.acc[vectors_at + k : vectors_at + k + 1, :] += value

    def rows_of(i):
        return slice(i * length, (i + 1) * length)

    def alive(i):
        place = anchor + iota((length, width), 0)
        return jnp.where(place < v.counts[i], 1.0, 0.0)

    def project(i):
        at = rows_of(i)
        cond_hat, cond_inv = normalize(v.cond[i].astype(F32))
        v.cond_hat[at, :] = cond_hat
        v.cond_inv[at, :] = cond_inv
        low1 = (cond_hat * w_.first_gain[...]).astype(BF16)
        yield
        pre = mm(low1, lanes(w_.first_scale[...], w_.first_shift[...]))
        single_hat, single_inv = normalize(v.single[i].astype(F32))
        v.single_hat[at, :] = single_hat
        v.single_inv[at, :] = single_inv
        yield
        scaling = sigmoid(pre[:, :width] + w_.first_lift[...])
        v.scaling[at, :] = scaling
        first = (scaling * single_hat + pre[:, width:]).astype(BF16)
        v.first[at, :] = first
        yield
        key_value = mm(first, lanes(w_.key_weight[...], w_.value_weight[...]))
        query_gate = mm(first, lanes(w_.query_weight[...], w_.gate_weight[...]))
        yield
        v.keys[i, HALO : HALO + length, :] = key_value.astype(BF16)
        v.query[at, :] = (query_gate[:, :width] + w_.query_bias[...]).astype(BF16)
        v.gating[at, :] = sigmoid(query_gate[:, width:])

    weave([project(i) for i in range(items)], PROJECT_START)

    pl.semaphore_wait(barrier, n_a - 1 + n_d - 1)
    right, left = lax.rem(me + 1, n_a), lax.rem(me + n_a - 1, n_a)

    def to_right(src, dst, send_sem, recv_sem):
        return pltpu.make_async_remote_copy(
            src, dst, send_sem, recv_sem, device_id={"atoms": right}, device_id_type=MESH
        )

    def to_left(src, dst, send_sem, recv_sem):
        return pltpu.make_async_remote_copy(
            src, dst, send_sem, recv_sem, device_id={"atoms": left}, device_id_type=MESH
        )

    kv_right = to_right(
        v.keys.at[:, pl.ds(length, HALO), :],
        v.keys.at[:, pl.ds(0, HALO), :],
        v.kv_send.at[0],
        v.kv_recv.at[0],
    )
    kv_left = to_left(
        v.keys.at[:, pl.ds(HALO, HALO), :],
        v.keys.at[:, pl.ds(HALO + length, HALO), :],
        v.kv_send.at[1],
        v.kv_recv.at[1],
    )

    def where_right(*actions):
        @pl.when(has_right)
        def _():
            for action in actions:
                action()

    def where_left(*actions):
        @pl.when(has_left)
        def _():
            for action in actions:
                action()

    where_right(kv_right.start)
    where_left(kv_left.start)

    def window_at(i, w):
        at = i * length + w * QW
        return slice(at, at + QW)

    def pair_rows(i, w):
        return v.pair[i, :, w * QW : (w + 1) * QW, :]

    def pair_forward(i, w):
        both = lanes(pair_rows(i, w).reshape(cq, KW), pair_rows(i, w + 1).reshape(cq, KW))
        product = mm(v.wide[...], both)
        invs = []
        for u in (w, w + 1):
            block = pair_rows(i, u).astype(F32)
            mean = jnp.mean(block, axis=0)
            centre = block - mean[None]
            inv = lax.rsqrt(jnp.mean(centre * centre, axis=0) + EPSILON)
            v.pair_mean[window_at(i, u), :] = mean
            v.pair_inv[window_at(i, u), :] = inv
            invs.append(inv)
        yield
        product = product[:hq] + product[hq:]
        for u in (0, 1):
            part = product[:, u * KW : (u + 1) * KW].reshape(heads, QW, KW)
            v.term[i, w + u] = (part * invs[u][None]).reshape(hq, KW)

    for i in range(items):
        pair_copy(i).wait()
        weave([pair_forward(i, w) for w in range(0, windows, 2)], PAIR_START)

    inner = [w for w in range(windows) if w * QW >= HALO and (w + 1) * QW + HALO <= length]
    outer = [w for w in range(windows) if w not in inner]

    def every(ws):
        return [(i, w) for i in range(items) for w in ws]

    def spread_heads(block):
        return rows(*([block] * heads)) * v.head_mask[...]

    def gather_heads(wide_block):
        lane = iota((QW, width), 1)
        result = wide_block[(heads - 1) * QW :]
        for h in range(heads - 2, -1, -1):
            result = jnp.where(
                lane < (h + 1) * head_dim, wide_block[h * QW : (h + 1) * QW], result
            )
        return result

    def keys_of(i, w):
        return v.keys[i, w * QW : w * QW + KW, 0:width]

    def values_of(i, w):
        return v.keys[i, w * QW : w * QW + KW, width : 2 * width]

    def attend(i, w):
        at = window_at(i, w)
        scores = mm_t(spread_heads(v.query[at, :]), keys_of(i, w))
        yield
        place = anchor + (w * QW - HALO) + iota((1, KW), 1)
        valid = (place >= 0) & (place < v.counts[i])
        logits = jnp.where(valid, scores * factor + v.term[i, w], MASKED)
        top = jnp.max(logits, axis=-1, keepdims=True)
        yield
        raised = jnp.exp(logits - top)
        total = jnp.sum(raised, axis=-1, keepdims=True)
        yield
        probs = raised * (1.0 / total)
        v.probs[i, w] = probs
        attended = mm(probs.astype(BF16), values_of(i, w))
        yield
        v.attended[at, :] = gather_heads(attended)

    for load in late:
        load.wait()
    weave([attend(*a) for a in every(inner)], ATTEND_START)
    where_left(kv_right.wait_recv)
    where_right(kv_left.wait_recv)
    weave([attend(*a) for a in every(outer)], ATTEND_START)
    where_right(kv_right.wait_send)
    where_left(kv_left.wait_send)

    def middle(i):
        at = rows_of(i)
        cond_rows = v.cond[i]
        att = v.attended[at, :]
        gating = v.gating[at, :]
        gated = (gating * att).astype(BF16)
        branch = mm(gated, w_.output_weight[...])
        zeros = mm(cond_rows, lanes(w_.branch_gate[...], w_.closing_gate[...]))
        low2 = (v.cond_hat[at, :] * w_.second_gain[...]).astype(BF16)
        pre = mm(low2, lanes(w_.second_scale[...], w_.second_shift[...]))
        yield
        live = alive(i)
        zero_one = sigmoid(zeros[:, :width] + w_.branch_lift[...])
        zero_two = sigmoid(zeros[:, width:] + w_.closing_lift[...])
        live_one = live * zero_one
        live_two = live * zero_two
        mid = v.single[i].astype(F32) + live_one * branch
        mid_hat, mid_inv = normalize(mid)
        scaling = sigmoid(pre[:, :width] + w_.second_lift[...])
        second = (scaling * mid_hat + pre[:, width:]).astype(BF16)
        yield
        pre = mm(second, lanes(w_.hidden_gate[...], w_.hidden_up[...]))
        half = pre.shape[1] // 2
        gate_pre, up_pre = pre[:, :half], pre[:, half:]
        yield
        gate_sig = sigmoid(gate_pre)
        gate_silu = gate_pre * gate_sig
        hidden = (gate_silu * up_pre).astype(BF16)
        out_grad = v.cot[i].astype(F32)
        closing_full = out_grad * live_two
        closing_grad = closing_full.astype(BF16)
        yield
        closing = mm(hidden, w_.hidden_down[...])
        hidden_grad = mm_t(closing_grad, w_.hidden_down[...])
        add(HIDDEN_DOWN, t_mm(hidden, closing_grad))
        yield
        gate_slope = gate_sig + gate_silu * (1.0 - gate_sig)
        gate_pre_grad = (hidden_grad * up_pre * gate_slope).astype(BF16)
        up_pre_grad = (hidden_grad * gate_silu).astype(BF16)
        gate_up_grad = lanes(gate_pre_grad, up_pre_grad)
        yield
        second_grad = mm_t(gate_up_grad, lanes(w_.hidden_gate[...], w_.hidden_up[...]))
        wide_grad = t_mm(second, gate_up_grad)
        for k in range(4):
            add((0, k), wide_grad[:, k * width : (k + 1) * width])
        out.layer[i] = (mid + live_two * closing).astype(BF16)
        zero_two_pre = closing_full * closing * (1.0 - zero_two)
        add_vector(V_CLOSING_LIFT, col_sum(zero_two_pre))
        if i == items - 1:
            hidden_sum.scatter()
        yield
        scaled_grad = second_grad * scaling
        mid_grad = out_grad + normalize_back(mid_hat, mid_inv, scaled_grad)
        v.mid_grad[at, :] = mid_grad
        branch_full = mid_grad * live_one
        branch_grad = branch_full.astype(BF16)
        yield
        attended_grad = mm_t(branch_grad, w_.output_weight[...]) * gating
        v.attended_low[at, :] = attended_grad.astype(BF16)
        yield
        add(OUTPUT, t_mm(gated, branch_grad))
        before = scaled_grad * mid_hat * (1.0 - scaling)
        both = lanes(before.astype(BF16), second_grad.astype(BF16))
        add_vector(V_SECOND_LIFT, col_sum(before))
        both_grad = t_mm(low2, both)
        add(SECOND_SCALE, both_grad[:, :width])
        add(SECOND_SHIFT, both_grad[:, width:])
        cond_normed = mm_t(both, lanes(w_.second_scale[...], w_.second_shift[...]))
        yield
        gate_low = (attended_grad * att * (1.0 - gating)).astype(BF16)
        v.gate_low[at, :] = gate_low
        zero_one_pre = branch_full * branch * (1.0 - zero_one)
        add_vector(V_BRANCH_LIFT, col_sum(zero_one_pre))
        zero_grads = lanes(zero_one_pre.astype(BF16), zero_two_pre.astype(BF16))
        add(GATE, t_mm(v.first[at, :], gate_low))
        gate_grads = t_mm(cond_rows, zero_grads)
        add(BRANCH, gate_grads[:, :width])
        add(CLOSING, gate_grads[:, width:])
        v.cond_direct[at, :] = mm_t(zero_grads, lanes(w_.branch_gate[...], w_.closing_gate[...]))
        add_vector(V_SECOND_GAIN, col_sum(cond_normed * v.cond_hat[at, :]))
        v.cond_normed[at, :] = cond_normed * w_.second_gain[...]

    middles = [middle(i) for i in range(items)]
    for _ in range(MIDDLE_STEPS):
        for part in middles:
            next(part)

    def halo_right(i):
        return to_right(
            v.halo_send.at[i, 1], v.halo_recv.at[i, 0], v.hg_send.at[i, 1], v.hg_recv.at[i, 0]
        )

    def halo_left(i):
        return to_left(
            v.halo_send.at[i, 0], v.halo_recv.at[i, 1], v.hg_send.at[i, 0], v.hg_recv.at[i, 1]
        )

    folded = {}

    def attend_back(i, w):
        at = window_at(i, w)
        wide_grad = spread_heads(v.attended_low[at, :])
        probs_grad = mm_t(wide_grad, values_of(i, w))
        probs = v.probs[i, w]
        value_grad = t_mm(probs.astype(BF16), wide_grad)
        yield
        inner_sum = jnp.sum(probs_grad * probs, axis=-1, keepdims=True)
        yield
        logits_grad = probs * (probs_grad - inner_sum)
        low = logits_grad.astype(BF16)
        by_head = logits_grad.reshape(heads, QW, KW)
        v.slopes[i, w] = (by_head * v.pair_inv[at, :][None]).astype(BF16).reshape(hq, KW)
        v.probs[i, w] = logits_grad
        query_grad = mm(low, keys_of(i, w))
        key_grad = t_mm(low, spread_heads(v.query[at, :]))
        yield
        v.row_grad[at, :] = gather_heads(query_grad) * factor
        for k in range(SPREAD):
            piece = slice(k * QW, (k + 1) * QW)
            piece = (key_grad[piece], value_grad[piece])
            if (i, w + k) in folded:
                piece = [a + b for a, b in zip(folded[i, w + k], piece)]
            folded[i, w + k] = piece

    def fold(i, blocks):
        for b in blocks:
            key_grad, value_grad = folded.pop((i, b))
            v.keys_grad[i, b * QW : (b + 1) * QW, :width] = key_grad * factor
            v.keys_grad[i, b * QW : (b + 1) * QW, width:] = value_grad

    blocks = range(windows + SPREAD - 1)
    ends = -(-HALO // QW)
    for group in (range(items // 2), range(items // 2, items)):
        weave([attend_back(i, w) for i in group for w in outer], BACK_START)
        for i in group:
            for side, at in ((0, blocks[:ends]), (1, blocks[-ends:])):
                for k in (0, 1):
                    edge = rows(*[folded[i, b][k] for b in at])
                    edge = edge[:HALO] if side == 0 else edge[-HALO:]
                    if k == 0:
                        edge = edge * factor
                    v.halo_send[i, side, :, k * width : (k + 1) * width] = edge.astype(BF16)
        where_right(*[halo_right(i).start for i in group])
        where_left(*[halo_left(i).start for i in group])
    weave([attend_back(*a) for a in every(inner)], BACK_START)
    weave(middles, items)
    middle_sum.scatter()
    for i in range(items):
        fold(i, blocks)
    for i in range(items):
        if i == items // 2:
            hidden_sum.over_dp()
        pair_all = lanes(*[pair_rows(i, w).reshape(cq, KW) for w in range(windows)])
        slopes_all = lanes(*[v.slopes[i, w] for w in range(windows)])
        for k in (0, 1):
            half = slice(k * cq // 2, (k + 1) * cq // 2)
            v.pair_sums[half, :] += mm_t(pair_all[half], slopes_all)

    diagonal = jnp.where(iota((cq, hq), 0) % QW == iota((cq, hq), 1) % QW, v.pair_sums[...], 0.0)
    by_channel = jnp.sum(diagonal.reshape(channels, QW, hq), axis=1)
    gather = jnp.where(iota((hq, width), 0) // QW == iota((hq, width), 1), 1.0, 0.0)
    channel_sums = mm(by_channel, gather, HIGHEST)
    first_sum.acc[pair_at : pair_at + channels, :] = channel_sums - jnp.mean(
        channel_sums, axis=0, keepdims=True
    )

    def finish_rows(parts, last):
        def read(ref):
            return rows(*[ref[i * length + a : i * length + b, :] for i, a, b in parts])

        def write(ref, value):
            done = 0
            for i, a, b in parts:
                ref[i * length + a : i * length + b, :] = value[done : done + b - a]
                done += b - a

        query_grad = read(v.row_grad)
        add_vector(V_QUERY_BIAS, col_sum(query_grad))
        key_value = rows(*[v.keys_grad[i, HALO + a : HALO + b, :] for i, a, b in parts])
        grads = lanes(query_grad.astype(BF16), key_value.astype(BF16), read(v.gate_low))
        yield
        weight_grads = t_mm(read(v.first), grads[:, : 3 * width])
        for k in range(3):
            add((2, k), weight_grads[:, k * width : (k + 1) * width])
        if last:
            qkv_sum.scatter()
        first_grad = mm_t(
            grads,
            lanes(
                w_.query_weight[...],
                w_.key_weight[...],
                w_.value_weight[...],
                w_.gate_weight[...],
            ),
        )
        yield
        scaling = read(v.scaling)
        scaled_grad = first_grad * scaling
        before = scaled_grad * read(v.single_hat) * (1.0 - scaling)
        both = lanes(before.astype(BF16), first_grad.astype(BF16))
        add_vector(V_FIRST_LIFT, col_sum(before))
        write(v.row_grad, scaled_grad)
        yield
        cond_hat = read(v.cond_hat)
        low1 = (cond_hat * w_.first_gain[...]).astype(BF16)
        both_grad = t_mm(low1, both)
        add(FIRST_SCALE, both_grad[:, :width])
        add(FIRST_SHIFT, both_grad[:, width:])
        cond_normed = mm_t(both, lanes(w_.first_scale[...], w_.first_shift[...]))
        add_vector(V_FIRST_GAIN, col_sum(cond_normed * cond_hat))
        write(v.cond_normed, read(v.cond_normed) + cond_normed * w_.first_gain[...])

    weave(
        [finish_rows([(i, HALO, length - HALO)], False) for i in range(items)], FINISH_START
    )
    where_left(*[halo_right(i).wait_recv for i in range(items)])
    where_right(*[halo_left(i).wait_recv for i in range(items)])
    rim = []
    for i in range(items):
        v.keys_grad[i, HALO : 2 * HALO, :] += v.halo_recv[i, 0].astype(F32)
        v.keys_grad[i, length : length + HALO, :] += v.halo_recv[i, 1].astype(F32)
        rim += [(i, 0, HALO), (i, length - HALO, length)]
    weave([finish_rows(rim, True)], FINISH_START)

    def close_rows(i):
        at = rows_of(i)
        atom_grad = normalize_back(v.single_hat[at, :], v.single_inv[at, :], v.row_grad[at, :])
        out.agrad[i] = v.mid_grad[at, :] + atom_grad
        cond_grad = normalize_back(v.cond_hat[at, :], v.cond_inv[at, :], v.cond_normed[at, :])
        out.cgrad[i] = cond_grad + v.cond_direct[at, :]

    def pair_back(i):
        wide = v.wide_turned[...]
        for w in range(0, windows, 2):
            both = lanes(v.slopes[i, w], v.slopes[i, w + 1])
            both = rows(both, both)
            half = cq // 2
            product = rows(mm(wide[:half], both), mm(wide[half:], both))
            for u in (0, 1):
                at = window_at(i, w + u)
                grad = v.probs[i, w + u] * v.term[i, w + u]
                dot = jnp.sum(grad.reshape(heads, QW, KW), axis=0)
                inv = v.pair_inv[at, :]
                slope = dot * inv * inv * (1.0 / channels)
                block = pair_rows(i, w + u).astype(F32)
                part = product[:, u * KW : (u + 1) * KW].reshape(channels, QW, KW)
                out.pgrad[i, :, (w + u) * QW : (w + u + 1) * QW, :] = (
                    part - (block - v.pair_mean[at, :][None]) * slope[None]
                )

    def close_part(part):
        for i in range(part * items // 4, (part + 1) * items // 4):
            close_rows(i)
            pair_back(i)

    first_sum.scatter()
    close_part(0)
    middle_sum.over_dp()
    close_part(1)
    close_part(2)
    hidden_sum.gather()
    qkv_sum.over_dp()
    first_sum.over_dp()
    close_part(3)
    where_right(*[halo_right(i).wait_send for i in range(items)])
    where_left(*[halo_left(i).wait_send for i in range(items)])
    middle_sum.gather()
    qkv_sum.gather()
    first_sum.gather()
    for group in sums:
        group.finish()


def results_kernel(*refs):
    ins = Outputs(*refs[:6])
    reds, refs = refs[6 : 6 + SUMS], refs[6 + SUMS :]
    (pgrad, layer, agrad, cgrad), refs = refs[:4], refs[4:]
    count = len(Params._fields)
    grads, stages = Params(*refs[:count]), refs[count : count + SUMS]
    vectors, weight_s, gain_s, sem = refs[count + SUMS :]
    copies = []

    def send(src, dst):
        copy = pltpu.make_async_copy(src, dst, sem.at[len(copies)])
        copy.start()
        copies.append(copy)

    send(ins.pgrad, pgrad)
    send(ins.agrad, agrad)
    send(ins.cgrad, cgrad)
    send(ins.layer, layer)
    for stage, red in zip(stages, reds):
        stage[...] = red[...].astype(F32)
    width = layer.shape[-1]

    def block(place, n=1):
        return stages[place[0]].at[pl.ds(place[1] * width, n * width), :]

    for place, ref in (
        (OUTPUT, grads.output_weight),
        (BRANCH, grads.branch_gate),
        (CLOSING, grads.closing_gate),
        (SECOND_SCALE, grads.second_scale),
        (SECOND_SHIFT, grads.second_shift),
        (GATE, grads.gate_weight),
        (QUERY, grads.query_weight),
        (KEY, grads.key_weight),
        (VALUE, grads.value_weight),
        (FIRST_SCALE, grads.first_scale),
        (FIRST_SHIFT, grads.first_shift),
    ):
        send(block(place), ref)
    send(block(HIDDEN_DOWN, 2), grads.hidden_down)
    for place, ref in ((HIDDEN_GATE, grads.hidden_gate), (HIDDEN_UP, grads.hidden_up)):
        for k in (0, 1):
            send(block((place[0], place[1] + k)), ref.at[:, pl.ds(k * width, width)])
    tail = stages[-1]
    vectors_at = BLOCKS[-1] * width
    for k, ref in (
        (V_FIRST_GAIN, grads.first_gain),
        (V_FIRST_LIFT, grads.first_lift),
        (V_QUERY_BIAS, grads.query_bias),
        (V_BRANCH_LIFT, grads.branch_lift),
        (V_SECOND_GAIN, grads.second_gain),
        (V_SECOND_LIFT, grads.second_lift),
        (V_CLOSING_LIFT, grads.closing_lift),
    ):
        vectors[k] = tail[vectors_at + k : vectors_at + k + 1, :]
        send(vectors.at[k], ref)
    heads, channels = ins.weight.shape
    pair_at = vectors_at + VECTOR_ROWS
    pick = jnp.where(iota((heads, width), 0) == iota((heads, width), 1), 1.0, 0.0)
    turned = mm_t(pick, tail[pair_at : pair_at + channels, :], HIGHEST)
    weight_s[...] = turned * ins.gain[...]
    gain_s[...] = jnp.sum(ins.weight[...] * turned, axis=0, keepdims=True)
    send(weight_s, grads.pair_weight)
    send(gain_s, grads.pair_gain)
    for copy in copies:
        copy.wait()


def shards(n_a, n_d, single, cond, pair, counts, cot, *params):
    items, length, width = single.shape
    windows = length // QW
    channels = pair.shape[1]
    params = Params(*params)
    flat = Params(
        *[p.reshape(1, -1) if p.ndim == 1 else p for p in params._replace(pair_weight=params.pair_weight.T)]
    )
    heads = flat.pair_weight.shape[0]
    hq, cq = heads * QW, channels * QW
    totals = [count * width for count in BLOCKS]
    totals[-1] += VECTOR_ROWS + channels
    shard = [shard_rows(total, n_a) for total in totals]

    vmem = pl.BlockSpec(memory_space=pltpu.VMEM)
    anywhere = pl.BlockSpec(memory_space=pl.ANY)
    by_items = (items, length, width)
    ext = length + 2 * HALO
    dma = pltpu.SemaphoreType.DMA

    def f32(*shape):
        return pltpu.VMEM(shape, F32)

    def bf16(*shape):
        return pltpu.VMEM(shape, BF16)

    by_rows = f32(items * length, width)
    by_rows_low = bf16(items * length, width)
    by_keys = f32(items * length, KW)
    by_window = f32(items, windows, hq, KW)
    scratch = Scratch(
        counts=pltpu.SMEM(counts.shape, counts.dtype),
        single=bf16(*by_items),
        cond=bf16(*by_items),
        cot=bf16(*by_items),
        pair=bf16(*pair.shape),
        keys=bf16(items, ext, 2 * width),
        keys_grad=f32(items, ext, 2 * width),
        query=by_rows_low,
        first=by_rows_low,
        attended_low=by_rows_low,
        gate_low=by_rows_low,
        cond_hat=by_rows,
        cond_inv=by_rows,
        single_hat=by_rows,
        single_inv=by_rows,
        scaling=by_rows,
        gating=by_rows,
        attended=by_rows,
        mid_grad=by_rows,
        cond_normed=by_rows,
        cond_direct=by_rows,
        row_grad=by_rows,
        pair_inv=by_keys,
        pair_mean=by_keys,
        term=by_window,
        probs=by_window,
        slopes=bf16(items, windows, hq, KW),
        wide=bf16(2 * hq, cq),
        wide_turned=bf16(cq, 2 * hq),
        head_mask=bf16(hq, width),
        pair_sums=f32(cq, hq),
        halo_send=bf16(items, 2, HALO, 2 * width),
        halo_recv=bf16(items, 2, HALO, 2 * width),
        in_sem=dma((4 + len(params),)),
        pair_sem=dma((items,)),
        kv_send=dma((2,)),
        kv_recv=dma((2,)),
        hg_send=dma((items, 2)),
        hg_recv=dma((items, 2)),
        rs_send=dma((SUMS, n_a)),
        rs_recv=dma((SUMS, n_a)),
        ag_send=dma((SUMS, n_a)),
        ag_recv=dma((SUMS, n_a)),
        z_send=dma((SUMS, n_d)),
        z_recv=dma((SUMS, n_d)),
    )
    sum_scratch = [
        SumScratch(
            acc=f32(n_a * size, width),
            send=bf16(n_a, size, width),
            recv=bf16(n_a, size, width),
            zall=bf16(n_d, size, width),
        )
        for size in shard
    ]

    def in_hbm(value):
        return pltpu.with_memory_space_constraint(value, pltpu.HBM)

    outs = pl.pallas_call(
        functools.partial(main_kernel, n_a, n_d),
        out_shape=[
            *Outputs(
                layer=bf16(*by_items),
                agrad=f32(*by_items),
                cgrad=f32(*by_items),
                pgrad=f32(*pair.shape),
                gain=f32(1, channels),
                weight=f32(heads, channels),
            ),
            *[bf16(n_a, size, width) for size in shard],
        ],
        in_specs=[anywhere] * (5 + len(params)),
        out_specs=[vmem] * (6 + SUMS),
        scratch_shapes=[
            *scratch,
            *[pltpu.VMEM(p.shape, p.dtype) for p in flat],
            *[buf for bufs in sum_scratch for buf in bufs],
        ],
        compiler_params=pltpu.CompilerParams(
            collective_id=0, has_side_effects=True, vmem_limit_bytes=48 * 1024 * 1024
        ),
        name="block",
    )(*[in_hbm(x) for x in (counts, pair, single, cond, cot, *flat)])
    kept = Outputs(*outs[:6])
    reds = [red.reshape(-1, width) for red in outs[6:]]

    def sds(shape, dtype):
        return jax.ShapeDtypeStruct(shape, dtype)

    pgrad, layer, agrad, cgrad, *grads = pl.pallas_call(
        results_kernel,
        out_shape=[
            sds(pair.shape, F32),
            sds(by_items, BF16),
            sds(by_items, F32),
            sds(by_items, F32),
            *[sds(p.shape, F32) for p in flat],
        ],
        in_specs=[anywhere] * 4 + [vmem] * (2 + SUMS),
        out_specs=[anywhere] * (4 + len(params)),
        scratch_shapes=[
            *[f32(n_a * size, width) for size in shard],
            f32(VECTOR_ROWS, 1, width),
            f32(heads, channels),
            f32(1, channels),
            dma((6 + len(params),)),
        ],
        compiler_params=pltpu.CompilerParams(vmem_limit_bytes=16 * 1024 * 1024),
        name="results",
    )(*kept, *reds)
    grads = Params(*grads)
    grads = grads._replace(pair_weight=grads.pair_weight.T)
    return (layer, agrad, pgrad, cgrad, *[g.reshape(p.shape) for g, p in zip(grads, params)])


def solution(mesh):
    atoms = P("dp", "atoms", None)
    pair = P("dp", None, "atoms", None)
    count = len(Params._fields)
    return jax.shard_map(
        functools.partial(shards, mesh.shape["atoms"], mesh.shape["dp"]),
        mesh=mesh,
        in_specs=(atoms, atoms, pair, P("dp"), atoms) + (P(),) * count,
        out_specs=(atoms, atoms, pair, atoms) + (P(),) * count,
        check_vma=False,
    )
```
